32 devices in a mesh: dp: 8 (over z, x), mp: 4 (over y, core).
Axes of the slice: x: 2, y: 2, z: 4, core: 2. Of those that a mesh axis runs over, the one named last changes fastest.
Arguments:
- hidden_in: bfloat16 [12288, 768], P('dp'), may hold values from -6 to 6
- page_ids: int32 [12288], P('dp'), may hold values from 0 to 7, as said below
- pad_mask: int32 [12288], P('dp'), may hold values from 0 to 1, as said below
- boxes: int32 [12288, 2], P('dp'), may hold values from 0 to 999
- out_grad: bfloat16 [12288, 768], P('dp'), may hold values from -6 to 6
- attn_in: float32 [5, 768, 768], P(None, 'dp', 'mp'), may hold values from -0.21875 to 0.21875
- attn_in_moment: float32 [5, 768, 768], P(None, 'dp', 'mp'), may hold values from -20 to 20
- attn_in_second: float32 [5, 768, 768], P(None, 'dp', 'mp'), may hold values from 0.24576 to 2.4576
- attn_out: float32 [768, 768], P('mp', 'dp'), may hold values from -0.875 to 0.875
- attn_out_moment: float32 [768, 768], P('mp', 'dp'), may hold values from -10 to 10
- attn_out_second: float32 [768, 768], P('mp', 'dp'), may hold values from 0.12288 to 0.98304
- ffn_in: float32 [768, 3072], P('dp', 'mp'), may hold values from -0.21875 to 0.21875
- ffn_in_moment: float32 [768, 3072], P('dp', 'mp'), may hold values from -20 to 20
- ffn_in_second: float32 [768, 3072], P('dp', 'mp'), may hold values from 0.6144 to 4.9152
- ffn_out: float32 [3072, 768], P('mp', 'dp'), may hold values from -0.109375 to 0.109375
- ffn_out_moment: float32 [3072, 768], P('mp', 'dp'), may hold values from -32 to 32
- ffn_out_second: float32 [3072, 768], P('mp', 'dp'), may hold values from 1.2288 to 7.3728
- norm_weight: float32 [4, 768], P(None, 'dp'), may hold values from -0.9 to 1.5
- norm_moment: float32 [4, 768], P(None, 'dp'), may hold values from -64 to 64
- norm_second: float32 [4, 768], P(None, 'dp'), may hold values from 6.144 to 49.152
Outputs:
- mixed: bfloat16 [12288, 768], P('dp')
- input_grad: float32 [12288, 768], P('dp')
- new_attn_in: float32 [5, 768, 768], P(None, 'dp', 'mp')
- new_attn_in_moment: float32 [5, 768, 768], P(None, 'dp', 'mp')
- new_attn_in_second: float32 [5, 768, 768], P(None, 'dp', 'mp')
- new_attn_out: float32 [768, 768], P('mp', 'dp')
- new_attn_out_moment: float32 [768, 768], P('mp', 'dp')
- new_attn_out_second: float32 [768, 768], P('mp', 'dp')
- new_ffn_in: float32 [768, 3072], P('dp', 'mp')
- new_ffn_in_moment: float32 [768, 3072], P('dp', 'mp')
- new_ffn_in_second: float32 [768, 3072], P('dp', 'mp')
- new_ffn_out: float32 [3072, 768], P('mp', 'dp')
- new_ffn_out_moment: float32 [3072, 768], P('mp', 'dp')
- new_ffn_out_second: float32 [3072, 768], P('mp', 'dp')
- new_norm_weight: float32 [4, 768], P(None, 'dp')
- new_norm_moment: float32 [4, 768], P(None, 'dp')
- new_norm_second: float32 [4, 768], P(None, 'dp')
The draws below stay inside these ranges and needn't reach their ends.
Inputs may be any that keep to these rules, and one draw needn't show every extreme that they name: `page_ids`: within each row of 512 tokens the page numbers start at 0, never fall, and each of the 8 pages holds at least one token. `pad_mask`: each row of 512 tokens ends with 1 to 64 padding tokens; all other tokens are 0.
All inputs are finite; a program needn't handle non-finite values.
Results may differ from the reference program's by a relative error of at most 0.02.
The reference program's roundings to bfloat16 on the way count: a program that leaves them out, or rounds other values in their place, can miss the bound.
Values may be sent and summed in bfloat16 or wider, within the bound.
A program may use at most 128 MiB of HBM per device.

```python
import math
import jax
import jax.numpy as jnp
from jax import lax

D = 768
HEADS = 12
HEAD_DIM = 64
FF = 3072
SEQ = 512
PAGES = 8
STEP = 10
TOKENS = 12288
N_MP = 4


def page_layout(key):
    row_count = TOKENS // SEQ
    row_keys = jax.random.split(key, row_count)

    def one_row(row_key):
        order_key, length_key = jax.random.split(row_key)
        ordering = jax.random.permutation(order_key, SEQ - 1) + 1
        starts = jnp.sort(ordering[:PAGES - 1])
        places = jnp.arange(SEQ, dtype=jnp.int32)
        page_numbers = jnp.sum((places[:, None] >= starts[None, :]).astype(jnp.int32), axis=1)
        padded = jax.random.randint(length_key, (), 1, SEQ // 8 + 1)
        padding = (places >= SEQ - padded).astype(jnp.int32)
        return (page_numbers, padding)
    page_numbers, padding = jax.vmap(one_row)(row_keys)
    return (page_numbers.reshape(-1).astype(jnp.int32), padding.reshape(-1).astype(jnp.int32))


def draw_page_ids(key, part):
    return page_layout(key)[0]


def draw_pad_mask(key, part):
    return page_layout(key)[1]


def draw_norm_weight(key, part):
    key = jax.random.fold_in(key, 7)
    scale_key, offset_key = jax.random.split(key)
    scaling = jax.random.uniform(scale_key, (2, D), jnp.float32, 0.5, 1.5)
    offsets = jnp.clip(0.3 * jax.random.normal(offset_key, (2, D), jnp.float32), -0.9, 0.9)
    return jnp.stack([scaling[0], offsets[0], scaling[1], offsets[1]]).astype(jnp.float32)


def touch_ends(result, stream_key, smallest, top_value):
    shape = result.shape
    spot = [jax.random.randint(jax.random.fold_in(stream_key, axis), (), 0, shape[axis]) for axis in range(len(shape))]
    result = result.at[tuple(spot)].set(smallest)
    longest = shape.index(max(shape))
    spot[longest] = (spot[longest] + 1) % shape[longest]
    return result.at[tuple(spot)].set(top_value)


def level_of(stream_key, extent, cuts, smallest, largest):
    level, own = 1.0, jax.random.fold_in(stream_key, 6)
    for dim, parts in cuts:
        steps = jnp.exp(jax.random.uniform(jax.random.fold_in(own, dim), (parts,), jnp.float32, smallest / len(cuts), largest / len(cuts)))
        level = level * jnp.repeat(steps, extent[dim] // parts).reshape([-1 if axis == dim else 1 for axis in range(len(extent))])
    return level


def bell_draw(own_key, dims, deviation, bound, cuts=(), kind=jnp.bfloat16):
    array = jax.random.normal(own_key, dims, jnp.float32) * deviation
    if len(cuts) > 0:
        array = level_of(own_key, dims, cuts, -0.22, 0.18) * array
    return jnp.clip(array, min=-bound, max=bound).astype(kind)


def setup_inputs(seed: int = 0) -> dict:
    keys = jax.random.split(jax.random.key(seed), 21)
    return {
        "hidden_in": bell_draw(keys[0], (TOKENS, D), 1.0, 6.0, ((0, 8),)),
        "page_ids": draw_page_ids(jax.random.fold_in(keys[20], 71), 0),
        "pad_mask": draw_pad_mask(jax.random.fold_in(keys[20], 71), 0),
        "boxes": touch_ends(jax.random.randint(keys[3], (TOKENS, 2), 0, 1000), jax.random.fold_in(keys[3], 1), 0, 999).astype(jnp.int32),
        "out_grad": bell_draw(keys[4], (TOKENS, D), 1.0, 6.0, ((0, 8),)),
        "attn_in": bell_draw(keys[5], (5, D, D), D ** -0.5, 0.21875, ((1, 8), (2, 4)), jnp.float32),
        "attn_in_moment": bell_draw(keys[6], (5, D, D), (0.03 * TOKENS ** 0.5), 20.0, ((1, 8), (2, 4)), jnp.float32),
        "attn_in_second": jnp.clip(jnp.exp(math.log(2.4576) - 2.3025852 * jax.random.uniform(keys[7], (5, D, D), jnp.float32) ** level_of(keys[7], (5, D, D), ((1, 8), (2, 4)), -0.2, 0.2)), 0.24576, 2.4576),
        "attn_out": bell_draw(keys[8], (D, D), (D // 16) ** -0.5, 0.875, ((0, 4), (1, 8)), jnp.float32),
        "attn_out_moment": bell_draw(keys[9], (D, D), (0.015 * TOKENS ** 0.5), 10.0, ((0, 4), (1, 8)), jnp.float32),
        "attn_out_second": jnp.clip(jnp.exp(math.log(0.98304) - 2.0794415 * jax.random.uniform(keys[10], (D, D), jnp.float32) ** level_of(keys[10], (D, D), ((0, 4), (1, 8)), -0.2, 0.2)), 0.12288, 0.98304),
        "ffn_in": bell_draw(keys[11], (D, FF), D ** -0.5, 0.21875, ((0, 8), (1, 4)), jnp.float32),
        "ffn_in_moment": bell_draw(keys[12], (D, FF), (0.03 * TOKENS ** 0.5), 20.0, ((0, 8), (1, 4)), jnp.float32),
        "ffn_in_second": jnp.clip(jnp.exp(math.log(4.9152) - 2.0794415 * jax.random.uniform(keys[13], (D, FF), jnp.float32) ** level_of(keys[13], (D, FF), ((0, 8), (1, 4)), -0.2, 0.2)), 0.6144, 4.9152),
        "ffn_out": bell_draw(keys[14], (FF, D), FF ** -0.5, 0.109375, ((0, 4), (1, 8)), jnp.float32),
        "ffn_out_moment": bell_draw(keys[15], (FF, D), (0.045 * TOKENS ** 0.5), 32.0, ((0, 4), (1, 8)), jnp.float32),
        "ffn_out_second": jnp.clip(jnp.exp(math.log(7.3728) - 1.7917594 * jax.random.uniform(keys[16], (FF, D), jnp.float32) ** level_of(keys[16], (FF, D), ((0, 4), (1, 8)), -0.2, 0.2)), 1.2288, 7.3728),
        "norm_weight": draw_norm_weight(jax.random.fold_in(keys[20], 71), 0),
        "norm_moment": bell_draw(keys[18], (4, D), (0.1 * TOKENS ** 0.5), 64.0, ((1, 8),), jnp.float32),
        "norm_second": jnp.clip(jnp.exp(math.log(49.152) - 2.0794415 * jax.random.uniform(keys[19], (4, D), jnp.float32) ** level_of(keys[19], (4, D), ((1, 8),), -0.2, 0.2)), 6.144, 49.152),
    }


@jax.custom_vjp
def low(v):
    return lax.optimization_barrier(v.astype(jnp.bfloat16)).astype(jnp.float32)

@jax.custom_vjp
def low_back(v):
    return v

def low_keep(v):
    return (low(v), None)

def low_pass(kept, grad):
    return (grad,)

def back_keep(v):
    return (v, None)

def back_low(kept, grad):
    return (low(grad),)
low.defvjp(low_keep, low_pass)
low_back.defvjp(back_keep, back_low)
epsilon_norm = 1e-12
epsilon_adam = 1e-08
beta_first = 0.9
beta_second = 0.999
rate_matrix = 0.05
rate_norm = 0.2
decay_matrix = 0.01
masked_score = -1e+30
highest = lax.Precision.HIGHEST

def both_ways(values):
    return low_back(low(values))

def box_embed(boxes):
    quarter = D // 4
    ladder = jnp.arange(quarter).astype(jnp.float32)
    frequency = jnp.exp(ladder * (-math.log(10000.0) / quarter))
    coords = boxes.astype(jnp.float32)
    across = coords[:, 0:1] * frequency[None, :]
    upward = coords[:, 1:2] * frequency[None, :]
    return jnp.concatenate([jnp.sin(across), jnp.cos(across), jnp.sin(upward), jnp.cos(upward)], axis=1)

def layer_norm(values, scaling, offset):
    center = lax.optimization_barrier(jnp.mean(values, axis=-1, keepdims=True))
    shifted = values - center
    spread = lax.optimization_barrier(jnp.mean(shifted * shifted, axis=-1, keepdims=True))
    return shifted * lax.rsqrt(spread + epsilon_norm) * scaling + offset

def mask_of(page_numbers, padding):
    places = jnp.arange(page_numbers.shape[0])
    same_page = page_numbers[:, None] == page_numbers[None, :]
    usable = (padding[None, :] == 0) | (places[:, None] == places[None, :])
    return same_page & usable

def attend_one(pieces):
    query_rows, key_rows, value_rows, box_query, box_key, page_numbers, padding = pieces
    left_side = jnp.concatenate([query_rows, query_rows, box_query], axis=-1)
    right_side = jnp.concatenate([key_rows, box_key, key_rows], axis=-1)
    scores = jnp.einsum('qhe,khe->hqk', left_side, right_side, precision=highest) * HEAD_DIM ** (-0.5)
    scores = low_back(scores)
    allowed = mask_of(page_numbers, padding)
    scores = jnp.where(allowed[None], scores, masked_score)
    highest_score = lax.optimization_barrier(jnp.max(scores, axis=-1, keepdims=True))
    raised = jnp.exp(scores - highest_score)
    softmax_out = raised / lax.optimization_barrier(jnp.sum(raised, axis=-1, keepdims=True))
    return jnp.einsum('hqk,khe->qhe', low(softmax_out), value_rows, precision=highest)

def forward(hidden, weight_in, weight_out, weight_up, weight_down, norm_full, embed, page_ids, pad_mask):
    token_count = hidden.shape[0]
    block_count = token_count // SEQ
    group_width = D // N_MP
    inner_width = FF // N_MP
    low_in = low(weight_in)
    low_out = low(weight_out)
    low_up = low(weight_up)
    low_down = low(weight_down)
    low_embed = low(embed)
    pieces_all = [[] for number in range(5)]
    for member in range(N_MP):
        window = slice(member * group_width, (member + 1) * group_width)
        source = low_back(hidden)
        for number in range(3):
            pieces_all[number].append(jnp.dot(source, low_in[number][:, window], precision=highest))
        for number in (3, 4):
            pieces_all[number].append(jnp.dot(low_embed, low_in[number][:, window], precision=highest))
    head_arrays = [both_ways(jnp.concatenate(column, axis=1)).reshape(block_count, SEQ, HEADS, HEAD_DIM) for column in pieces_all]
    blocked = tuple(head_arrays) + (page_ids.reshape(block_count, SEQ), pad_mask.reshape(block_count, SEQ))
    context = lax.map(jax.checkpoint(attend_one), blocked).reshape(token_count, D)
    context = both_ways(context)
    attn_total = jnp.zeros((token_count, D), jnp.float32)
    for member in range(N_MP):
        window = slice(member * group_width, (member + 1) * group_width)
        attn_total = attn_total + low(jnp.dot(context[:, window], low_out[window, :], precision=highest))
    residual_one = hidden + low_back(attn_total)
    normed_one = layer_norm(residual_one, norm_full[0], norm_full[1])
    shared = low(normed_one)
    ffn_total = jnp.zeros((token_count, D), jnp.float32)
    for member in range(N_MP):
        window = slice(member * inner_width, (member + 1) * inner_width)
        pre_active = low_back(jnp.dot(low_back(shared), low_up[:, window], precision=highest))
        active = low(jax.nn.gelu(pre_active, approximate=False))
        ffn_total = ffn_total + low(jnp.dot(active, low_down[window, :], precision=highest))
    return layer_norm(normed_one + low_back(ffn_total), norm_full[2], norm_full[3])

def adam_step(weight, gradient, moment, second, rate, decay):
    moment_new = beta_first * moment + (1.0 - beta_first) * gradient
    second_new = beta_second * second + (1.0 - beta_second) * gradient * gradient
    moment_hat = moment_new / (1.0 - beta_first ** STEP)
    second_hat = second_new / (1.0 - beta_second ** STEP)
    weight_new = weight - rate * (moment_hat / (jnp.sqrt(second_hat) + epsilon_adam) + decay * weight)
    return (weight_new, moment_new, second_new)

def reference(hidden_in, page_ids, pad_mask, boxes, out_grad, attn_in, attn_in_moment, attn_in_second, attn_out, attn_out_moment, attn_out_second, ffn_in, ffn_in_moment, ffn_in_second, ffn_out, ffn_out_moment, ffn_out_second, norm_weight, norm_moment, norm_second):
    embed = box_embed(boxes)

    def layer(hidden, weight_in, weight_out, weight_up, weight_down, norm_full):
        return forward(hidden, weight_in, weight_out, weight_up, weight_down, norm_full, embed, page_ids, pad_mask)
    final, pullback = jax.vjp(layer, hidden_in.astype(jnp.float32), attn_in, attn_out, ffn_in, ffn_out, norm_weight)
    grad_hidden, grad_in, grad_out, grad_up, grad_down, grad_norm = pullback(out_grad.astype(jnp.float32))
    new_in = adam_step(attn_in, grad_in, attn_in_moment, attn_in_second, rate_matrix, decay_matrix)
    new_out = adam_step(attn_out, grad_out, attn_out_moment, attn_out_second, rate_matrix, decay_matrix)
    new_up = adam_step(ffn_in, grad_up, ffn_in_moment, ffn_in_second, rate_matrix, decay_matrix)
    new_down = adam_step(ffn_out, grad_down, ffn_out_moment, ffn_out_second, rate_matrix, decay_matrix)
    new_norm = adam_step(norm_weight, grad_norm, norm_moment, norm_second, rate_norm, 0.0)
    return (final.astype(jnp.bfloat16), grad_hidden, new_in[0], new_in[1], new_in[2], new_out[0], new_out[1], new_out[2], new_up[0], new_up[1], new_up[2], new_down[0], new_down[1], new_down[2], new_norm[0], new_norm[1], new_norm[2])
```

```python
from functools import partial
import math

import jax
import jax.numpy as jnp
from jax import lax
from jax.experimental import pallas as pl
from jax.experimental.pallas import tpu as pltpu
from jax.sharding import PartitionSpec as P

D = 768
HEAD_DIM = 64
SEQ = 512
HALF = SEQ // 2
STEP = 10
HEADS = 3
QK = HEADS * 128
ATT = 3 * QK
FFN = 2 * D

epsilon_norm = 1e-12
epsilon_adam = 1e-08
beta_first = 0.9
beta_second = 0.999
rate_matrix = 0.05
rate_norm = 0.2
decay_matrix = 0.01
masked_score = -1e30

F32 = jnp.float32
BF16 = jnp.bfloat16
VMEM_LIMIT = 60 * 1024 * 1024


def dot(a, b):
    return jnp.dot(a, b, preferred_element_type=F32)


def dot_nt(a, b):
    return lax.dot_general(a, b, (((1,), (1,)), ((), ())), preferred_element_type=F32)


def dot_tn(a, b):
    return lax.dot_general(a, b, (((0,), (0,)), ((), ())), preferred_element_type=F32)


def remote(src, dst, send, recv, device):
    return pltpu.make_async_remote_copy(
        src_ref=src,
        dst_ref=dst,
        send_sem=send,
        recv_sem=recv,
        device_id=device,
        device_id_type=pl.DeviceIdType.MESH,
    )


def steps(total, size, body):
    def run(i, carry):
        body(pl.multiple_of(i * size, size))
        return carry

    lax.fori_loop(0, total // size, run, 0)


def lower_half(shape):
    return lax.broadcasted_iota(jnp.int32, shape, len(shape) - 1) % 128 < HEAD_DIM


class Place:
    def __init__(self, ring):
        self.dp = lax.axis_index("dp")
        self.mp = lax.axis_index("mp")
        self.half = self.mp % 2
        self.pair = (self.dp, self.mp + 1 - 2 * self.half)
        self.across = (self.dp, (self.mp + 2) % 4)
        self.ring = ring
        self.z = self.dp // 2
        self.x = self.dp % 2
        self.xdev = (self.dp + 1 - 2 * self.x, self.mp)

    def zdev(self, k):
        return (((self.z + k) % self.ring) * 2 + self.x, self.mp)

    def came(self, k):
        return ((self.z + self.ring - k) % self.ring) * 2 + self.x

    def came_other(self, k):
        return ((self.z + self.ring - k) % self.ring) * 2 + 1 - self.x

    def greet(self):
        peers = [self.pair, self.across]
        if self.ring:
            peers += [self.xdev] + [self.zdev(k) for k in range(1, self.ring)]
        barrier = pltpu.get_barrier_semaphore()
        for peer in peers:
            pl.semaphore_signal(
                barrier, inc=1, device_id=peer, device_id_type=pl.DeviceIdType.MESH
            )
        pl.semaphore_wait(barrier, len(peers))

    def own(self, r):
        return pl.ds(pl.multiple_of(r * SEQ + self.half * HALF, HALF), HALF)

    def other(self, r):
        return pl.ds(pl.multiple_of(r * SEQ + (1 - self.half) * HALF, HALF), HALF)


class Gather:
    def __init__(self, place, kind, src, at, sems):
        self.p, self.src, self.at = place, src, at
        zs, zr, xs, xr = sems
        self.zs, self.zr, self.xs, self.xr = (
            zs.at[kind],
            zr.at[kind],
            xs.at[kind],
            xr.at[kind],
        )

    def along(self, k):
        p = self.p
        return remote(self.src, self.at(p.dp), self.zs.at[k], self.zr.at[k], p.zdev(k))

    def onward(self, k):
        p = self.p
        src = self.src if k == 0 else self.at(p.came(k))
        return remote(src, self.at(p.came(k)), self.xs.at[k], self.xr.at[k], p.xdev)

    def start(self):
        for k in range(1, self.p.ring):
            self.along(k).start()
        self.onward(0).start()

    def forward(self):
        p = self.p
        for k in range(1, p.ring):
            remote(
                self.src, self.at(p.came(k)), self.zs.at[k], self.zr.at[k], p.zdev(k)
            ).wait_recv()
            self.onward(k).start()

    def finish(self):
        p = self.p
        for k in range(p.ring):
            remote(
                self.src, self.at(p.came_other(k)), self.xs.at[k], self.xr.at[k], p.xdev
            ).wait_recv()
        for k in range(1, p.ring):
            self.along(k).wait_send()
        for k in range(p.ring):
            self.onward(k).wait_send()


class Sum:
    def __init__(self, place, parity, psend, precv, sums, yrecv, sems):
        self.p = place
        self.psend, self.precv = psend, precv
        self.sums, self.yrecv = sums.at[parity], yrecv.at[parity]
        ps, pr, ys, yr = sems
        self.ps, self.pr, self.ys, self.yr = (
            ps.at[parity],
            pr.at[parity],
            ys.at[parity],
            yr.at[parity],
        )

    def to_pair(self, r):
        return remote(
            self.psend.at[r], self.precv.at[r], self.ps.at[r], self.pr.at[r], self.p.pair
        )

    def over(self, r):
        return remote(
            self.sums.at[r], self.yrecv.at[r], self.ys.at[r], self.yr.at[r], self.p.across
        )

    def give(self, r, value):
        self.psend[r] = value.astype(BF16)
        self.to_pair(r).start()

    def keep(self, r, value):
        self.to_pair(r).wait_recv()
        self.sums[r] = (value + self.precv[r].astype(F32)).astype(BF16)
        self.over(r).start()

    def wait(self, r):
        self.over(r).wait_recv()

    def total(self, r, rows):
        return self.sums[r, rows, :].astype(F32) + self.yrecv[r, rows, :].astype(F32)

    def sent(self, r):
        self.to_pair(r).wait_send()

    def close(self, r):
        self.over(r).wait_send()


def rolled(value):
    return pltpu.roll(value.astype(F32), HEAD_DIM, 1)


def embed_rows(coords, lanes, out, row):
    rows = pl.ds(row, 32)
    here = coords[rows, :]
    across, upward = here[:, 0:1], here[:, 1:2]
    frequency, second, shift = lanes[0:1, :], lanes[1:2, :], lanes[2:3, :]
    angle = (across + (upward - across) * second) * frequency
    turns = jnp.round(angle * (2.0 / math.pi))
    rest = ((angle - turns * 1.5703125) - turns * 4.837512969970703125e-4) - turns * (
        7.54978995489188216e-8
    )
    square = rest * rest
    sine = rest + rest * square * (
        -1.6666654611e-1 + square * (8.3321608736e-3 + square * -1.9515295891e-4)
    )
    cosine = (
        1.0
        - 0.5 * square
        + square
        * square
        * (
            4.166664568298827e-2
            + square * (-1.388731625493765e-3 + square * 2.443315711809948e-5)
        )
    )
    quarter = (turns + shift).astype(jnp.int32)
    value = jnp.where((quarter & 1) == 1, cosine, sine)
    out[rows, :] = jnp.where((quarter & 2) == 2, -value, value).astype(BF16)


def attend_kernel(
    ring,
    chunks,
    hidden,
    cols,
    keyrow,
    lanes,
    packa,
    packf,
    pnorm,
    wtx,
    wop,
    wf,
    nbuf,
    lq,
    rk,
    vk,
    probs,
    ctx,
    emb,
    total,
    wa,
    scores,
    psend,
    precv,
    sums,
    yrecv,
    zs,
    zr,
    xs,
    xr,
    ps,
    pr,
    ys,
    yr,
):
    p = Place(ring)
    p.greet()
    sems = (zs, zr, xs, xr)
    if ring:
        share = packa.shape[0]

        def rows_of(ref):
            return lambda d: ref.at[pl.ds(pl.multiple_of(d * share, share), share), :]

        gather_a = Gather(p, 0, packa, rows_of(wa), sems)
        gather_f = Gather(p, 1, packf, rows_of(wf), sems)
        gather_n = Gather(p, 2, pnorm, lambda d: nbuf.at[d], sems)
        gather_a.start()
        gather_n.start()
        mine = pl.ds(pl.multiple_of(p.dp * share, share), share)
        wa[mine, :] = packa[...]
        wf[mine, :] = packf[...]
        nbuf[p.dp] = pnorm[...]
    else:
        wa[...] = packa[...]
    tokens = hidden.shape[0]
    steps(tokens, 32, partial(embed_rows, cols, lanes, emb))
    if ring:
        gather_a.forward()
        gather_n.forward()
        gather_a.finish()
        gather_n.finish()
        gather_f.start()

    def build(row):
        rows = pl.ds(row, 128)
        low = lower_half((128, 128))
        wtx[rows, :QK] = wa[rows, :QK]
        for h in range(HEADS):
            qk_cols = slice(h * 128, (h + 1) * 128)
            ov_cols = slice(QK + h * 128, QK + (h + 1) * 128)
            ov = wa[rows, ov_cols].astype(F32)
            wtx[rows, ov_cols] = jnp.where(low, rolled(wa[rows, qk_cols]), ov).astype(BF16)
            wop[rows, qk_cols] = jnp.where(low, 0.0, rolled(ov)).astype(BF16)

    steps(D, 128, build)

    def project(row):
        rows = pl.ds(row, HALF)
        text = dot(hidden[rows, :], wtx[...])
        box = dot(emb[rows, :], wa[:, 2 * QK :])
        low = lower_half((HALF, QK))
        lq[rows, :] = jnp.where(low, text[:, :QK], box).astype(BF16)
        rk[rows, :] = jnp.where(low, box, text[:, :QK]).astype(BF16)
        vk[rows, :] = text[:, QK:].astype(BF16)

    steps(tokens, HALF, project)
    reduce = Sum(p, 0, psend, precv, sums, yrecv, (ps, pr, ys, yr))

    def attend(r, side):
        start = side * HALF
        q_rows = pl.ds(pl.multiple_of(r * SEQ + start, HALF), HALF)
        k_rows = pl.ds(pl.multiple_of(r * SEQ, SEQ), SEQ)
        low = lower_half((HALF, 128))
        for h in range(HEADS):
            tile = slice(h * 128, (h + 1) * 128)
            left = lq[q_rows, tile]
            both = jnp.concatenate([left, jnp.where(low, left, jnp.zeros_like(left))], axis=1)
            right = jnp.concatenate([rk[k_rows, tile], vk[k_rows, tile]], axis=1)
            scores[...] = dot_nt(both, right)

            def softmax(row):
                rows = pl.ds(row, 32)
                pages = cols[pl.ds(r * SEQ + start + row, 32), 2:3]
                here = lax.broadcasted_iota(jnp.int32, (32, SEQ), 0) + (start + row)
                there = lax.broadcasted_iota(jnp.int32, (32, SEQ), 1)
                allowed = (pages == keyrow[r]) | (here == there)
                value = jnp.where(allowed, scores[rows, :] * HEAD_DIM**-0.5, masked_score)
                raised = jnp.exp(value - jnp.max(value, axis=-1, keepdims=True))
                value = raised / jnp.sum(raised, axis=-1, keepdims=True)
                probs[r, h, pl.ds(pl.multiple_of(start + row, 32), 32), :] = value.astype(BF16)

            steps(HALF, 32, softmax)
            found = dot(
                probs[r, h, pl.ds(pl.multiple_of(start, HALF), HALF), :], vk[k_rows, tile]
            )
            ctx[q_rows, tile] = jnp.where(low, pltpu.roll(found, HEAD_DIM, 1), 0.0).astype(BF16)
        return dot_nt(ctx[q_rows, :], wa[:, QK : 2 * QK])

    def chunk(r, carry):
        reduce.give(r, attend(r, 1 - p.half))
        reduce.keep(r, attend(r, p.half))
        return carry

    lax.fori_loop(0, chunks, chunk, 0)
    if ring:
        gather_f.forward()

    def collect(r, carry):
        reduce.wait(r)
        total[r] = reduce.total(r, slice(None))
        reduce.sent(r)
        reduce.close(r)
        return carry

    lax.fori_loop(0, chunks, collect, 0)
    if ring:
        gather_f.finish()


def norm_of(values):
    center = jnp.mean(values, axis=-1, keepdims=True)
    shifted = values - center
    spread = jnp.mean(shifted * shifted, axis=-1, keepdims=True)
    scale = lax.rsqrt(spread + epsilon_norm)
    return shifted * scale, scale


def norm_back(upstream, normal, scale):
    first = jnp.mean(upstream, axis=-1, keepdims=True)
    second = jnp.mean(upstream * normal, axis=-1, keepdims=True)
    return (upstream - first - normal * second) * scale


def fold(values):
    rows, width = values.shape
    return jnp.sum(values.reshape(rows // 8, 8, width), axis=0)


def forward_kernel(
    chunks,
    attn,
    hidden,
    out_grad,
    norm,
    wf,
    mixed,
    gtwo,
    xone,
    rone,
    tback,
    gup,
    gdown,
    ngrad,
    shared,
    active,
    slope,
    low_two,
    pre,
    stage,
    psend,
    precv,
    sums,
    yrecv,
    ss,
    sr,
    gs,
    gr,
    ms,
    mr,
    ml,
    ps,
    pr,
    ys,
    yr,
):
    p = Place(0)
    p.greet()
    gain_one, bias_one = norm[0:1, :], norm[1:2, :]
    gain_two, bias_two = norm[2:3, :], norm[3:4, :]

    def share_one(rows, r):
        view = shared.at[rows, :]
        return remote(view, view, ss.at[r], sr.at[r], p.pair)

    def share_two(rows, r):
        view = low_two.at[rows, :]
        return remote(view, view, gs.at[r], gr.at[r], p.pair)

    def first_norm(r, carry):
        base = r * SEQ + p.half * HALF

        def part(row):
            rows = pl.ds(pl.multiple_of(base + row, 32), 32)
            here = pl.ds(row, 32)
            normal, scale = norm_of(hidden[rows, :].astype(F32) + attn[r, here, :])
            xone[r, here, :] = normal
            rone[r, here, :] = jnp.broadcast_to(scale, (32, 128))
            shared[rows, :] = (normal * gain_one + bias_one).astype(BF16)

        steps(HALF, 32, part)
        share_one(p.own(r), r).start()
        return carry

    lax.fori_loop(0, chunks, first_norm, 0)
    first = Sum(p, 0, psend, precv, sums, yrecv, (ps, pr, ys, yr))
    second = Sum(p, 1, psend, precv, sums, yrecv, (ps, pr, ys, yr))

    def up_down(rows_at):
        rows = pl.ds(rows_at, HALF)
        pre[...] = dot(shared[rows, :], wf[:, :D])

        def gelu(row):
            here = pl.ds(row, 16)
            there = pl.ds(pl.multiple_of(rows_at + row, 16), 16)
            value = pre[here, :]
            below = 0.5 + 0.5 * lax.erf(value * math.sqrt(0.5))
            active[there, :] = (value * below).astype(BF16)
            density = jnp.exp(-0.5 * value * value) * (1.0 / math.sqrt(2.0 * math.pi))
            slope[there, :] = (below + value * density).astype(BF16)

        steps(HALF, 16, gelu)
        return dot_nt(active[rows, :], wf[:, D:])

    def feed(r, carry):
        share_one(p.other(r), r).wait_recv()
        first.give(r, up_down(pl.multiple_of(r * SEQ + (1 - p.half) * HALF, HALF)))
        first.keep(r, up_down(pl.multiple_of(r * SEQ + p.half * HALF, HALF)))
        return carry

    lax.fori_loop(0, chunks, feed, 0)
    ngrad[...] = jnp.zeros_like(ngrad)

    def mixed_here(r):
        return pltpu.make_async_copy(stage.at[r], mixed.at[p.own(r), :], ml.at[r])

    def mixed_pair(rows, r):
        return remote(stage.at[r], mixed.at[rows, :], ms.at[r], mr.at[r], p.pair)

    def back(rows_at):
        rows = pl.ds(rows_at, HALF)
        pre[...] = dot(low_two[rows, :], wf[:, D:])

        def times(row):
            here = pl.ds(row, 32)
            there = pl.ds(pl.multiple_of(rows_at + row, 32), 32)
            slope[there, :] = (pre[here, :] * slope[there, :].astype(F32)).astype(BF16)

        steps(HALF, 32, times)
        return dot_nt(slope[rows, :], wf[:, :D])

    def turn(r, carry):
        first.wait(r)
        base = r * SEQ + p.half * HALF

        def part(row):
            rows = pl.ds(pl.multiple_of(base + row, 32), 32)
            here = pl.ds(row, 32)
            residual = xone[r, here, :] * gain_one + bias_one + first.total(r, here)
            normal, scale = norm_of(residual)
            stage[r, here, :] = (normal * gain_two + bias_two).astype(BF16)
            grad = out_grad[rows, :].astype(F32)
            value = norm_back(grad * gain_two, normal, scale)
            gtwo[r, here, :] = value
            low_two[rows, :] = value.astype(BF16)
            ngrad[0:8, :] += fold(grad * normal)
            ngrad[8:16, :] += fold(grad)

        steps(HALF, 32, part)
        share_two(p.own(r), r).start()
        mixed_here(r).start()
        mixed_pair(p.own(r), r).start()
        share_two(p.other(r), r).wait_recv()
        first.sent(r)
        second.give(r, back(pl.multiple_of(r * SEQ + (1 - p.half) * HALF, HALF)))
        second.keep(r, back(pl.multiple_of(r * SEQ + p.half * HALF, HALF)))
        return carry

    lax.fori_loop(0, chunks, turn, 0)

    def weights(row):
        rows = pl.ds(row, 128)
        gup[rows, :] = dot_tn(shared[:, rows], slope[...])
        gdown[rows, :] = dot_tn(low_two[:, rows], active[...])

    steps(D, 128, weights)

    def collect(r, carry):
        second.wait(r)
        tback[r] = second.total(r, slice(None))
        second.sent(r)
        first.close(r)
        second.close(r)
        share_one(p.own(r), r).wait_send()
        share_two(p.own(r), r).wait_send()
        mixed_here(r).wait()
        mixed_pair(p.own(r), r).wait_send()
        mixed_pair(p.other(r), r).wait_recv()
        return carry

    lax.fori_loop(0, chunks, collect, 0)


class Scatter:
    def __init__(self, place, share, src, xsend, xrecv, zsend, zrecv, sems):
        self.p, self.share, self.src = place, share, src
        self.xsend, self.xrecv, self.zsend, self.zrecv = xsend, xrecv, zsend, zrecv
        self.xs, self.xr, self.zs, self.zr = sems

    def rows(self, k, x):
        d = ((self.p.z + k) % self.p.ring) * 2 + x
        return pl.ds(pl.multiple_of(d * self.share, self.share), self.share)

    def xcopy(self, k):
        return remote(
            self.xsend.at[k], self.xrecv.at[k], self.xs.at[k], self.xr.at[k], self.p.xdev
        )

    def zcopy(self, k):
        return remote(
            self.zsend.at[k], self.zrecv.at[k], self.zs.at[k], self.zr.at[k], self.p.zdev(k)
        )

    def order(self):
        return list(range(1, self.p.ring)) + [0]

    def start(self):
        for k in self.order():
            self.xsend[k] = self.src[self.rows(k, 1 - self.p.x), :].astype(BF16)
            self.xcopy(k).start()

    def middle(self):
        for k in range(1, self.p.ring):
            self.xcopy(k).wait_recv()
            value = self.src[self.rows(k, self.p.x), :] + self.xrecv[k].astype(F32)
            self.zsend[k] = value.astype(BF16)
            self.zcopy(k).start()

    def finish(self, out):
        self.xcopy(0).wait_recv()
        value = self.src[self.rows(0, self.p.x), :] + self.xrecv[0].astype(F32)
        for k in range(1, self.p.ring):
            self.zcopy(k).wait_recv()
            value = value + self.zrecv[k].astype(F32)
        out[...] = value
        for k in range(self.p.ring):
            self.xcopy(k).wait_send()
        for k in range(1, self.p.ring):
            self.zcopy(k).wait_send()


def backward_kernel(
    ring,
    chunks,
    tback,
    gtwo,
    xone,
    rone,
    norm,
    lq,
    rk,
    vk,
    probs,
    ctx,
    hidden,
    emb,
    wtx,
    wop,
    gup,
    gdown,
    ntwo,
    igrad,
    outa,
    outup,
    outdown,
    nout,
    low_one,
    gone,
    gtext,
    gbox,
    gscore,
    gctx,
    dprob,
    ga,
    stage,
    psend,
    precv,
    sums,
    yrecv,
    nbuf,
    nrecv,
    *rest,
):
    scatters, rest = rest[:12], rest[12:]
    (gs, gr, ims, imr, iml, ps, pr, ys, yr, ns, nr), rest = rest[:11], rest[11:]
    p = Place(ring)
    p.greet()
    gain_one = norm[0:1, :]
    if ring:
        share = outup.shape[0]
        up = Scatter(p, share, gup, *scatters[0:4], [s.at[0] for s in rest])
        down = Scatter(p, share, gdown, *scatters[4:8], [s.at[1] for s in rest])
        att = Scatter(p, share, ga, *scatters[8:12], [s.at[2] for s in rest])
        up.start()
        down.start()
    nbuf[0:16, :] = jnp.zeros((16, D), F32)
    nbuf[16:32, :] = ntwo[...]

    def share_one(rows, r):
        view = low_one.at[rows, :]
        return remote(view, view, gs.at[r], gr.at[r], p.pair)

    def first_norm(r, carry):
        base = r * SEQ + p.half * HALF

        def part(row):
            rows = pl.ds(pl.multiple_of(base + row, 32), 32)
            here = pl.ds(row, 32)
            grad = gtwo[r, here, :] + tback[r, here, :]
            normal = xone[r, here, :]
            value = norm_back(grad * gain_one, normal, rone[r, here, 0:1])
            gone[r, here, :] = value
            low_one[rows, :] = value.astype(BF16)
            nbuf[0:8, :] += fold(grad * normal)
            nbuf[8:16, :] += fold(grad)

        steps(HALF, 32, part)
        share_one(p.own(r), r).start()
        return carry

    lax.fori_loop(0, chunks, first_norm, 0)
    for row in range(4):
        nbuf[row : row + 1, :] = jnp.sum(nbuf[row * 8 : row * 8 + 8, :], axis=0, keepdims=True)
    if ring:
        norm_pair = remote(nbuf.at[0:8], nrecv.at[0], ns.at[0], nr.at[0], p.pair)
        norm_pair.start()
    reduce = Sum(p, 0, psend, precv, sums, yrecv, (ps, pr, ys, yr))
    score_scale = HEAD_DIM**-0.5

    def attend(r):
        k_rows = pl.ds(pl.multiple_of(r * SEQ, SEQ), SEQ)
        for side in range(2):
            rows = pl.ds(pl.multiple_of(r * SEQ + side * HALF, HALF), HALF)
            gctx[side * HALF : (side + 1) * HALF, :] = dot(low_one[rows, :], wop[...]).astype(BF16)
        low = lower_half((SEQ, 128))
        for h in range(HEADS):
            tile = slice(h * 128, (h + 1) * 128)
            right_v = vk[k_rows, tile]
            right_k = rk[k_rows, tile]
            dprob[...] = dot_nt(gctx[:, tile], right_v)

            def soften(row):
                rows = pl.ds(row, 32)
                grad = dprob[rows, :]
                prob = probs[r, h, rows, :].astype(F32)
                weighted = jnp.sum(prob * grad, axis=-1, keepdims=True)
                gscore[rows, :] = (prob * (grad - weighted)).astype(BF16)

            steps(SEQ, 32, soften)
            left = dot(gscore[...], right_k) * score_scale
            right = dot_tn(gscore[...], lq[k_rows, tile]) * score_scale
            value = dot_tn(probs[r, h], gctx[:, tile])
            gtext[k_rows, tile] = jnp.where(
                low, left + pltpu.roll(left, HEAD_DIM, 1), right + pltpu.roll(right, HEAD_DIM, 1)
            ).astype(BF16)
            gbox[k_rows, tile] = jnp.where(low, right, left).astype(BF16)
            gtext[k_rows, QK + h * 128 : QK + (h + 1) * 128] = value.astype(BF16)

    def partial_of(rows):
        return dot_nt(gtext[rows, :], wtx[...])

    def igrad_here(r):
        return pltpu.make_async_copy(stage.at[r], igrad.at[p.own(r), :], iml.at[r])

    def igrad_pair(rows, r):
        return remote(stage.at[r], igrad.at[rows, :], ims.at[r], imr.at[r], p.pair)

    def chunk(r, carry):
        share_one(p.other(r), r).wait_recv()
        attend(r)
        reduce.give(r, partial_of(p.other(r)))
        reduce.keep(r, partial_of(p.own(r)))
        return carry

    lax.fori_loop(0, chunks, chunk, 0)

    def weights(row):
        rows = pl.ds(row, 128)
        text = dot_tn(hidden[:, rows], gtext[...])
        ga[rows, :QK] = text[:, :QK]
        ga[rows, QK : 2 * QK] = text[:, QK:] + dot_tn(low_one[:, rows], ctx[...])
        ga[rows, 2 * QK :] = dot_tn(emb[:, rows], gbox[...])

    steps(D, 128, weights)
    if ring:
        att.start()
        up.middle()
        down.middle()
        norm_pair.wait_recv()
        nbuf[8:16, :] = nbuf[0:8, :] + nrecv[0]
        norm_x = remote(nbuf.at[8:16], nrecv.at[1], ns.at[1], nr.at[1], p.xdev)
        norm_x.start()
        att.middle()
        norm_x.wait_recv()
        nbuf[16:24, :] = nbuf[8:16, :] + nrecv[1]
        norm_z = [
            remote(nbuf.at[16:24], nrecv.at[1 + k], ns.at[1 + k], nr.at[1 + k], p.zdev(k))
            for k in range(1, ring)
        ]
        for copy in norm_z:
            copy.start()

    def collect(r, carry):
        reduce.wait(r)

        def part(row):
            here = pl.ds(row, 32)
            stage[r, here, :] = gone[r, here, :] + reduce.total(r, here)

        steps(HALF, 32, part)
        igrad_here(r).start()
        igrad_pair(p.own(r), r).start()
        reduce.sent(r)
        reduce.close(r)
        share_one(p.own(r), r).wait_send()
        return carry

    lax.fori_loop(0, chunks, collect, 0)
    if ring:
        up.finish(outup)
        down.finish(outdown)
        att.finish(outa)
        summed = nbuf[16:24, :]
        for k in range(1, ring):
            norm_z[k - 1].wait_recv()
            summed = summed + nrecv[1 + k]
        nout[...] = summed
        for copy in [norm_pair, norm_x] + norm_z:
            copy.wait_send()
    else:
        outa[...] = ga[...]
        nout[...] = nbuf[0:8, :]

    def settle(r, carry):
        igrad_here(r).wait()
        igrad_pair(p.own(r), r).wait_send()
        igrad_pair(p.other(r), r).wait_recv()
        return carry

    lax.fori_loop(0, chunks, settle, 0)


def adam_step(weight, gradient, moment, second, rate, decay):
    moment_new = beta_first * moment + (1.0 - beta_first) * gradient
    second_new = beta_second * second + (1.0 - beta_second) * gradient * gradient
    moment_hat = moment_new / (1.0 - beta_first**STEP)
    second_hat = second_new / (1.0 - beta_second**STEP)
    weight_new = weight - rate * (
        moment_hat / (jnp.sqrt(second_hat) + epsilon_adam) + decay * weight
    )
    return (weight_new, moment_new, second_new)


def vmem():
    return pl.BlockSpec(memory_space=pltpu.VMEM)


def dma(*shape):
    return pltpu.SemaphoreType.DMA(shape)


def sum_scratch(chunks, sums):
    return [pltpu.VMEM((chunks, HALF, D), BF16)] * 2 + [
        pltpu.VMEM((sums, chunks, HALF, D), BF16)
    ] * 2


def params(number):
    return pltpu.CompilerParams(
        collective_id=number, has_side_effects=True, vmem_limit_bytes=VMEM_LIMIT
    )


def interleave(first, second):
    rows = first.shape[0]
    pair = [part.reshape(rows, HEADS, 1, HEAD_DIM) for part in (first, second)]
    return jnp.concatenate(pair, axis=2).reshape(rows, QK)


def split_pair(both):
    rows = both.shape[0]
    pair = both.reshape(rows, HEADS, 2, HEAD_DIM)
    return pair[:, :, 0].reshape(rows, QK // 2), pair[:, :, 1].reshape(rows, QK // 2)


def box_lanes():
    quarter = D // 4
    ladder = jnp.arange(quarter).astype(F32)
    frequency = jnp.exp(ladder * (-math.log(10000.0) / quarter))
    zero, one = jnp.zeros((quarter,), F32), jnp.ones((quarter,), F32)
    return jnp.stack(
        [
            jnp.concatenate([frequency] * 4),
            jnp.concatenate([zero, zero, one, one]),
            jnp.concatenate([zero, one, zero, one]),
        ]
        + [jnp.zeros((D,), F32)] * 5
    )


def per_device(
    devices,
    hidden_in,
    page_ids,
    pad_mask,
    boxes,
    out_grad,
    attn_in,
    attn_in_moment,
    attn_in_second,
    attn_out,
    attn_out_moment,
    attn_out_second,
    ffn_in,
    ffn_in_moment,
    ffn_in_second,
    ffn_out,
    ffn_out_moment,
    ffn_out_second,
    norm_weight,
    norm_moment,
    norm_second,
):
    tokens = hidden_in.shape[0]
    chunks = tokens // SEQ
    share = attn_in.shape[1]
    ring = devices // 2 if share % 16 == 0 else 0
    low_in = attn_in.astype(BF16)
    packa = jnp.concatenate(
        [
            interleave(low_in[0], low_in[1]),
            interleave(attn_out.T.astype(BF16), low_in[2]),
            interleave(low_in[4], low_in[3]),
        ],
        axis=1,
    )
    packf = jnp.concatenate([ffn_in.astype(BF16), ffn_out.T.astype(BF16)], axis=1)
    pnorm = jnp.pad(norm_weight, ((0, 4), (0, -share % 128)))
    if not ring:
        packa = lax.all_gather(packa, "dp", axis=0, tiled=True)
        wf_full = lax.all_gather(packf, "dp", axis=0, tiled=True)
        norm_full = lax.all_gather(norm_weight, "dp", axis=1, tiled=True)
        packf = packf[:16]
    pages = page_ids.astype(F32)
    cols = jnp.stack([boxes[:, 0].astype(F32), boxes[:, 1].astype(F32), pages], axis=1)
    keyrow = jnp.where(pad_mask == 0, pages, -1.0).reshape(chunks, 1, SEQ)
    own = jax.ShapeDtypeStruct((chunks, HALF, D), F32)
    wide = jax.ShapeDtypeStruct((tokens, QK), BF16)
    whole = jax.ShapeDtypeStruct((tokens, D), BF16)
    wtx, wop, wf, nbuf, lq, rk, vk, probs, ctx, emb, attn = pl.pallas_call(
        partial(attend_kernel, ring, chunks),
        out_shape=(
            jax.ShapeDtypeStruct((D, D), BF16),
            jax.ShapeDtypeStruct((D, QK), BF16),
            jax.ShapeDtypeStruct((D, FFN) if ring else (16, 128), BF16),
            jax.ShapeDtypeStruct((devices,) + pnorm.shape if ring else (1, 8, 128), F32),
            wide,
            wide,
            wide,
            jax.ShapeDtypeStruct((chunks, HEADS, SEQ, SEQ), BF16),
            wide,
            whole,
            own,
        ),
        in_specs=[vmem()] * 7,
        out_specs=(vmem(),) * 11,
        scratch_shapes=[pltpu.VMEM((D, ATT), BF16), pltpu.VMEM((HALF, SEQ), F32)]
        + sum_scratch(chunks, 1)
        + [dma(3, max(ring, 1))] * 4
        + [dma(2, chunks)] * 4,
        compiler_params=params(0),
    )(hidden_in, cols, keyrow, box_lanes(), packa, packf, pnorm)
    if ring:
        norm_full = nbuf[:, :4, :share].transpose(1, 0, 2).reshape(4, D)
    else:
        wf = wf_full
    norm_full = jnp.pad(norm_full, ((0, 4), (0, 0)))
    grad = jax.ShapeDtypeStruct((D, D), F32)
    mixed, gtwo, xone, rone, tback, gup, gdown, ntwo = pl.pallas_call(
        partial(forward_kernel, chunks),
        out_shape=(
            whole,
            own,
            own,
            jax.ShapeDtypeStruct((chunks, HALF, 128), F32),
            own,
            grad,
            grad,
            jax.ShapeDtypeStruct((16, D), F32),
        ),
        in_specs=[vmem()] * 5,
        out_specs=(pl.BlockSpec(memory_space=pl.ANY),) + (vmem(),) * 7,
        scratch_shapes=[pltpu.VMEM((tokens, D), BF16)] * 4
        + [pltpu.VMEM((HALF, D), F32), pltpu.VMEM((chunks, HALF, D), BF16)]
        + sum_scratch(chunks, 2)
        + [dma(chunks)] * 7
        + [dma(2, chunks)] * 4,
        compiler_params=params(1),
    )(attn, hidden_in, out_grad, norm_full, wf)
    count = max(ring, 1)
    buffers = []
    for width in (D, D, ATT):
        buffers += [pltpu.VMEM((count, share, width) if ring else (16, 128), BF16)] * 4
    small = (share, D) if ring else (16, 128)
    input_grad, reda, redup, reddown, nred = pl.pallas_call(
        partial(backward_kernel, ring, chunks),
        out_shape=(
            jax.ShapeDtypeStruct((tokens, D), F32),
            jax.ShapeDtypeStruct((share, ATT) if ring else (D, ATT), F32),
            jax.ShapeDtypeStruct(small, F32),
            jax.ShapeDtypeStruct(small, F32),
            jax.ShapeDtypeStruct((8, D), F32),
        ),
        in_specs=[vmem()] * 17,
        out_specs=(pl.BlockSpec(memory_space=pl.ANY),) + (vmem(),) * 4,
        scratch_shapes=[
            pltpu.VMEM((tokens, D), BF16),
            pltpu.VMEM((chunks, HALF, D), F32),
            pltpu.VMEM((tokens, D), BF16),
            pltpu.VMEM((tokens, QK), BF16),
            pltpu.VMEM((SEQ, SEQ), BF16),
            pltpu.VMEM((SEQ, QK), BF16),
            pltpu.VMEM((SEQ, SEQ), F32),
            pltpu.VMEM((D, ATT), F32),
            pltpu.VMEM((chunks, HALF, D), F32),
        ]
        + sum_scratch(chunks, 1)
        + [pltpu.VMEM((32, D), F32), pltpu.VMEM((count + 1, 8, D), F32)]
        + buffers
        + [dma(chunks)] * 5
        + [dma(2, chunks)] * 4
        + [dma(count + 1)] * 2
        + [dma(3, count)] * 4,
        compiler_params=params(2),
    )(
        tback,
        gtwo,
        xone,
        rone,
        norm_full,
        lq,
        rk,
        vk,
        probs,
        ctx,
        hidden_in,
        emb,
        wtx,
        wop,
        gup,
        gdown,
        ntwo,
    )
    position = lax.axis_index("dp")
    if not ring:
        reda, redup, reddown = (
            lax.psum_scatter(part, "dp", scatter_dimension=0, tiled=True)
            for part in (reda, gup, gdown)
        )
        nred = lax.psum(nred, ("dp", "mp")) * 0.5
    grad_norm = lax.dynamic_slice_in_dim(nred[:4], position * share, share, 1)
    grad_q, grad_k = split_pair(reda[:, :QK])
    grad_o, grad_v = split_pair(reda[:, QK : 2 * QK])
    grad_kb, grad_qb = split_pair(reda[:, 2 * QK :])
    grad_in = jnp.stack([grad_q, grad_k, grad_v, grad_qb, grad_kb])
    new_in = adam_step(
        attn_in, grad_in, attn_in_moment, attn_in_second, rate_matrix, decay_matrix
    )
    new_out = adam_step(
        attn_out, grad_o.T, attn_out_moment, attn_out_second, rate_matrix, decay_matrix
    )
    new_up = adam_step(ffn_in, redup, ffn_in_moment, ffn_in_second, rate_matrix, decay_matrix)
    new_down = adam_step(
        ffn_out, reddown.T, ffn_out_moment, ffn_out_second, rate_matrix, decay_matrix
    )
    new_norm = adam_step(norm_weight, grad_norm, norm_moment, norm_second, rate_norm, 0.0)
    return (mixed, input_grad) + new_in + new_out + new_up + new_down + new_norm


def solution(mesh):
    rows = P("dp", None)
    into = P(None, "dp", "mp")
    out = P("mp", "dp")
    up = P("dp", "mp")
    norm = P(None, "dp")
    return jax.shard_map(
        partial(per_device, mesh.shape["dp"]),
        mesh=mesh,
        in_specs=(rows, P("dp"), P("dp"), rows, rows)
        + (into,) * 3
        + (out,) * 3
        + (up,) * 3
        + (out,) * 3
        + (norm,) * 3,
        out_specs=(rows, rows) + (into,) * 3 + (out,) * 3 + (up,) * 3 + (out,) * 3 + (norm,) * 3,
        check_vma=False,
    )
```

```python
from functools import partial
import math

import jax
import jax.numpy as jnp
from jax import lax
from jax.experimental import pallas as pl
from jax.experimental.pallas import tpu as pltpu
from jax.sharding import PartitionSpec as P

D = 768
HEAD_DIM = 64
SEQ = 512
HALF = SEQ // 2
STEP = 10
HEADS = 3
QK = HEADS * 128
ATT = 3 * QK
FFN = 2 * D

epsilon_norm = 1e-12
epsilon_adam = 1e-08
beta_first = 0.9
beta_second = 0.999
rate_matrix = 0.05
rate_norm = 0.2
decay_matrix = 0.01
masked_score = -1e30

F32 = jnp.float32
BF16 = jnp.bfloat16
VMEM_LIMIT = 60 * 1024 * 1024


def dot(a, b):
    return jnp.dot(a, b, preferred_element_type=F32)


def dot_nt(a, b):
    return lax.dot_general(a, b, (((1,), (1,)), ((), ())), preferred_element_type=F32)


def dot_tn(a, b):
    return lax.dot_general(a, b, (((0,), (0,)), ((), ())), preferred_element_type=F32)


def remote(src, dst, send, recv, device):
    return pltpu.make_async_remote_copy(
        src_ref=src,
        dst_ref=dst,
        send_sem=send,
        recv_sem=recv,
        device_id=device,
        device_id_type=pl.DeviceIdType.MESH,
    )


def steps(total, size, body):
    def run(i, carry):
        body(pl.multiple_of(i * size, size))
        return carry

    lax.fori_loop(0, total // size, run, 0)


def lower_half(shape):
    return lax.broadcasted_iota(jnp.int32, shape, len(shape) - 1) % 128 < HEAD_DIM


class Place:
    def __init__(self, ring):
        self.dp = lax.axis_index("dp")
        self.mp = lax.axis_index("mp")
        self.half = self.mp % 2
        self.pair = (self.dp, self.mp + 1 - 2 * self.half)
        self.across = (self.dp, (self.mp + 2) % 4)
        self.ring = ring
        self.z = self.dp // 2
        self.x = self.dp % 2
        self.xdev = (self.dp + 1 - 2 * self.x, self.mp)

    def zdev(self, k):
        return (((self.z + k) % self.ring) * 2 + self.x, self.mp)

    def came(self, k):
        return ((self.z + self.ring - k) % self.ring) * 2 + self.x

    def came_other(self, k):
        return ((self.z + self.ring - k) % self.ring) * 2 + 1 - self.x

    def greet(self):
        peers = [self.pair, self.across]
        if self.ring:
            peers += [self.xdev] + [self.zdev(k) for k in range(1, self.ring)]
        barrier = pltpu.get_barrier_semaphore()
        for peer in peers:
            pl.semaphore_signal(
                barrier, inc=1, device_id=peer, device_id_type=pl.DeviceIdType.MESH
            )
        pl.semaphore_wait(barrier, len(peers))

    def own(self, r):
        return pl.ds(pl.multiple_of(r * SEQ + self.half * HALF, HALF), HALF)

    def other(self, r):
        return pl.ds(pl.multiple_of(r * SEQ + (1 - self.half) * HALF, HALF), HALF)


class Gather:
    def __init__(self, place, kind, src, at, sems):
        self.p, self.src, self.at = place, src, at
        zs, zr, xs, xr = sems
        self.zs, self.zr, self.xs, self.xr = (
            zs.at[kind],
            zr.at[kind],
            xs.at[kind],
            xr.at[kind],
        )

    def along(self, k):
        p = self.p
        return remote(self.src, self.at(p.dp), self.zs.at[k], self.zr.at[k], p.zdev(k))

    def onward(self, k):
        p = self.p
        src = self.src if isinstance(k, int) and k == 0 else self.at(p.came(k))
        return remote(src, self.at(p.came(k)), self.xs.at[k], self.xr.at[k], p.xdev)

    def start_along(self):
        for k in range(1, self.p.ring):
            self.along(k).start()

    def forward(self, k):
        p = self.p
        remote(
            self.src, self.at(p.came(k)), self.zs.at[k], self.zr.at[k], p.zdev(k)
        ).wait_recv()
        self.onward(k).start()

    def forward_all(self):
        for k in range(1, self.p.ring):
            self.forward(k)

    def finish(self):
        p = self.p
        for k in range(p.ring):
            remote(
                self.src, self.at(p.came_other(k)), self.xs.at[k], self.xr.at[k], p.xdev
            ).wait_recv()
        for k in range(1, p.ring):
            self.along(k).wait_send()
        for k in range(p.ring):
            self.onward(k).wait_send()


class Sum:
    def __init__(self, place, parity, psend, precv, sums, yrecv, sems):
        self.p = place
        self.psend, self.precv = psend, precv
        self.sums, self.yrecv = sums, yrecv.at[parity]
        ps, pr, ys, yr = sems
        self.ps, self.pr, self.ys, self.yr = (
            ps.at[parity],
            pr.at[parity],
            ys.at[parity],
            yr.at[parity],
        )

    def to_pair(self, r):
        return remote(
            self.psend.at[r], self.precv.at[r], self.ps.at[r], self.pr.at[r], self.p.pair
        )

    def over(self, r):
        return remote(
            self.sums.at[r], self.yrecv.at[r], self.ys.at[r], self.yr.at[r], self.p.across
        )

    def give(self, r, value):
        self.psend[r] = value.astype(BF16)
        self.to_pair(r).start()

    def keep(self, r, value):
        self.to_pair(r).wait_recv()
        self.sums[r] = (value + self.precv[r].astype(F32)).astype(BF16)
        self.over(r).start()

    def wait(self, r):
        self.over(r).wait_recv()

    def total(self, r, rows):
        return self.sums[r, rows, :].astype(F32) + self.yrecv[r, rows, :].astype(F32)

    def close(self, r):
        self.to_pair(r).wait_send()
        self.over(r).wait_send()


def rolled(value):
    return pltpu.roll(value.astype(F32), HEAD_DIM, 1)


def embed_rows(coords, lanes, out, row):
    rows = pl.ds(row, 64)
    here = coords[rows, :]
    across, upward = here[:, 0:1], here[:, 1:2]
    frequency, second, shift = lanes[0:1, :], lanes[1:2, :], lanes[2:3, :]
    angle = (across + (upward - across) * second) * frequency
    turns = jnp.round(angle * (2.0 / math.pi))
    rest = ((angle - turns * 1.5703125) - turns * 4.837512969970703125e-4) - turns * (
        7.54978995489188216e-8
    )
    square = rest * rest
    sine = rest + rest * square * (
        -1.6666654611e-1 + square * (8.3321608736e-3 + square * -1.9515295891e-4)
    )
    cosine = (
        1.0
        - 0.5 * square
        + square
        * square
        * (
            4.166664568298827e-2
            + square * (-1.388731625493765e-3 + square * 2.443315711809948e-5)
        )
    )
    quarter = (turns + shift).astype(jnp.int32)
    value = jnp.where((quarter & 1) == 1, cosine, sine)
    out[rows, :] = jnp.where((quarter & 2) == 2, -value, value).astype(BF16)


def norm_of(values):
    center = jnp.mean(values, axis=-1, keepdims=True)
    shifted = values - center
    spread = jnp.mean(shifted * shifted, axis=-1, keepdims=True)
    scale = lax.rsqrt(spread + epsilon_norm)
    return shifted * scale, scale


def norm_back(upstream, normal, scale):
    first = jnp.mean(upstream, axis=-1, keepdims=True)
    second = jnp.mean(upstream * normal, axis=-1, keepdims=True)
    return (upstream - first - normal * second) * scale


def fold(values):
    rows, width = values.shape
    return jnp.sum(values.reshape(rows // 8, 8, width), axis=0)


class Scatter:
    def __init__(self, place, share, src, width, xsend, xrecv, zsend, zrecv, sems):
        self.p, self.share, self.src, self.width = place, share, src, width
        self.xsend, self.xrecv, self.zsend, self.zrecv = xsend, xrecv, zsend, zrecv
        self.xs, self.xr, self.zs, self.zr = sems

    def rows(self, k, x):
        d = ((self.p.z + k) % self.p.ring) * 2 + x
        return pl.ds(pl.multiple_of(d * self.share, self.share), self.share)

    def xcopy(self, k):
        return remote(
            self.xsend.at[k, :, : self.width],
            self.xrecv.at[k],
            self.xs.at[k],
            self.xr.at[k],
            self.p.xdev,
        )

    def zcopy(self, k):
        return remote(
            self.zsend.at[k, :, : self.width],
            self.zrecv.at[k],
            self.zs.at[k],
            self.zr.at[k],
            self.p.zdev(k),
        )

    def start(self, k):
        value = self.src[self.rows(k, 1 - self.p.x), : self.width]
        self.xsend[k, :, : self.width] = value.astype(BF16)
        self.xcopy(k).start()

    def middle(self, k):
        self.xcopy(k).wait_recv()
        value = self.src[self.rows(k, self.p.x), : self.width] + self.xrecv[k].astype(F32)
        self.zsend[k, :, : self.width] = value.astype(BF16)
        self.zcopy(k).start()

    def own(self, out):
        self.xcopy(0).wait_recv()
        out[...] = self.src[self.rows(0, self.p.x), : self.width] + self.xrecv[0].astype(F32)

    def sent(self):
        for k in range(self.p.ring):
            self.xcopy(k).wait_send()
        for k in range(1, self.p.ring):
            self.zcopy(k).wait_send()

    def finish(self, out):
        value = out[...]
        for k in range(1, self.p.ring):
            self.zcopy(k).wait_recv()
            value = value + self.zrecv[k].astype(F32)
        out[...] = value


def layer_kernel(
    ring,
    chunks,
    hidden,
    cols,
    keyrow,
    lanes,
    packa,
    packf,
    pnorm,
    out_grad,
    mixed,
    igrad,
    outa,
    outf,
    nout,
    wa,
    wf,
    nbuf,
    norm,
    wtx,
    wop,
    lq,
    rk,
    vk,
    probs,
    ctx,
    emb,
    big,
    ograd,
    xone,
    rone,
    gtwo,
    shared,
    active,
    slope,
    low_two,
    stage,
    grads,
    nsum,
    nrecv,
    xsend,
    zsend,
    fxrecv,
    fzrecv,
    axrecv,
    azrecv,
    psend,
    precv,
    sums,
    yrecv,
    free,
    gather_zs,
    gather_zr,
    gather_xs,
    gather_xr,
    ps,
    pr,
    ys,
    yr,
    share_s,
    share_r,
    out_s,
    out_r,
    out_l,
    ol,
    ns,
    nr,
    sxs,
    sxr,
    szs,
    szr,
):
    p = Place(ring)
    tokens = hidden.shape[0]

    def ograd_copy(r):
        return pltpu.make_async_copy(out_grad.at[p.own(r), :], ograd.at[r], ol.at[r])

    for r in range(chunks):
        ograd_copy(r).start()
    p.greet()
    sums_sems = (ps, pr, ys, yr)
    sum_a, sum_b, sum_c, sum_d = (
        Sum(p, stage_number % 2, psend, precv, sums, yrecv, sums_sems)
        for stage_number in range(4)
    )
    if ring:
        share = packa.shape[0]
        gather_sems = (gather_zs, gather_zr, gather_xs, gather_xr)

        def rows_of(ref):
            return lambda d: ref.at[pl.ds(pl.multiple_of(d * share, share), share), :]

        gather_a = Gather(p, 0, packa, rows_of(wa), gather_sems)
        gather_f = Gather(p, 1, packf, rows_of(wf), gather_sems)
        gather_n = Gather(p, 2, pnorm, lambda d: nbuf.at[d], gather_sems)
        gather_a.start_along()
        gather_a.onward(0).start()
        mine = pl.ds(pl.multiple_of(p.dp * share, share), share)
        wa[mine, :] = packa[...]
        wf[mine, :] = packf[...]
        nbuf[p.dp] = pnorm[...]
    else:
        wa[...] = packa[...]
        wf[...] = packf[...]
        norm[...] = pnorm[...]
    steps(tokens, 64, partial(embed_rows, cols, lanes, emb))
    if ring:
        gather_a.forward_all()
        gather_f.start_along()
        gather_n.start_along()
        gather_a.finish()
        gather_f.onward(0).start()
        gather_n.onward(0).start()

    def build(row):
        rows = pl.ds(row, 256)
        low = lower_half((256, 128))
        wtx[rows, :QK] = wa[rows, :QK]
        for h in range(HEADS):
            qk_cols = slice(h * 128, (h + 1) * 128)
            ov_cols = slice(QK + h * 128, QK + (h + 1) * 128)
            ov = wa[rows, ov_cols].astype(F32)
            wtx[rows, ov_cols] = jnp.where(low, rolled(wa[rows, qk_cols]), ov).astype(BF16)
            wop[rows, qk_cols] = jnp.where(low, 0.0, rolled(ov)).astype(BF16)

    steps(D, 256, build)

    def project(row):
        rows = pl.ds(row, HALF)
        text = dot(hidden[rows, :], wtx[...])
        box = dot(emb[rows, :], wa[:, 2 * QK :])
        low = lower_half((HALF, QK))
        lq[rows, :] = jnp.where(low, text[:, :QK], box).astype(BF16)
        rk[rows, :] = jnp.where(low, box, text[:, :QK]).astype(BF16)
        vk[rows, :] = text[:, QK:].astype(BF16)

    steps(tokens, HALF, project)
    scores = big.at[:HALF, :SEQ]
    pre = big.at[:HALF, :]
    dprob = big.at[:, :SEQ]

    def attend(r, side):
        start = pl.multiple_of(side * HALF, HALF)
        q_rows = pl.ds(pl.multiple_of(r * SEQ + start, HALF), HALF)
        k_rows = pl.ds(pl.multiple_of(r * SEQ, SEQ), SEQ)
        low = lower_half((HALF, 128))
        pages = cols[q_rows, 2:3]
        here = lax.broadcasted_iota(jnp.int32, (HALF, SEQ), 0) + start
        there = lax.broadcasted_iota(jnp.int32, (HALF, SEQ), 1)
        allowed = (pages == keyrow[r]) | (here == there)
        for h in range(HEADS):
            tile = slice(h * 128, (h + 1) * 128)
            left = lq[q_rows, tile]
            both = jnp.concatenate([left, jnp.where(low, left, jnp.zeros_like(left))], axis=1)
            right = jnp.concatenate([rk[k_rows, tile], vk[k_rows, tile]], axis=1)
            scores[...] = dot_nt(both, right)
            value = jnp.where(allowed, scores[...] * HEAD_DIM**-0.5, masked_score)
            raised = jnp.exp(value - jnp.max(value, axis=-1, keepdims=True))
            value = raised / jnp.sum(raised, axis=-1, keepdims=True)
            probs[r, h, pl.ds(start, HALF), :] = value.astype(BF16)
            found = dot(probs[r, h, pl.ds(start, HALF), :], vk[k_rows, tile])
            ctx[q_rows, tile] = jnp.where(low, pltpu.roll(found, HEAD_DIM, 1), 0.0).astype(BF16)
        return dot_nt(ctx[q_rows, :], wa[:, QK : 2 * QK])

    spread = ring - 1 == chunks

    def stage_a(r, carry):
        sum_a.give(r, attend(r, 1 - p.half))
        sum_a.keep(r, attend(r, p.half))
        if spread:
            gather_f.forward(r + 1)
        return carry

    lax.fori_loop(0, chunks, stage_a, 0)
    if ring:
        if not spread:
            gather_f.forward_all()
        gather_n.forward_all()
        gather_n.finish()
        norm[...] = jnp.concatenate([nbuf[d, :, :share] for d in range(2 * ring)], axis=1)
        gather_f.finish()
    gain_one, bias_one = norm[0:1, :], norm[1:2, :]
    gain_two, bias_two = norm[2:3, :], norm[3:4, :]

    def pass_on(ref, number, rows, r):
        view = ref.at[rows, :]
        return remote(view, view, share_s.at[number, r], share_r.at[number, r], p.pair)

    def up_down(rows_at):
        rows = pl.ds(rows_at, HALF)
        pre[...] = dot(shared[rows, :], wf[:, :D])

        def gelu(row):
            here = pl.ds(row, 64)
            there = pl.ds(pl.multiple_of(rows_at + row, 64), 64)
            value = pre[here, :]
            below = 0.5 + 0.5 * lax.erf(value * math.sqrt(0.5))
            active[there, :] = (value * below).astype(BF16)
            density = jnp.exp(-0.5 * value * value) * (1.0 / math.sqrt(2.0 * math.pi))
            slope[there, :] = (below + value * density).astype(BF16)

        steps(HALF, 64, gelu)
        return dot_nt(active[rows, :], wf[:, D:])

    def own_at(r):
        return pl.multiple_of(r * SEQ + p.half * HALF, HALF)

    def other_at(r):
        return pl.multiple_of(r * SEQ + (1 - p.half) * HALF, HALF)

    def stage_b(r, carry):
        sum_a.wait(r)

        def part(row):
            rows = pl.ds(pl.multiple_of(own_at(r) + row, 128), 128)
            here = pl.ds(row, 128)
            normal, scale = norm_of(hidden[rows, :].astype(F32) + sum_a.total(r, here))
            xone[r, here, :] = normal
            rone[r, here, :] = jnp.broadcast_to(scale, (128, 128))
            shared[rows, :] = (normal * gain_one + bias_one).astype(BF16)

        steps(HALF, 128, part)
        pass_on(shared, 0, p.own(r), r).start()
        sum_a.close(r)
        pass_on(shared, 0, p.other(r), r).wait_recv()
        sum_b.give(r, up_down(other_at(r)))
        sum_b.keep(r, up_down(own_at(r)))
        return carry

    lax.fori_loop(0, chunks, stage_b, 0)
    nsum[...] = jnp.zeros_like(nsum)

    def mixed_here(r):
        return pltpu.make_async_copy(stage.at[r], mixed.at[p.own(r), :], out_l.at[0, r])

    def mixed_pair(rows, r):
        return remote(stage.at[r], mixed.at[rows, :], out_s.at[0, r], out_r.at[0, r], p.pair)

    def back(rows_at):
        rows = pl.ds(rows_at, HALF)
        pre[...] = dot(low_two[rows, :], wf[:, D:])

        def times(row):
            here = pl.ds(row, 64)
            there = pl.ds(pl.multiple_of(rows_at + row, 64), 64)
            slope[there, :] = (pre[here, :] * slope[there, :].astype(F32)).astype(BF16)

        steps(HALF, 64, times)
        return dot_nt(slope[rows, :], wf[:, :D])

    def stage_c(r, carry):
        ograd_copy(r).wait()
        sum_b.wait(r)

        def part(row):
            rows = pl.ds(pl.multiple_of(own_at(r) + row, 128), 128)
            here = pl.ds(row, 128)
            residual = xone[r, here, :] * gain_one + bias_one + sum_b.total(r, here)
            normal, scale = norm_of(residual)
            stage[r, here, :] = (normal * gain_two + bias_two).astype(BF16)
            grad = ograd[r, here, :].astype(F32)
            value = norm_back(grad * gain_two, normal, scale)
            gtwo[r, here, :] = value
            low_two[rows, :] = value.astype(BF16)
            nsum[16:24, :] += fold(grad * normal)
            nsum[24:32, :] += fold(grad)

        steps(HALF, 128, part)
        pass_on(low_two, 1, p.own(r), r).start()
        mixed_here(r).start()
        mixed_pair(p.own(r), r).start()
        sum_b.close(r)
        pass_on(low_two, 1, p.other(r), r).wait_recv()
        sum_c.give(r, back(other_at(r)))
        sum_c.keep(r, back(own_at(r)))
        return carry

    lax.fori_loop(0, chunks, stage_c, 0)
    if ring:
        scatter_sems = (sxs, sxr, szs, szr)
        scatter_f = Scatter(
            p, share, grads, FFN, xsend, fxrecv, zsend, fzrecv, [s.at[0] for s in scatter_sems]
        )
        scatter_a = Scatter(
            p, share, grads, ATT, xsend, axrecv, zsend, azrecv, [s.at[1] for s in scatter_sems]
        )
    block = 4 * share if ring else D // 2

    def weight_blocks(work, scatter):
        def run(i, carry):
            place = (p.z // 2 + 1 + i) % (ring // 2) if ring else i
            work(pl.ds(pl.multiple_of(place * block, block), block))
            if ring:
                far = 1 - p.z % 2
                for line in (far, 1 - far):
                    scatter.start((2 * place + line + ring - p.z) % ring)
            return carry

        lax.fori_loop(0, D // block, run, 0)

    def ffn_weights(rows):
        grads[rows, :D] = grad_of(shared, rows, slope)
        grads[rows, D:] = grad_of(low_two, rows, active)

    def grad_of(left, rows, right):
        return dot_tn(left[:, rows], right[...])

    weight_blocks(ffn_weights, scatter_f if ring else None)

    def settle(r, carry):
        pass_on(shared, 0, p.own(r), r).wait_send()
        pass_on(low_two, 1, p.own(r), r).wait_send()
        return carry

    lax.fori_loop(0, chunks, settle, 0)
    pl.semaphore_signal(free, inc=1, device_id=p.pair, device_id_type=pl.DeviceIdType.MESH)
    if not ring:
        pltpu.sync_copy(grads, outf)
    low_one, gtext, gbox = shared, active, slope.at[:, :QK]
    gctx, gscore = slope.at[:SEQ, QK:], low_two.at[:SEQ, :SEQ]
    score_scale = HEAD_DIM**-0.5

    def attend_back(r):
        k_rows = pl.ds(pl.multiple_of(r * SEQ, SEQ), SEQ)
        for side in range(2):
            rows = pl.ds(pl.multiple_of(r * SEQ + side * HALF, HALF), HALF)
            gctx[side * HALF : (side + 1) * HALF, :] = dot(low_one[rows, :], wop[...]).astype(BF16)
        low = lower_half((SEQ, 128))
        for h in range(HEADS):
            tile = slice(h * 128, (h + 1) * 128)
            dprob[...] = dot_nt(gctx[:, tile], vk[k_rows, tile])

            def soften(row):
                rows = pl.ds(row, 256)
                grad = dprob[rows, :]
                prob = probs[r, h, rows, :].astype(F32)
                weighted = jnp.sum(prob * grad, axis=-1, keepdims=True)
                gscore[rows, :] = (prob * (grad - weighted)).astype(BF16)

            steps(SEQ, 256, soften)
            left = dot(gscore[...], rk[k_rows, tile]) * score_scale
            right = dot_tn(gscore[...], lq[k_rows, tile]) * score_scale
            value = dot_tn(probs[r, h], gctx[:, tile])
            gtext[k_rows, tile] = jnp.where(
                low, left + pltpu.roll(left, HEAD_DIM, 1), right + pltpu.roll(right, HEAD_DIM, 1)
            ).astype(BF16)
            gbox[k_rows, tile] = jnp.where(low, right, left).astype(BF16)
            gtext[k_rows, QK + h * 128 : QK + (h + 1) * 128] = value.astype(BF16)

    def partial_of(rows):
        return dot_nt(gtext[rows, :], wtx[...])

    pl.semaphore_wait(free, 1)

    def stage_d(r, carry):
        sum_c.wait(r)

        def part(row):
            rows = pl.ds(pl.multiple_of(own_at(r) + row, 128), 128)
            here = pl.ds(row, 128)
            grad = gtwo[r, here, :] + sum_c.total(r, here)
            normal = xone[r, here, :]
            value = norm_back(grad * gain_one, normal, rone[r, here, 0:1])
            gtwo[r, here, :] = value
            low_one[rows, :] = value.astype(BF16)
            nsum[0:8, :] += fold(grad * normal)
            nsum[8:16, :] += fold(grad)

        steps(HALF, 128, part)
        pass_on(low_one, 2, p.own(r), r).start()
        sum_c.close(r)
        pass_on(low_one, 2, p.other(r), r).wait_recv()
        attend_back(r)
        sum_d.give(r, partial_of(p.other(r)))
        sum_d.keep(r, partial_of(p.own(r)))
        if spread:
            scatter_f.middle(r + 1)
        return carry

    lax.fori_loop(0, chunks, stage_d, 0)
    if ring:
        if not spread:
            for k in range(1, ring):
                scatter_f.middle(k)
        scatter_f.own(outf)
        scatter_f.sent()

    def attention_weights(rows):
        text = grad_of(hidden, rows, gtext)
        grads[rows, :QK] = text[:, :QK]
        grads[rows, QK : 2 * QK] = text[:, QK:] + grad_of(low_one, rows, ctx)
        grads[rows, 2 * QK : ATT] = grad_of(emb, rows, gbox)

    weight_blocks(attention_weights, scatter_a if ring else None)
    for row in range(4):
        nsum[row : row + 1, :] = jnp.sum(nsum[row * 8 : row * 8 + 8, :], axis=0, keepdims=True)
    if ring:
        norm_pair = remote(nsum.at[0:8], nrecv.at[0], ns.at[0], nr.at[0], p.pair)
        norm_pair.start()
        scatter_a.middle(1)
        norm_pair.wait_recv()
        nsum[8:16, :] = nsum[0:8, :] + nrecv[0]
        norm_x = remote(nsum.at[8:16], nrecv.at[1], ns.at[1], nr.at[1], p.xdev)
        norm_x.start()
        for k in range(2, ring):
            scatter_a.middle(k)
        scatter_a.own(outa)
        norm_x.wait_recv()
        nsum[16:24, :] = nsum[8:16, :] + nrecv[1]
        norm_z = [
            remote(nsum.at[16:24], nrecv.at[1 + k], ns.at[1 + k], nr.at[1 + k], p.zdev(k))
            for k in range(1, ring)
        ]
        for copy in norm_z:
            copy.start()
    else:
        pltpu.sync_copy(grads.at[:, :ATT], outa)
        nout[...] = nsum[0:8, :]

    def igrad_here(r):
        return pltpu.make_async_copy(gtwo.at[r], igrad.at[p.own(r), :], out_l.at[1, r])

    def igrad_pair(rows, r):
        return remote(gtwo.at[r], igrad.at[rows, :], out_s.at[1, r], out_r.at[1, r], p.pair)

    def stage_e(r, carry):
        sum_d.wait(r)
        gtwo[r] = gtwo[r] + sum_d.total(r, slice(None))
        igrad_here(r).start()
        igrad_pair(p.own(r), r).start()
        sum_d.close(r)
        pass_on(low_one, 2, p.own(r), r).wait_send()
        mixed_here(r).wait()
        mixed_pair(p.own(r), r).wait_send()
        mixed_pair(p.other(r), r).wait_recv()
        return carry

    lax.fori_loop(0, chunks, stage_e, 0)
    if ring:
        scatter_f.finish(outf)
        scatter_a.finish(outa)
        scatter_a.sent()
        summed = nsum[16:24, :]
        for k in range(1, ring):
            norm_z[k - 1].wait_recv()
            summed = summed + nrecv[1 + k]
        nout[...] = summed
        for copy in [norm_pair, norm_x] + norm_z:
            copy.wait_send()

    def end(r, carry):
        igrad_here(r).wait()
        igrad_pair(p.own(r), r).wait_send()
        igrad_pair(p.other(r), r).wait_recv()
        return carry

    lax.fori_loop(0, chunks, end, 0)


def adam_step(weight, gradient, moment, second, rate, decay):
    moment_new = beta_first * moment + (1.0 - beta_first) * gradient
    second_new = beta_second * second + (1.0 - beta_second) * gradient * gradient
    moment_hat = moment_new / (1.0 - beta_first**STEP)
    second_hat = second_new / (1.0 - beta_second**STEP)
    weight_new = weight - rate * (
        moment_hat / (jnp.sqrt(second_hat) + epsilon_adam) + decay * weight
    )
    return (weight_new, moment_new, second_new)


def vmem():
    return pl.BlockSpec(memory_space=pltpu.VMEM)


def dma(*shape):
    return pltpu.SemaphoreType.DMA(shape)


def interleave(first, second):
    rows = first.shape[0]
    pair = [part.reshape(rows, HEADS, 1, HEAD_DIM) for part in (first, second)]
    return jnp.concatenate(pair, axis=2).reshape(rows, QK)


def split_pair(both):
    rows = both.shape[0]
    pair = both.reshape(rows, HEADS, 2, HEAD_DIM)
    return pair[:, :, 0].reshape(rows, QK // 2), pair[:, :, 1].reshape(rows, QK // 2)


def box_lanes():
    quarter = D // 4
    ladder = jnp.arange(quarter).astype(F32)
    frequency = jnp.exp(ladder * (-math.log(10000.0) / quarter))
    zero, one = jnp.zeros((quarter,), F32), jnp.ones((quarter,), F32)
    return jnp.stack(
        [
            jnp.concatenate([frequency] * 4),
            jnp.concatenate([zero, zero, one, one]),
            jnp.concatenate([zero, one, zero, one]),
        ]
        + [jnp.zeros((D,), F32)] * 5
    )


def per_device(
    devices,
    hidden_in,
    page_ids,
    pad_mask,
    boxes,
    out_grad,
    attn_in,
    attn_in_moment,
    attn_in_second,
    attn_out,
    attn_out_moment,
    attn_out_second,
    ffn_in,
    ffn_in_moment,
    ffn_in_second,
    ffn_out,
    ffn_out_moment,
    ffn_out_second,
    norm_weight,
    norm_moment,
    norm_second,
):
    tokens = hidden_in.shape[0]
    chunks = tokens // SEQ
    share = attn_in.shape[1]
    ring = devices // 2 if devices % 4 == 0 and share % 32 == 0 else 0
    low_in = attn_in.astype(BF16)
    packa = jnp.concatenate(
        [
            interleave(low_in[0], low_in[1]),
            interleave(attn_out.T.astype(BF16), low_in[2]),
            interleave(low_in[4], low_in[3]),
        ],
        axis=1,
    )
    packf = jnp.concatenate([ffn_in.astype(BF16), ffn_out.T.astype(BF16)], axis=1)
    pnorm = jnp.pad(norm_weight, ((0, 4), (0, -share % 128)))
    if not ring:
        packa = lax.all_gather(packa, "dp", axis=0, tiled=True)
        packf = lax.all_gather(packf, "dp", axis=0, tiled=True)
        pnorm = lax.all_gather(norm_weight, "dp", axis=1, tiled=True)
        pnorm = jnp.pad(pnorm, ((0, 4), (0, 0)))
    pages = page_ids.astype(F32)
    cols = jnp.stack([boxes[:, 0].astype(F32), boxes[:, 1].astype(F32), pages], axis=1)
    keyrow = jnp.where(pad_mask == 0, pages, -1.0).reshape(chunks, 1, SEQ)
    count = max(ring, 1)
    any_space = pl.BlockSpec(memory_space=pl.ANY)
    inner = share if ring else 16
    tile = pltpu.VMEM((tokens, D), BF16)
    wide = pltpu.VMEM((tokens, QK), BF16)
    own = pltpu.VMEM((chunks, HALF, D), F32)
    own_low = pltpu.VMEM((chunks, HALF, D), BF16)
    att_share = pltpu.VMEM((count, inner, ATT), BF16)
    ffn_share = pltpu.VMEM((count, inner, FFN), BF16)
    mixed, input_grad, reda, redf, nred = pl.pallas_call(
        partial(layer_kernel, ring, chunks),
        out_shape=(
            jax.ShapeDtypeStruct((tokens, D), BF16),
            jax.ShapeDtypeStruct((tokens, D), F32),
            jax.ShapeDtypeStruct((share if ring else D, ATT), F32),
            jax.ShapeDtypeStruct((share if ring else D, FFN), F32),
            jax.ShapeDtypeStruct((8, D), F32),
        ),
        in_specs=[vmem()] * 7 + [any_space],
        out_specs=(any_space,) * 2 + (vmem() if ring else any_space,) * 2 + (vmem(),),
        scratch_shapes=[
            pltpu.VMEM((D, ATT), BF16),
            pltpu.VMEM((D, FFN), BF16),
            pltpu.VMEM((2 * count,) + pnorm.shape, F32),
            pltpu.VMEM((8, D), F32),
            pltpu.VMEM((D, D), BF16),
            pltpu.VMEM((D, QK), BF16),
            wide,
            wide,
            wide,
            pltpu.VMEM((chunks, HEADS, SEQ, SEQ), BF16),
            wide,
            tile,
            pltpu.VMEM((SEQ, D), F32),
            own_low,
            own,
            pltpu.VMEM((chunks, HALF, 128), F32),
            own,
            tile,
            tile,
            tile,
            tile,
            own_low,
            pltpu.VMEM((D, FFN), F32),
            pltpu.VMEM((32, D), F32),
            pltpu.VMEM((count + 1, 8, D), F32),
            ffn_share,
            ffn_share,
            ffn_share,
            ffn_share,
            att_share,
            att_share,
            own_low,
            own_low,
            own_low,
            pltpu.VMEM((2, chunks, HALF, D), BF16),
            pltpu.SemaphoreType.REGULAR,
        ]
        + [dma(3, count)] * 4
        + [dma(2, chunks)] * 4
        + [dma(3, chunks)] * 2
        + [dma(2, chunks)] * 3
        + [dma(chunks)]
        + [dma(count + 1)] * 2
        + [dma(2, count)] * 4,
        compiler_params=pltpu.CompilerParams(
            collective_id=0, has_side_effects=True, vmem_limit_bytes=VMEM_LIMIT
        ),
    )(hidden_in, cols, keyrow, box_lanes(), packa, packf, pnorm, out_grad)
    redup, reddown = redf[:, :D], redf[:, D:]
    position = lax.axis_index("dp")
    if not ring:
        reda, redup, reddown = (
            lax.psum_scatter(part, "dp", scatter_dimension=0, tiled=True)
            for part in (reda, redup, reddown)
        )
        nred = lax.psum(nred, ("dp", "mp")) * 0.5
    grad_norm = lax.dynamic_slice_in_dim(nred[:4], position * share, share, 1)
    grad_q, grad_k = split_pair(reda[:, :QK])
    grad_o, grad_v = split_pair(reda[:, QK : 2 * QK])
    grad_kb, grad_qb = split_pair(reda[:, 2 * QK :])
    grad_in = jnp.stack([grad_q, grad_k, grad_v, grad_qb, grad_kb])
    new_in = adam_step(
        attn_in, grad_in, attn_in_moment, attn_in_second, rate_matrix, decay_matrix
    )
    new_out = adam_step(
        attn_out, grad_o.T, attn_out_moment, attn_out_second, rate_matrix, decay_matrix
    )
    new_up = adam_step(ffn_in, redup, ffn_in_moment, ffn_in_second, rate_matrix, decay_matrix)
    new_down = adam_step(
        ffn_out, reddown.T, ffn_out_moment, ffn_out_second, rate_matrix, decay_matrix
    )
    new_norm = adam_step(norm_weight, grad_norm, norm_moment, norm_second, rate_norm, 0.0)
    return (mixed, input_grad) + new_in + new_out + new_up + new_down + new_norm


def solution(mesh):
    rows = P("dp", None)
    into = P(None, "dp", "mp")
    out = P("mp", "dp")
    up = P("dp", "mp")
    norm = P(None, "dp")
    return jax.shard_map(
        partial(per_device, mesh.shape["dp"]),
        mesh=mesh,
        in_specs=(rows, P("dp"), P("dp"), rows, rows)
        + (into,) * 3
        + (out,) * 3
        + (up,) * 3
        + (out,) * 3
        + (norm,) * 3,
        out_specs=(rows, rows) + (into,) * 3 + (out,) * 3 + (up,) * 3 + (out,) * 3 + (norm,) * 3,
        check_vma=False,
    )
```

```python
from functools import partial
import math

import jax
import jax.numpy as jnp
import numpy as np
from jax import lax
from jax.experimental import pallas as pl
from jax.experimental.pallas import tpu as pltpu
from jax.sharding import PartitionSpec as P

D = 768
HEAD_DIM = 64
SEQ = 512
HALF = SEQ // 2
STEP = 10
HEADS = 3
QK = HEADS * 128
ATT = 3 * QK
FFN = 2 * D

epsilon_norm = 1e-12
epsilon_adam = 1e-08
beta_first = 0.9
beta_second = 0.999
rate_matrix = 0.05
rate_norm = 0.2
decay_matrix = 0.01
masked_score = -1e30

F32 = jnp.float32
BF16 = jnp.bfloat16
VMEM_LIMIT = 60 * 1024 * 1024


def dot(a, b):
    return jnp.dot(a, b, preferred_element_type=F32)


def dot_nt(a, b):
    return lax.dot_general(a, b, (((1,), (1,)), ((), ())), preferred_element_type=F32)


def dot_tn(a, b):
    return lax.dot_general(a, b, (((0,), (0,)), ((), ())), preferred_element_type=F32)


def remote(src, dst, send, recv, device):
    return pltpu.make_async_remote_copy(
        src_ref=src,
        dst_ref=dst,
        send_sem=send,
        recv_sem=recv,
        device_id=device,
        device_id_type=pl.DeviceIdType.MESH,
    )


def steps(total, size, body):
    def run(i, carry):
        body(pl.multiple_of(i * size, size))
        return carry

    lax.fori_loop(0, total // size, run, 0)


def lower_half(shape):
    return lax.broadcasted_iota(jnp.int32, shape, len(shape) - 1) % 128 < HEAD_DIM


class Place:
    def __init__(self, ring):
        self.dp = lax.axis_index("dp")
        self.mp = lax.axis_index("mp")
        self.half = self.mp % 2
        self.pair = (self.dp, self.mp + 1 - 2 * self.half)
        self.across = (self.dp, (self.mp + 2) % 4)
        self.ring = ring
        self.z = self.dp // 2
        self.x = self.dp % 2
        self.xdev = (self.dp + 1 - 2 * self.x, self.mp)

    def zdev(self, k):
        return (((self.z + k) % self.ring) * 2 + self.x, self.mp)

    def greet(self):
        peers = [self.pair, self.across]
        if self.ring:
            peers += [self.xdev] + [self.zdev(k) for k in range(1, self.ring)]
        barrier = pltpu.get_barrier_semaphore()
        for peer in peers:
            pl.semaphore_signal(
                barrier, inc=1, device_id=peer, device_id_type=pl.DeviceIdType.MESH
            )
        pl.semaphore_wait(barrier, len(peers))

    def own(self, r):
        return pl.ds(pl.multiple_of(r * SEQ + self.half * HALF, HALF), HALF)

    def other(self, r):
        return pl.ds(pl.multiple_of(r * SEQ + (1 - self.half) * HALF, HALF), HALF)


class Gather:
    def __init__(self, place, kind, at, sems):
        self.p, self.at = place, at
        zs, zr, xs, xr = sems
        self.zs, self.zr, self.xs, self.xr = (
            zs.at[kind],
            zr.at[kind],
            xs.at[kind],
            xr.at[kind],
        )

    def hop(self, line, up):
        p = self.p
        view = self.at(2 * line + p.x)
        peer = (p.dp + 2, p.mp) if up else (p.dp - 2, p.mp)
        return remote(view, view, self.zs.at[int(up), line], self.zr.at[line], peer)

    def side(self, line, x):
        view = self.at(2 * line + x)
        return remote(view, view, self.xs.at[line], self.xr.at[line], self.p.xdev)

    def send(self, line, up):
        p = self.p

        @pl.when(p.z < p.ring - 1 if up else p.z > 0)
        def _():
            self.hop(line, up).start()

    def start(self):
        self.send(self.p.z, True)
        self.send(self.p.z, False)

    def cross(self):
        self.side(self.p.z, self.p.x).start()

    def step(self, s):
        p = self.p

        @pl.when(p.z >= s)
        def _():
            self.hop(p.z - s, True).wait_recv()
            self.send(p.z - s, True)
            self.side(p.z - s, p.x).start()

        @pl.when(p.z + s < p.ring)
        def _():
            self.hop(p.z + s, False).wait_recv()
            self.send(p.z + s, False)
            self.side(p.z + s, p.x).start()

    def finish(self):
        for line in range(self.p.ring):
            self.side(line, 1 - self.p.x).wait_recv()

    def drain(self):
        p = self.p
        for line in range(p.ring):
            self.side(line, p.x).wait_send()

            @pl.when((p.z >= line) & (p.z < p.ring - 1))
            def _():
                self.hop(line, True).wait_send()

            @pl.when((p.z <= line) & (p.z > 0))
            def _():
                self.hop(line, False).wait_send()


class Sum:
    def __init__(self, place, parity, psend, precv, sums, yrecv, sems):
        self.p = place
        self.psend, self.precv = psend, precv
        self.sums, self.yrecv = sums, yrecv.at[parity]
        ps, pr, ys, yr = sems
        self.ps, self.pr, self.ys, self.yr = (
            ps.at[parity],
            pr.at[parity],
            ys.at[parity],
            yr.at[parity],
        )

    def to_pair(self, r):
        return remote(
            self.psend.at[r], self.precv.at[r], self.ps.at[r], self.pr.at[r], self.p.pair
        )

    def over(self, r):
        return remote(
            self.sums.at[r], self.yrecv.at[r], self.ys.at[r], self.yr.at[r], self.p.across
        )

    def give(self, r, value):
        self.psend[r] = value.astype(BF16)
        self.to_pair(r).start()

    def keep(self, r, value):
        self.to_pair(r).wait_recv()
        self.sums[r] = (value + self.precv[r].astype(F32)).astype(BF16)
        self.over(r).start()

    def wait(self, r):
        self.over(r).wait_recv()

    def total(self, r, rows):
        return self.sums[r, rows, :].astype(F32) + self.yrecv[r, rows, :].astype(F32)

    def close(self, r):
        self.to_pair(r).wait_send()
        self.over(r).wait_send()


def rolled(value):
    return pltpu.roll(value.astype(F32), HEAD_DIM, 1)


def embed_rows(coords, lanes, out, row):
    rows = pl.ds(row, 64)
    here = coords[rows, :]
    across, upward = here[:, 0:1], here[:, 1:2]
    frequency, second, shift = lanes[0:1, :], lanes[1:2, :], lanes[2:3, :]
    angle = (across + (upward - across) * second) * frequency
    turns = jnp.round(angle * (2.0 / math.pi))
    rest = ((angle - turns * 1.5703125) - turns * 4.837512969970703125e-4) - turns * (
        7.54978995489188216e-8
    )
    square = rest * rest
    sine = rest + rest * square * (
        -1.6666654611e-1 + square * (8.3321608736e-3 + square * -1.9515295891e-4)
    )
    cosine = (
        1.0
        - 0.5 * square
        + square
        * square
        * (
            4.166664568298827e-2
            + square * (-1.388731625493765e-3 + square * 2.443315711809948e-5)
        )
    )
    quarter = (turns + shift).astype(jnp.int32)
    value = jnp.where((quarter & 1) == 1, cosine, sine)
    out[rows, :] = jnp.where((quarter & 2) == 2, -value, value).astype(BF16)


def norm_of(values):
    center = jnp.mean(values, axis=-1, keepdims=True)
    shifted = values - center
    spread = jnp.mean(shifted * shifted, axis=-1, keepdims=True)
    scale = lax.rsqrt(spread + epsilon_norm)
    return shifted * scale, scale


def norm_back(upstream, normal, scale):
    first = jnp.mean(upstream, axis=-1, keepdims=True)
    second = jnp.mean(upstream * normal, axis=-1, keepdims=True)
    return (upstream - first - normal * second) * scale


def fold(values):
    rows, width = values.shape
    return jnp.sum(values.reshape(rows // 8, 8, width), axis=0)


class Scatter:
    def __init__(self, place, share, src, width, xsend, xrecv, zsend, zrecv, sems):
        self.p, self.share, self.src, self.width = place, share, src, width
        self.xsend, self.xrecv, self.zsend, self.zrecv = xsend, xrecv, zsend, zrecv
        self.xs, self.xr, self.zs, self.zr = sems

    def rows(self, k, x):
        d = ((self.p.z + k) % self.p.ring) * 2 + x
        return pl.ds(pl.multiple_of(d * self.share, self.share), self.share)

    def xcopy(self, k):
        return remote(
            self.xsend.at[k, :, : self.width],
            self.xrecv.at[k],
            self.xs.at[k],
            self.xr.at[k],
            self.p.xdev,
        )

    def zcopy(self, k):
        return remote(
            self.zsend.at[k, :, : self.width],
            self.zrecv.at[k],
            self.zs.at[k],
            self.zr.at[k],
            self.p.zdev(k),
        )

    def start(self, k):
        value = self.src[self.rows(k, 1 - self.p.x), : self.width]
        self.xsend[k, :, : self.width] = value.astype(BF16)
        self.xcopy(k).start()

    def middle(self, k):
        self.xcopy(k).wait_recv()
        value = self.src[self.rows(k, self.p.x), : self.width] + self.xrecv[k].astype(F32)
        self.zsend[k, :, : self.width] = value.astype(BF16)
        self.zcopy(k).start()

    def own(self, out):
        self.xcopy(0).wait_recv()
        out[...] = self.src[self.rows(0, self.p.x), : self.width] + self.xrecv[0].astype(F32)

    def sent(self):
        for k in range(self.p.ring):
            self.xcopy(k).wait_send()
        for k in range(1, self.p.ring):
            self.zcopy(k).wait_send()

    def finish(self, out):
        value = out[...]
        for k in range(1, self.p.ring):
            self.zcopy(k).wait_recv()
            value = value + self.zrecv[k].astype(F32)
        out[...] = value


def layer_kernel(
    ring,
    chunks,
    hidden_hbm,
    boxes,
    pages,
    padding,
    lanes,
    weights,
    out_grad,
    mixed,
    igrad,
    outa,
    outf,
    nout,
    wa,
    wf,
    nbuf,
    norm,
    tags,
    cols,
    hidden,
    wtx,
    wop,
    lq,
    rk,
    vk,
    probs,
    ctx,
    emb,
    big,
    ograd,
    xone,
    rone,
    gtwo,
    shared,
    active,
    slope,
    low_two,
    stage,
    grads,
    nsum,
    nrecv,
    xsend,
    zsend,
    fxrecv,
    fzrecv,
    axrecv,
    azrecv,
    psend,
    precv,
    sums,
    yrecv,
    free,
    gather_zs,
    gather_zr,
    gather_xs,
    gather_xr,
    ps,
    pr,
    ys,
    yr,
    share_s,
    share_r,
    out_s,
    out_r,
    out_l,
    ol,
    ns,
    nr,
    hs,
    sxs,
    sxr,
    szs,
    szr,
):
    p = Place(ring)
    tokens = hidden.shape[0]

    def ograd_copy(r):
        return pltpu.make_async_copy(out_grad.at[p.own(r), :], ograd.at[r], ol.at[r])

    hidden_copy = pltpu.make_async_copy(hidden_hbm, hidden, hs)
    hidden_copy.start()
    for r in range(chunks):
        ograd_copy(r).start()
    sums_sems = (ps, pr, ys, yr)
    sum_a, sum_b, sum_c, sum_d = (
        Sum(p, stage_number % 2, psend, precv, sums, yrecv, sums_sems)
        for stage_number in range(4)
    )
    if ring:
        attn_in, attn_out, ffn_in, ffn_out, norm_in = weights
        share = ffn_in.shape[0]
        gather_sems = (gather_zs, gather_zr, gather_xs, gather_xr)

        def rows_of(ref):
            return lambda d: ref.at[pl.ds(pl.multiple_of(d * share, share), share), :]

        gather_a = Gather(p, 0, rows_of(wa), gather_sems)
        gather_f = Gather(p, 1, rows_of(wf), gather_sems)
        gather_n = Gather(p, 2, lambda d: nbuf.at[d], gather_sems)
        mine = pl.ds(pl.multiple_of(p.dp * share, share), share)
        wa[mine, :] = pack_attention(attn_in, attn_out)
        p.greet()
        gather_a.start()
        gather_a.cross()
        wf[mine, :D] = ffn_in[...].astype(BF16)
        wf[mine, D:] = ffn_out[...].astype(BF16)
        nbuf[p.dp] = jnp.zeros_like(nbuf[0])
        nbuf[p.dp, 0:4, :share] = norm_in[...]
    else:
        p.greet()
        wa[...], wf[...], norm[...] = (part[...] for part in weights)
    key = jnp.where(padding[...] == 0, pages[...], -1)
    tags[...] = jnp.zeros_like(tags)
    tags[0:2, :] = boxes[...].astype(F32)
    for row in range(tokens // 128):
        span = slice(row * 128, row * 128 + 128)
        tags[2:3, span] = pages[row : row + 1, :].astype(F32)
        tags[3:4, span] = key[row : row + 1, :].astype(F32)
    for row in range(0, tokens, SEQ):
        cols[row : row + SEQ, 0:8] = tags[:, row : row + SEQ].T
    parts = max(ring - 1, 1) if tokens % (64 * max(ring - 1, 1)) == 0 else 1
    for part in range(parts):
        base = part * (tokens // parts)
        steps(
            tokens // parts,
            64,
            lambda row: embed_rows(cols, lanes, emb, pl.multiple_of(base + row, 64)),
        )
        if ring and part + 1 < parts:
            gather_a.step(part + 1)
    if ring:
        gather_f.start()
        gather_n.start()
        for s in range(parts, ring):
            gather_a.step(s)
        gather_f.cross()
        gather_n.cross()
        gather_a.finish()
        gather_f.step(1)
        gather_n.step(1)

    def build(row):
        rows = pl.ds(row, 256)
        low = lower_half((256, 128))
        wtx[rows, :QK] = wa[rows, :QK]
        for h in range(HEADS):
            qk_cols = slice(h * 128, (h + 1) * 128)
            ov_cols = slice(QK + h * 128, QK + (h + 1) * 128)
            ov = wa[rows, ov_cols].astype(F32)
            wtx[rows, ov_cols] = jnp.where(low, rolled(wa[rows, qk_cols]), ov).astype(BF16)
            wop[rows, qk_cols] = jnp.where(low, 0.0, rolled(ov)).astype(BF16)

    steps(D, 256, build)
    hidden_copy.wait()

    def project(row):
        rows = pl.ds(row, HALF)
        text = dot(hidden[rows, :], wtx[...])
        box = dot(emb[rows, :], wa[:, 2 * QK :])
        low = lower_half((HALF, QK))
        lq[rows, :] = jnp.where(low, text[:, :QK], box).astype(BF16)
        rk[rows, :] = jnp.where(low, box, text[:, :QK]).astype(BF16)
        vk[rows, :] = text[:, QK:].astype(BF16)

    steps(tokens, HALF, project)
    if ring > 2:
        gather_f.step(2)
        gather_n.step(2)
    scores = big.at[:HALF, :SEQ]
    pre = big.at[:HALF, :]
    dprob = big.at[:, :SEQ]

    def attend(r, side):
        start = pl.multiple_of(side * HALF, HALF)
        q_rows = pl.ds(pl.multiple_of(r * SEQ + start, HALF), HALF)
        k_rows = pl.ds(pl.multiple_of(r * SEQ, SEQ), SEQ)
        low = lower_half((HALF, 128))
        pages = cols[q_rows, 2:3]
        here = lax.broadcasted_iota(jnp.int32, (HALF, SEQ), 0) + start
        there = lax.broadcasted_iota(jnp.int32, (HALF, SEQ), 1)
        allowed = (pages == tags[3:4, k_rows]) | (here == there)
        for h in range(HEADS):
            tile = slice(h * 128, (h + 1) * 128)
            left = lq[q_rows, tile]
            both = jnp.concatenate([left, jnp.where(low, left, jnp.zeros_like(left))], axis=1)
            right = jnp.concatenate([rk[k_rows, tile], vk[k_rows, tile]], axis=1)
            scores[...] = dot_nt(both, right)
            value = jnp.where(allowed, scores[...] * HEAD_DIM**-0.5, masked_score)
            raised = jnp.exp(value - jnp.max(value, axis=-1, keepdims=True))
            value = raised / jnp.sum(raised, axis=-1, keepdims=True)
            probs[r, h, pl.ds(start, HALF), :] = value.astype(BF16)
            found = dot(probs[r, h, pl.ds(start, HALF), :], vk[k_rows, tile])
            ctx[q_rows, tile] = jnp.where(low, pltpu.roll(found, HEAD_DIM, 1), 0.0).astype(BF16)
        return dot_nt(ctx[q_rows, :], wa[:, QK : 2 * QK])

    spread = ring - 1 == chunks

    def stage_a(r, carry):
        sum_a.give(r, attend(r, 1 - p.half))
        sum_a.keep(r, attend(r, p.half))
        if ring > 3:

            @pl.when(r == 0)
            def _():
                gather_f.step(3)
                gather_n.step(3)

        return carry

    lax.fori_loop(0, chunks, stage_a, 0)
    if ring:
        for s in range(4, ring):
            gather_f.step(s)
            gather_n.step(s)
        gather_n.finish()
        norm[...] = jnp.concatenate([nbuf[d, :, :share] for d in range(2 * ring)], axis=1)
        gather_f.finish()
    gain_one, bias_one = norm[0:1, :], norm[1:2, :]
    gain_two, bias_two = norm[2:3, :], norm[3:4, :]

    def pass_on(ref, number, rows, r):
        view = ref.at[rows, :]
        return remote(view, view, share_s.at[number, r], share_r.at[number, r], p.pair)

    def up_down(rows_at):
        rows = pl.ds(rows_at, HALF)
        pre[...] = dot(shared[rows, :], wf[:, :D])

        def gelu(row):
            here = pl.ds(row, 64)
            there = pl.ds(pl.multiple_of(rows_at + row, 64), 64)
            value = pre[here, :]
            below = 0.5 + 0.5 * lax.erf(value * math.sqrt(0.5))
            active[there, :] = (value * below).astype(BF16)
            density = jnp.exp(-0.5 * value * value) * (1.0 / math.sqrt(2.0 * math.pi))
            slope[there, :] = (below + value * density).astype(BF16)

        steps(HALF, 64, gelu)
        return dot_nt(active[rows, :], wf[:, D:])

    def own_at(r):
        return pl.multiple_of(r * SEQ + p.half * HALF, HALF)

    def other_at(r):
        return pl.multiple_of(r * SEQ + (1 - p.half) * HALF, HALF)

    def stage_b(r, carry):
        sum_a.wait(r)

        def part(row):
            rows = pl.ds(pl.multiple_of(own_at(r) + row, 128), 128)
            here = pl.ds(row, 128)
            normal, scale = norm_of(hidden[rows, :].astype(F32) + sum_a.total(r, here))
            xone[r, here, :] = normal
            rone[r, here, :] = jnp.broadcast_to(scale, (128, 128))
            shared[rows, :] = (normal * gain_one + bias_one).astype(BF16)

        steps(HALF, 128, part)
        pass_on(shared, 0, p.own(r), r).start()
        sum_a.close(r)
        pass_on(shared, 0, p.other(r), r).wait_recv()
        sum_b.give(r, up_down(other_at(r)))
        sum_b.keep(r, up_down(own_at(r)))
        return carry

    lax.fori_loop(0, chunks, stage_b, 0)
    nsum[...] = jnp.zeros_like(nsum)

    def mixed_here(r):
        return pltpu.make_async_copy(stage.at[r], mixed.at[p.own(r), :], out_l.at[0, r])

    def mixed_pair(rows, r):
        return remote(stage.at[r], mixed.at[rows, :], out_s.at[0, r], out_r.at[0, r], p.pair)

    def back(rows_at):
        rows = pl.ds(rows_at, HALF)
        pre[...] = dot(low_two[rows, :], wf[:, D:])

        def times(row):
            here = pl.ds(row, 64)
            there = pl.ds(pl.multiple_of(rows_at + row, 64), 64)
            slope[there, :] = (pre[here, :] * slope[there, :].astype(F32)).astype(BF16)

        steps(HALF, 64, times)
        return dot_nt(slope[rows, :], wf[:, :D])

    def stage_c(r, carry):
        ograd_copy(r).wait()
        sum_b.wait(r)

        def part(row):
            rows = pl.ds(pl.multiple_of(own_at(r) + row, 128), 128)
            here = pl.ds(row, 128)
            residual = xone[r, here, :] * gain_one + bias_one + sum_b.total(r, here)
            normal, scale = norm_of(residual)
            stage[r, here, :] = (normal * gain_two + bias_two).astype(BF16)
            grad = ograd[r, here, :].astype(F32)
            value = norm_back(grad * gain_two, normal, scale)
            gtwo[r, here, :] = value
            low_two[rows, :] = value.astype(BF16)
            nsum[16:24, :] += fold(grad * normal)
            nsum[24:32, :] += fold(grad)

        steps(HALF, 128, part)
        pass_on(low_two, 1, p.own(r), r).start()
        mixed_here(r).start()
        mixed_pair(p.own(r), r).start()
        sum_b.close(r)
        pass_on(low_two, 1, p.other(r), r).wait_recv()
        sum_c.give(r, back(other_at(r)))
        sum_c.keep(r, back(own_at(r)))
        return carry

    lax.fori_loop(0, chunks, stage_c, 0)
    if ring:
        scatter_sems = (sxs, sxr, szs, szr)
        scatter_f = Scatter(
            p, share, grads, FFN, xsend, fxrecv, zsend, fzrecv, [s.at[0] for s in scatter_sems]
        )
        scatter_a = Scatter(
            p, share, grads, ATT, xsend, axrecv, zsend, azrecv, [s.at[1] for s in scatter_sems]
        )
    block = 4 * share if ring else D // 2

    def weight_blocks(work, scatter):
        def run(i, carry):
            place = (p.z // 2 + 1 + i) % (ring // 2) if ring else i
            work(pl.ds(pl.multiple_of(place * block, block), block))
            if ring:
                far = 1 - p.z % 2
                for line in (far, 1 - far):
                    scatter.start((2 * place + line + ring - p.z) % ring)
            return carry

        lax.fori_loop(0, D // block, run, 0)

    def ffn_weights(rows):
        grads[rows, :D] = grad_of(shared, rows, slope)
        grads[rows, D:] = grad_of(low_two, rows, active)

    def grad_of(left, rows, right):
        return dot_tn(left[:, rows], right[...])

    weight_blocks(ffn_weights, scatter_f if ring else None)

    def settle(r, carry):
        pass_on(shared, 0, p.own(r), r).wait_send()
        pass_on(low_two, 1, p.own(r), r).wait_send()
        return carry

    lax.fori_loop(0, chunks, settle, 0)
    pl.semaphore_signal(free, inc=1, device_id=p.pair, device_id_type=pl.DeviceIdType.MESH)
    if not ring:
        pltpu.sync_copy(grads, outf)
    low_one, gtext, gbox = shared, active, slope.at[:, :QK]
    gctx, gscore = slope.at[:SEQ, QK:], low_two.at[:SEQ, :SEQ]
    score_scale = HEAD_DIM**-0.5

    def attend_back(r):
        k_rows = pl.ds(pl.multiple_of(r * SEQ, SEQ), SEQ)
        for side in range(2):
            rows = pl.ds(pl.multiple_of(r * SEQ + side * HALF, HALF), HALF)
            gctx[side * HALF : (side + 1) * HALF, :] = dot(low_one[rows, :], wop[...]).astype(BF16)
        low = lower_half((SEQ, 128))
        for h in range(HEADS):
            tile = slice(h * 128, (h + 1) * 128)
            dprob[...] = dot_nt(gctx[:, tile], vk[k_rows, tile])

            def soften(row):
                rows = pl.ds(row, 256)
                grad = dprob[rows, :]
                prob = probs[r, h, rows, :].astype(F32)
                weighted = jnp.sum(prob * grad, axis=-1, keepdims=True)
                gscore[rows, :] = (prob * (grad - weighted)).astype(BF16)

            steps(SEQ, 256, soften)
            left = dot(gscore[...], rk[k_rows, tile]) * score_scale
            right = dot_tn(gscore[...], lq[k_rows, tile]) * score_scale
            value = dot_tn(probs[r, h], gctx[:, tile])
            gtext[k_rows, tile] = jnp.where(
                low, left + pltpu.roll(left, HEAD_DIM, 1), right + pltpu.roll(right, HEAD_DIM, 1)
            ).astype(BF16)
            gbox[k_rows, tile] = jnp.where(low, right, left).astype(BF16)
            gtext[k_rows, QK + h * 128 : QK + (h + 1) * 128] = value.astype(BF16)

    def partial_of(rows):
        return dot_nt(gtext[rows, :], wtx[...])

    pl.semaphore_wait(free, 1)

    def stage_d(r, carry):
        sum_c.wait(r)

        def part(row):
            rows = pl.ds(pl.multiple_of(own_at(r) + row, 128), 128)
            here = pl.ds(row, 128)
            grad = gtwo[r, here, :] + sum_c.total(r, here)
            normal = xone[r, here, :]
            value = norm_back(grad * gain_one, normal, rone[r, here, 0:1])
            gtwo[r, here, :] = value
            low_one[rows, :] = value.astype(BF16)
            nsum[0:8, :] += fold(grad * normal)
            nsum[8:16, :] += fold(grad)

        steps(HALF, 128, part)
        pass_on(low_one, 2, p.own(r), r).start()
        sum_c.close(r)
        pass_on(low_one, 2, p.other(r), r).wait_recv()
        attend_back(r)
        sum_d.give(r, partial_of(p.other(r)))
        sum_d.keep(r, partial_of(p.own(r)))
        if spread:
            scatter_f.middle(r + 1)
        return carry

    lax.fori_loop(0, chunks, stage_d, 0)
    if ring:
        if not spread:
            for k in range(1, ring):
                scatter_f.middle(k)
        scatter_f.own(outf)
        scatter_f.sent()

    def attention_weights(rows):
        text = grad_of(hidden, rows, gtext)
        grads[rows, :QK] = text[:, :QK]
        grads[rows, QK : 2 * QK] = text[:, QK:] + grad_of(low_one, rows, ctx)
        grads[rows, 2 * QK : ATT] = grad_of(emb, rows, gbox)

    weight_blocks(attention_weights, scatter_a if ring else None)
    for row in range(4):
        nsum[row : row + 1, :] = jnp.sum(nsum[row * 8 : row * 8 + 8, :], axis=0, keepdims=True)
    if ring:
        norm_pair = remote(nsum.at[0:8], nrecv.at[0], ns.at[0], nr.at[0], p.pair)
        norm_pair.start()
        scatter_a.middle(1)
        norm_pair.wait_recv()
        nsum[8:16, :] = nsum[0:8, :] + nrecv[0]
        norm_x = remote(nsum.at[8:16], nrecv.at[1], ns.at[1], nr.at[1], p.xdev)
        norm_x.start()
        for k in range(2, ring):
            scatter_a.middle(k)
        scatter_a.own(outa)
        norm_x.wait_recv()
        nsum[16:24, :] = nsum[8:16, :] + nrecv[1]
        norm_z = [
            remote(nsum.at[16:24], nrecv.at[1 + k], ns.at[1 + k], nr.at[1 + k], p.zdev(k))
            for k in range(1, ring)
        ]
        for copy in norm_z:
            copy.start()
    else:
        pltpu.sync_copy(grads.at[:, :ATT], outa)
        nout[...] = nsum[0:8, :]

    def igrad_here(r):
        return pltpu.make_async_copy(gtwo.at[r], igrad.at[p.own(r), :], out_l.at[1, r])

    def igrad_pair(rows, r):
        return remote(gtwo.at[r], igrad.at[rows, :], out_s.at[1, r], out_r.at[1, r], p.pair)

    def stage_e(r, carry):
        sum_d.wait(r)
        gtwo[r] = gtwo[r] + sum_d.total(r, slice(None))
        igrad_here(r).start()
        igrad_pair(p.own(r), r).start()
        sum_d.close(r)
        pass_on(low_one, 2, p.own(r), r).wait_send()
        mixed_here(r).wait()
        mixed_pair(p.own(r), r).wait_send()
        mixed_pair(p.other(r), r).wait_recv()
        return carry

    lax.fori_loop(0, chunks, stage_e, 0)
    if ring:
        for gather in (gather_a, gather_f, gather_n):
            gather.drain()
        scatter_f.finish(outf)
        scatter_a.finish(outa)
        scatter_a.sent()
        summed = nsum[16:24, :]
        for k in range(1, ring):
            norm_z[k - 1].wait_recv()
            summed = summed + nrecv[1 + k]
        for d in range(2 * ring):

            @pl.when(p.dp == d)
            def _():
                nout[:, :share] = summed[:, d * share : (d + 1) * share]

        for copy in [norm_pair, norm_x] + norm_z:
            copy.wait_send()

    def end(r, carry):
        igrad_here(r).wait()
        igrad_pair(p.own(r), r).wait_send()
        igrad_pair(p.other(r), r).wait_recv()
        return carry

    lax.fori_loop(0, chunks, end, 0)


def adam_step(weight, gradient, moment, second, rate, decay):
    moment_new = beta_first * moment + (1.0 - beta_first) * gradient
    second_new = beta_second * second + (1.0 - beta_second) * gradient * gradient
    moment_hat = moment_new / (1.0 - beta_first**STEP)
    second_hat = second_new / (1.0 - beta_second**STEP)
    weight_new = weight - rate * (
        moment_hat / (jnp.sqrt(second_hat) + epsilon_adam) + decay * weight
    )
    return (weight_new, moment_new, second_new)


def vmem():
    return pl.BlockSpec(memory_space=pltpu.VMEM)


def dma(*shape):
    return pltpu.SemaphoreType.DMA(shape)


def heads_of(value):
    return [value[:, h * HEAD_DIM : (h + 1) * HEAD_DIM] for h in range(value.shape[1] // HEAD_DIM)]


def interleave(first, second):
    pairs = zip(heads_of(first), heads_of(second))
    return jnp.concatenate([part for pair in pairs for part in pair], axis=1)


def split_pair(both):
    parts = heads_of(both)
    return jnp.concatenate(parts[::2], axis=1), jnp.concatenate(parts[1::2], axis=1)


def pack_attention(attn_in, attn_out):
    low = [attn_in[i].astype(BF16) for i in range(5)]
    return jnp.concatenate(
        [
            interleave(low[0], low[1]),
            interleave(attn_out[...].T.astype(BF16), low[2]),
            interleave(low[4], low[3]),
        ],
        axis=1,
    )


def finish_kernel(*refs):
    grads, (mixed_in, igrad_in), olds = refs[:3], refs[3:5], refs[5:20]
    (mixed, igrad), news, held, made = refs[20:22], refs[22:37], refs[37:55], refs[55:70]
    passing, (in_sems, out_sems, fetch_sems, copy_sems) = refs[70:72], refs[72:]
    reads = [
        pltpu.make_async_copy(src, dst, in_sems.at[i])
        for i, (src, dst) in enumerate(zip(grads + olds, held))
    ]
    fetches, copies = [], []
    for src, mid, dst in zip((mixed_in, igrad_in), passing, (mixed, igrad)):
        size = src.shape[0] // 4
        for part in range(4):
            rows, i = pl.ds(part * size, size), len(copies)
            fetches.append(
                pltpu.make_async_copy(src.at[rows, :], mid.at[rows, :], fetch_sems.at[i])
            )
            copies.append(
                pltpu.make_async_copy(mid.at[rows, :], dst.at[rows, :], copy_sems.at[i])
            )
    for copy in reads + fetches:
        copy.start()
    writes = [
        pltpu.make_async_copy(src, dst, out_sems.at[i])
        for i, (src, dst) in enumerate(zip(made, news))
    ]
    for fetch, copy in zip(fetches, copies):
        fetch.wait()
        copy.start()
    for copy in reads[:3]:
        copy.wait()
    reda, redf, nred = held[:3]
    held = held[3:]

    def update(number, gradients, rate, decay):
        for copy in reads[3 + 3 * number : 6 + 3 * number]:
            copy.wait()
        for at, gradient in gradients:
            old = [held[3 * number + i][at] for i in range(3)]
            new = adam_step(old[0], gradient, old[1], old[2], rate, decay)
            for i in range(3):
                made[3 * number + i][at] = new[i]
        for copy in writes[3 * number : 3 * number + 3]:
            copy.start()

    grad_q, grad_k = split_pair(reda[:, :QK])
    grad_o, grad_v = split_pair(reda[:, QK : 2 * QK])
    grad_kb, grad_qb = split_pair(reda[:, 2 * QK :])
    update(0, enumerate((grad_q, grad_k, grad_v, grad_qb, grad_kb)), rate_matrix, decay_matrix)
    update(1, [(Ellipsis, grad_o.T)], rate_matrix, decay_matrix)
    update(2, [(Ellipsis, redf[:, :D])], rate_matrix, decay_matrix)
    update(3, [(Ellipsis, redf[:, D:])], rate_matrix, decay_matrix)
    update(4, [(Ellipsis, nred[0:4, : held[12].shape[1]])], rate_norm, 0.0)
    for copy in copies + writes:
        copy.wait()


def box_lanes():
    quarter = D // 4
    place = np.arange(D)
    rows = np.zeros((8, D), np.float32)
    rows[0] = np.exp((place % quarter) * (-math.log(10000.0) / quarter))
    rows[1] = place >= 2 * quarter
    rows[2] = place // quarter % 2
    return jnp.asarray(rows)


def per_device(
    devices,
    hidden_in,
    page_ids,
    pad_mask,
    boxes,
    out_grad,
    attn_in,
    attn_in_moment,
    attn_in_second,
    attn_out,
    attn_out_moment,
    attn_out_second,
    ffn_in,
    ffn_in_moment,
    ffn_in_second,
    ffn_out,
    ffn_out_moment,
    ffn_out_second,
    norm_weight,
    norm_moment,
    norm_second,
):
    tokens = hidden_in.shape[0]
    chunks = tokens // SEQ
    share = attn_in.shape[1]
    ring = devices // 2 if devices % 4 == 0 and share % 32 == 0 else 0
    weights = (attn_in, attn_out, ffn_in, ffn_out.T, norm_weight)
    if not ring:
        packf = jnp.concatenate([ffn_in.astype(BF16), ffn_out.T.astype(BF16)], axis=1)
        pnorm = lax.all_gather(norm_weight, "dp", axis=1, tiled=True)
        weights = (
            lax.all_gather(pack_attention(attn_in, attn_out), "dp", axis=0, tiled=True),
            lax.all_gather(packf, "dp", axis=0, tiled=True),
            jnp.pad(pnorm, ((0, 4), (0, 0))),
        )
    pages, padding = (part.reshape(tokens // 128, 128) for part in (page_ids, pad_mask))
    count = max(ring, 1)
    any_space = pl.BlockSpec(memory_space=pl.ANY)
    inner = share if ring else 16
    tile = pltpu.VMEM((tokens, D), BF16)
    wide = pltpu.VMEM((tokens, QK), BF16)
    own = pltpu.VMEM((chunks, HALF, D), F32)
    own_low = pltpu.VMEM((chunks, HALF, D), BF16)
    att_share = pltpu.VMEM((count, inner, ATT), BF16)
    ffn_share = pltpu.VMEM((count, inner, FFN), BF16)
    mixed, input_grad, reda, redf, nred = pl.pallas_call(
        partial(layer_kernel, ring, chunks),
        out_shape=(
            jax.ShapeDtypeStruct((tokens, D), BF16),
            jax.ShapeDtypeStruct((tokens, D), F32),
            jax.ShapeDtypeStruct((share if ring else D, ATT), F32),
            jax.ShapeDtypeStruct((share if ring else D, FFN), F32),
            jax.ShapeDtypeStruct((8, max(share, 128)) if ring else (8, D), F32),
        ),
        in_specs=[any_space] + [vmem()] * 4 + [(vmem(),) * len(weights), any_space],
        out_specs=(any_space,) * 2 + (vmem() if ring else any_space,) * 2 + (vmem(),),
        scratch_shapes=[
            pltpu.VMEM((D, ATT), BF16),
            pltpu.VMEM((D, FFN), BF16),
            pltpu.VMEM((2 * count, 8, max(share, 128)), F32),
            pltpu.VMEM((8, D), F32),
            pltpu.VMEM((8, tokens), F32),
            pltpu.VMEM((tokens, 128), F32),
            tile,
            pltpu.VMEM((D, D), BF16),
            pltpu.VMEM((D, QK), BF16),
            wide,
            wide,
            wide,
            pltpu.VMEM((chunks, HEADS, SEQ, SEQ), BF16),
            wide,
            tile,
            pltpu.VMEM((SEQ, D), F32),
            own_low,
            own,
            pltpu.VMEM((chunks, HALF, 128), F32),
            own,
            tile,
            tile,
            tile,
            tile,
            own_low,
            pltpu.VMEM((D, FFN), F32),
            pltpu.VMEM((32, D), F32),
            pltpu.VMEM((count + 1, 8, D), F32),
            ffn_share,
            ffn_share,
            ffn_share,
            ffn_share,
            att_share,
            att_share,
            own_low,
            own_low,
            own_low,
            pltpu.VMEM((2, chunks, HALF, D), BF16),
            pltpu.SemaphoreType.REGULAR,
        ]
        + [dma(3, 2, count)]
        + [dma(3, count)] * 3
        + [dma(2, chunks)] * 4
        + [dma(3, chunks)] * 2
        + [dma(2, chunks)] * 3
        + [dma(chunks)]
        + [dma(count + 1)] * 2
        + [pltpu.SemaphoreType.DMA]
        + [dma(2, count)] * 4,
        compiler_params=pltpu.CompilerParams(
            collective_id=0, has_side_effects=True, vmem_limit_bytes=VMEM_LIMIT
        ),
    )(hidden_in, boxes.T, pages, padding, box_lanes(), weights, out_grad)
    if not ring:
        reda, redf = (
            lax.psum_scatter(part, "dp", scatter_dimension=0, tiled=True) for part in (reda, redf)
        )
        nred = lax.psum(nred, ("dp", "mp")) * 0.5
        nred = lax.dynamic_slice_in_dim(nred, lax.axis_index("dp") * share, share, 1)
    old = (
        (attn_in, attn_in_moment, attn_in_second)
        + (attn_out, attn_out_moment, attn_out_second)
        + (ffn_in, ffn_in_moment, ffn_in_second)
        + (ffn_out.T, ffn_out_moment.T, ffn_out_second.T)
        + (norm_weight, norm_moment, norm_second)
    )
    large = (mixed, input_grad)
    summed = (reda, redf, nred)
    new = pl.pallas_call(
        finish_kernel,
        out_shape=tuple(jax.ShapeDtypeStruct(part.shape, part.dtype) for part in large + old),
        in_specs=[any_space] * 20,
        out_specs=(any_space,) * 17,
        scratch_shapes=[pltpu.VMEM(part.shape, F32) for part in summed + old + old]
        + [pltpu.VMEM(part.shape, part.dtype) for part in large]
        + [dma(18), dma(15), dma(8), dma(8)],
        compiler_params=pltpu.CompilerParams(vmem_limit_bytes=VMEM_LIMIT),
    )(*summed, *large, *old)
    return new[:11] + tuple(part.T for part in new[11:14]) + new[14:]


def solution(mesh):
    rows = P("dp", None)
    into = P(None, "dp", "mp")
    out = P("mp", "dp")
    up = P("dp", "mp")
    norm = P(None, "dp")
    return jax.shard_map(
        partial(per_device, mesh.shape["dp"]),
        mesh=mesh,
        in_specs=(rows, P("dp"), P("dp"), rows, rows)
        + (into,) * 3
        + (out,) * 3
        + (up,) * 3
        + (out,) * 3
        + (norm,) * 3,
        out_specs=(rows, rows) + (into,) * 3 + (out,) * 3 + (up,) * 3 + (out,) * 3 + (norm,) * 3,
        check_vma=False,
    )
```

```python
from functools import partial
import math

import jax
import jax.numpy as jnp
import numpy as np
from jax import lax
from jax.experimental import pallas as pl
from jax.experimental.pallas import tpu as pltpu
from jax.sharding import PartitionSpec as P

D = 768
HEAD_DIM = 64
SEQ = 512
HALF = SEQ // 2
STEP = 10
HEADS = 3
QK = HEADS * 128
ATT = 3 * QK
FFN = 2 * D

epsilon_norm = 1e-12
epsilon_adam = 1e-08
beta_first = 0.9
beta_second = 0.999
rate_matrix = 0.05
rate_norm = 0.2
decay_matrix = 0.01
masked_score = -1e30

F32 = jnp.float32
BF16 = jnp.bfloat16
VMEM_LIMIT = 60 * 1024 * 1024


def dot(a, b):
    return jnp.dot(a, b, preferred_element_type=F32)


def dot_nt(a, b):
    return lax.dot_general(a, b, (((1,), (1,)), ((), ())), preferred_element_type=F32)


def dot_tn(a, b):
    return lax.dot_general(a, b, (((0,), (0,)), ((), ())), preferred_element_type=F32)


def remote(src, dst, send, recv, device):
    return pltpu.make_async_remote_copy(
        src_ref=src,
        dst_ref=dst,
        send_sem=send,
        recv_sem=recv,
        device_id=device,
        device_id_type=pl.DeviceIdType.MESH,
    )


def steps(total, size, body):
    def run(i, carry):
        body(pl.multiple_of(i * size, size))
        return carry

    lax.fori_loop(0, total // size, run, 0)


def lower_half(shape):
    return lax.broadcasted_iota(jnp.int32, shape, len(shape) - 1) % 128 < HEAD_DIM


class Place:
    def __init__(self, ring):
        self.dp = lax.axis_index("dp")
        self.mp = lax.axis_index("mp")
        self.half = self.mp % 2
        self.pair = (self.dp, self.mp + 1 - 2 * self.half)
        self.across = (self.dp, (self.mp + 2) % 4)
        self.ring = ring
        self.z = self.dp // 2
        self.x = self.dp % 2
        self.xdev = (self.dp + 1 - 2 * self.x, self.mp)

    def zdev(self, k):
        return (((self.z + k) % self.ring) * 2 + self.x, self.mp)

    def greet(self):
        peers = [self.pair, self.across]
        if self.ring:
            peers += [self.xdev] + [self.zdev(k) for k in range(1, self.ring)]
        barrier = pltpu.get_barrier_semaphore()
        for peer in peers:
            pl.semaphore_signal(
                barrier, inc=1, device_id=peer, device_id_type=pl.DeviceIdType.MESH
            )
        pl.semaphore_wait(barrier, len(peers))

    def own(self, r):
        return pl.ds(pl.multiple_of(r * SEQ + self.half * HALF, HALF), HALF)

    def other(self, r):
        return pl.ds(pl.multiple_of(r * SEQ + (1 - self.half) * HALF, HALF), HALF)


class Gather:
    def __init__(self, place, kind, at, sems):
        self.p, self.at = place, at
        zs, zr, xs, xr = sems
        self.zs, self.zr, self.xs, self.xr = (
            zs.at[kind],
            zr.at[kind],
            xs.at[kind],
            xr.at[kind],
        )

    def hop(self, line, up):
        p = self.p
        view = self.at(2 * line + p.x)
        peer = (p.dp + 2, p.mp) if up else (p.dp - 2, p.mp)
        return remote(view, view, self.zs.at[int(up), line], self.zr.at[line], peer)

    def side(self, line, x):
        view = self.at(2 * line + x)
        return remote(view, view, self.xs.at[line], self.xr.at[line], self.p.xdev)

    def send(self, line, up):
        p = self.p

        @pl.when(p.z < p.ring - 1 if up else p.z > 0)
        def _():
            self.hop(line, up).start()

    def start(self):
        self.send(self.p.z, True)
        self.send(self.p.z, False)

    def cross(self):
        self.side(self.p.z, self.p.x).start()

    def step(self, s):
        p = self.p

        @pl.when(p.z >= s)
        def _():
            self.hop(p.z - s, True).wait_recv()
            self.send(p.z - s, True)
            self.side(p.z - s, p.x).start()

        @pl.when(p.z + s < p.ring)
        def _():
            self.hop(p.z + s, False).wait_recv()
            self.send(p.z + s, False)
            self.side(p.z + s, p.x).start()

    def finish(self):
        for line in range(self.p.ring):
            self.side(line, 1 - self.p.x).wait_recv()

    def drain(self):
        p = self.p
        for line in range(p.ring):
            self.side(line, p.x).wait_send()

            @pl.when((p.z >= line) & (p.z < p.ring - 1))
            def _():
                self.hop(line, True).wait_send()

            @pl.when((p.z <= line) & (p.z > 0))
            def _():
                self.hop(line, False).wait_send()


class Sum:
    def __init__(self, place, parity, psend, precv, sums, yrecv, sems):
        self.p = place
        self.psend, self.precv = psend, precv
        self.sums, self.yrecv = sums, yrecv.at[parity]
        ps, pr, ys, yr = sems
        self.ps, self.pr, self.ys, self.yr = (
            ps.at[parity],
            pr.at[parity],
            ys.at[parity],
            yr.at[parity],
        )

    def to_pair(self, r):
        return remote(
            self.psend.at[r], self.precv.at[r], self.ps.at[r], self.pr.at[r], self.p.pair
        )

    def over(self, r):
        return remote(
            self.sums.at[r], self.yrecv.at[r], self.ys.at[r], self.yr.at[r], self.p.across
        )

    def give(self, r, value):
        self.psend[r] = value.astype(BF16)
        self.to_pair(r).start()

    def hold(self, r, value):
        self.sums[r] = value.astype(BF16)

    def keep(self, r):
        self.to_pair(r).wait_recv()
        self.sums[r] = (self.sums[r].astype(F32) + self.precv[r].astype(F32)).astype(BF16)
        self.over(r).start()

    def keep_last(self, r):
        @pl.when(r > 0)
        def _():
            self.keep(r - 1)

    def wait(self, r):
        self.over(r).wait_recv()

    def total(self, r, rows):
        return self.sums[r, rows, :].astype(F32) + self.yrecv[r, rows, :].astype(F32)

    def close(self, r):
        self.to_pair(r).wait_send()
        self.over(r).wait_send()


def rolled(value):
    return pltpu.roll(value.astype(F32), HEAD_DIM, 1)


def embed_rows(coords, lanes, out, row):
    rows = pl.ds(row, 64)
    here = coords[rows, :]
    across, upward = here[:, 0:1], here[:, 1:2]
    frequency, second, shift = lanes[0:1, :], lanes[1:2, :], lanes[2:3, :]
    angle = (across + (upward - across) * second) * frequency
    turns = jnp.round(angle * (2.0 / math.pi))
    rest = ((angle - turns * 1.5703125) - turns * 4.837512969970703125e-4) - turns * (
        7.54978995489188216e-8
    )
    square = rest * rest
    sine = rest + rest * square * (
        -1.6666654611e-1 + square * (8.3321608736e-3 + square * -1.9515295891e-4)
    )
    cosine = (
        1.0
        - 0.5 * square
        + square
        * square
        * (
            4.166664568298827e-2
            + square * (-1.388731625493765e-3 + square * 2.443315711809948e-5)
        )
    )
    quarter = (turns + shift).astype(jnp.int32)
    value = jnp.where((quarter & 1) == 1, cosine, sine)
    out[rows, :] = jnp.where((quarter & 2) == 2, -value, value).astype(BF16)


def norm_of(values):
    center = jnp.mean(values, axis=-1, keepdims=True)
    shifted = values - center
    spread = jnp.mean(shifted * shifted, axis=-1, keepdims=True)
    scale = lax.rsqrt(spread + epsilon_norm)
    return shifted * scale, scale


def norm_back(upstream, normal, scale):
    first = jnp.mean(upstream, axis=-1, keepdims=True)
    second = jnp.mean(upstream * normal, axis=-1, keepdims=True)
    return (upstream - first - normal * second) * scale


def fold(values):
    rows, width = values.shape
    return jnp.sum(values.reshape(rows // 8, 8, width), axis=0)


class Scatter:
    def __init__(self, place, share, src, cols, xsend, xrecv, zsend, zrecv, sems):
        self.p, self.share, self.src, self.cols = place, share, src, cols
        self.xsend, self.xrecv, self.zsend, self.zrecv = xsend, xrecv, zsend, zrecv
        self.xs, self.xr, self.zs, self.zr = sems

    def rows(self, k, x):
        d = ((self.p.z + k) % self.p.ring) * 2 + x
        return pl.ds(pl.multiple_of(d * self.share, self.share), self.share)

    def xcopy(self, k):
        return remote(
            self.xsend.at[k, :, self.cols],
            self.xrecv.at[k, :, self.cols],
            self.xs.at[k],
            self.xr.at[k],
            self.p.xdev,
        )

    def zcopy(self, k):
        return remote(
            self.zsend.at[k - 1, :, self.cols],
            self.zrecv.at[k - 1, :, self.cols],
            self.zs.at[k],
            self.zr.at[k],
            self.p.zdev(k),
        )

    def start(self, k):
        value = self.src[self.rows(k, 1 - self.p.x), self.cols]
        self.xsend[k, :, self.cols] = value.astype(BF16)
        self.xcopy(k).start()

    def added(self, k):
        self.xcopy(k).wait_recv()
        mine = self.src[self.rows(k, self.p.x), self.cols]
        return mine + self.xrecv[k, :, self.cols].astype(F32)

    def middle(self, k):
        self.zsend[k - 1, :, self.cols] = self.added(k).astype(BF16)
        self.zcopy(k).start()

    def own(self, out):
        out[:, self.cols] = self.added(0)

    def sent(self):
        for k in range(self.p.ring):
            self.xcopy(k).wait_send()
        for k in range(1, self.p.ring):
            self.zcopy(k).wait_send()

    def finish(self, out):
        value = out[:, self.cols]
        for k in range(1, self.p.ring):
            self.zcopy(k).wait_recv()
            value = value + self.zrecv[k - 1, :, self.cols].astype(F32)
        out[:, self.cols] = value


def layer_kernel(
    ring,
    chunks,
    hidden_hbm,
    boxes,
    pages,
    padding,
    lanes,
    weights,
    out_grad,
    mixed,
    igrad,
    outa,
    outf,
    nout,
    wa,
    wf,
    nbuf,
    norm,
    tags,
    cols,
    hidden,
    wtx,
    wop,
    lq,
    rk,
    vk,
    probs,
    ctx,
    emb,
    big,
    ograd,
    xone,
    rone,
    gtwo,
    shared,
    active,
    slope,
    low_two,
    stage,
    grads,
    nsum,
    nrecv,
    xsend,
    zsend,
    fxrecv,
    fzrecv,
    axsend,
    azsend,
    axrecv,
    azrecv,
    psend,
    precv,
    sums,
    yrecv,
    free,
    gather_zs,
    gather_zr,
    gather_xs,
    gather_xr,
    ps,
    pr,
    ys,
    yr,
    share_s,
    share_r,
    out_s,
    out_r,
    out_l,
    ol,
    ns,
    nr,
    hs,
    sxs,
    sxr,
    szs,
    szr,
):
    p = Place(ring)
    tokens = hidden.shape[0]

    def ograd_copy(r):
        return pltpu.make_async_copy(out_grad.at[p.own(r), :], ograd.at[r], ol.at[r])

    hidden_copy = pltpu.make_async_copy(hidden_hbm, hidden, hs)
    hidden_copy.start()
    for r in range(chunks):
        ograd_copy(r).start()
    sums_sems = (ps, pr, ys, yr)
    sum_a, sum_b, sum_c, sum_d = (
        Sum(p, stage_number % 2, psend, precv, sums, yrecv, sums_sems)
        for stage_number in range(4)
    )
    if ring:
        attn_in, attn_out, ffn_in, ffn_out, norm_in = weights
        share = ffn_in.shape[0]
        gather_sems = (gather_zs, gather_zr, gather_xs, gather_xr)

        def rows_of(ref):
            return lambda d: ref.at[pl.ds(pl.multiple_of(d * share, share), share), :]

        gather_a = Gather(p, 0, rows_of(wa), gather_sems)
        gather_f = Gather(p, 1, rows_of(wf), gather_sems)
        gather_n = Gather(p, 2, lambda d: nbuf.at[d], gather_sems)
        mine = pl.ds(pl.multiple_of(p.dp * share, share), share)
        wa[mine, :] = pack_attention(attn_in, attn_out)
        p.greet()
        gather_a.start()
        gather_a.cross()
        wf[mine, :D] = ffn_in[...].astype(BF16)
        wf[mine, D:] = ffn_out[...].astype(BF16)
        nbuf[p.dp] = jnp.zeros_like(nbuf[0])
        nbuf[p.dp, 0:4, :share] = norm_in[...]
    else:
        p.greet()
        wa[...], wf[...], norm[...] = (part[...] for part in weights)
    key = jnp.where(padding[...] == 0, pages[...], -1)
    tags[...] = jnp.zeros_like(tags)
    tags[0:2, :] = boxes[...].astype(F32)
    for row in range(tokens // 128):
        span = slice(row * 128, row * 128 + 128)
        tags[2:3, span] = pages[row : row + 1, :].astype(F32)
        tags[3:4, span] = key[row : row + 1, :].astype(F32)
    for row in range(0, tokens, SEQ):
        cols[row : row + SEQ, 0:8] = tags[:, row : row + SEQ].T
    parts = max(ring - 1, 1) if tokens % (64 * max(ring - 1, 1)) == 0 else 1
    for part in range(parts):
        base = part * (tokens // parts)
        steps(
            tokens // parts,
            64,
            lambda row: embed_rows(cols, lanes, emb, pl.multiple_of(base + row, 64)),
        )
        if ring and part + 1 < parts:
            gather_a.step(part + 1)
    if ring:
        gather_f.start()
        gather_n.start()
        for s in range(parts, ring):
            gather_a.step(s)
        gather_f.cross()
        gather_n.cross()
        gather_a.finish()
        gather_f.step(1)
        gather_n.step(1)

    def build(row):
        rows = pl.ds(row, 256)
        low = lower_half((256, 128))
        wtx[rows, :QK] = wa[rows, :QK]
        for h in range(HEADS):
            qk_cols = slice(h * 128, (h + 1) * 128)
            ov_cols = slice(QK + h * 128, QK + (h + 1) * 128)
            ov = wa[rows, ov_cols].astype(F32)
            wtx[rows, ov_cols] = jnp.where(low, rolled(wa[rows, qk_cols]), ov).astype(BF16)
            wop[rows, qk_cols] = jnp.where(low, 0.0, rolled(ov)).astype(BF16)

    steps(D, 256, build)
    hidden_copy.wait()

    def project(row):
        rows = pl.ds(row, HALF)
        text = dot(hidden[rows, :], wtx[...])
        box = dot(emb[rows, :], wa[:, 2 * QK :])
        low = lower_half((HALF, QK))
        lq[rows, :] = jnp.where(low, text[:, :QK], box).astype(BF16)
        rk[rows, :] = jnp.where(low, box, text[:, :QK]).astype(BF16)
        vk[rows, :] = text[:, QK:].astype(BF16)

    scores = big.at[:HALF, :SEQ]
    pre = big.at[:HALF, :]
    dprob = big.at[:, :SEQ]

    def attend(r, side):
        start = pl.multiple_of(side * HALF, HALF)
        q_rows = pl.ds(pl.multiple_of(r * SEQ + start, HALF), HALF)
        k_rows = pl.ds(pl.multiple_of(r * SEQ, SEQ), SEQ)
        low = lower_half((HALF, 128))
        pages = cols[q_rows, 2:3]
        here = lax.broadcasted_iota(jnp.int32, (HALF, SEQ), 0) + start
        there = lax.broadcasted_iota(jnp.int32, (HALF, SEQ), 1)
        allowed = (pages == tags[3:4, k_rows]) | (here == there)
        for h in range(HEADS):
            tile = slice(h * 128, (h + 1) * 128)
            left = lq[q_rows, tile]
            both = jnp.concatenate([left, jnp.where(low, left, jnp.zeros_like(left))], axis=1)
            right = jnp.concatenate([rk[k_rows, tile], vk[k_rows, tile]], axis=1)
            scores[...] = dot_nt(both, right)
            value = jnp.where(allowed, scores[...] * HEAD_DIM**-0.5, masked_score)
            raised = jnp.exp(value - jnp.max(value, axis=-1, keepdims=True))
            value = raised / jnp.sum(raised, axis=-1, keepdims=True)
            probs[r, h, pl.ds(start, HALF), :] = value.astype(BF16)
            found = dot(probs[r, h, pl.ds(start, HALF), :], vk[k_rows, tile])
            ctx[q_rows, tile] = jnp.where(low, pltpu.roll(found, HEAD_DIM, 1), 0.0).astype(BF16)
        return dot_nt(ctx[q_rows, :], wa[:, QK : 2 * QK])

    def stage_a(r, carry):
        project(pl.multiple_of(r * SEQ, SEQ))
        project(pl.multiple_of(r * SEQ + HALF, HALF))
        sum_a.give(r, attend(r, 1 - p.half))
        sum_a.hold(r, attend(r, p.half))
        sum_a.keep(r)
        if ring > 3:

            @pl.when(r < 2)
            def _():
                gather_f.step(r + 2)
                gather_n.step(r + 2)

        return carry

    lax.fori_loop(0, chunks, stage_a, 0)
    if ring:
        for s in range(4 if ring > 3 and chunks > 1 else 2 + (ring > 3), ring):
            gather_f.step(s)
            gather_n.step(s)
        gather_n.finish()
        norm[...] = jnp.concatenate([nbuf[d, :, :share] for d in range(2 * ring)], axis=1)
        gather_f.finish()
    gain_one, bias_one = norm[0:1, :], norm[1:2, :]
    gain_two, bias_two = norm[2:3, :], norm[3:4, :]

    def pass_on(ref, number, rows, r):
        view = ref.at[rows, :]
        return remote(view, view, share_s.at[number, r], share_r.at[number, r], p.pair)

    def up_down(rows_at):
        rows = pl.ds(rows_at, HALF)
        pre[...] = dot(shared[rows, :], wf[:, :D])

        def gelu(row):
            here = pl.ds(row, 64)
            there = pl.ds(pl.multiple_of(rows_at + row, 64), 64)
            value = pre[here, :]
            below = 0.5 + 0.5 * lax.erf(value * math.sqrt(0.5))
            active[there, :] = (value * below).astype(BF16)
            density = jnp.exp(-0.5 * value * value) * (1.0 / math.sqrt(2.0 * math.pi))
            slope[there, :] = (below + value * density).astype(BF16)

        steps(HALF, 64, gelu)
        return dot_nt(active[rows, :], wf[:, D:])

    def own_at(r):
        return pl.multiple_of(r * SEQ + p.half * HALF, HALF)

    def other_at(r):
        return pl.multiple_of(r * SEQ + (1 - p.half) * HALF, HALF)

    def stage_b(r, carry):
        sum_a.wait(r)

        def part(row):
            rows = pl.ds(pl.multiple_of(own_at(r) + row, 128), 128)
            here = pl.ds(row, 128)
            normal, scale = norm_of(hidden[rows, :].astype(F32) + sum_a.total(r, here))
            xone[r, here, :] = normal
            rone[r, here, :] = jnp.broadcast_to(scale, (128, 128))
            shared[rows, :] = (normal * gain_one + bias_one).astype(BF16)

        steps(HALF, 128, part)
        pass_on(shared, 0, p.own(r), r).start()
        sum_a.close(r)
        sum_b.keep_last(r)
        sum_b.hold(r, up_down(own_at(r)))
        pass_on(shared, 0, p.other(r), r).wait_recv()
        sum_b.give(r, up_down(other_at(r)))
        return carry

    lax.fori_loop(0, chunks, stage_b, 0)
    sum_b.keep(chunks - 1)
    nsum[...] = jnp.zeros_like(nsum)

    def mixed_here(r):
        return pltpu.make_async_copy(stage.at[r], mixed.at[p.own(r), :], out_l.at[0, r])

    def mixed_pair(rows, r):
        return remote(stage.at[r], mixed.at[rows, :], out_s.at[0, r], out_r.at[0, r], p.pair)

    def back(rows_at):
        rows = pl.ds(rows_at, HALF)
        pre[...] = dot(low_two[rows, :], wf[:, D:])

        def times(row):
            here = pl.ds(row, 64)
            there = pl.ds(pl.multiple_of(rows_at + row, 64), 64)
            slope[there, :] = (pre[here, :] * slope[there, :].astype(F32)).astype(BF16)

        steps(HALF, 64, times)
        return dot_nt(slope[rows, :], wf[:, :D])

    if ring:
        scatter_sems = (sxs, sxr, szs, szr)
        scatter_up, scatter_down, scatter_a = (
            Scatter(p, share, src, cols_of, *held, [part.at[number] for part in scatter_sems])
            for number, (src, cols_of, held) in enumerate(
                (
                    (grads, slice(0, D), (xsend, fxrecv, zsend, fzrecv)),
                    (grads, slice(D, FFN), (xsend, fxrecv, zsend, fzrecv)),
                    (grads, slice(0, ATT), (axsend, axrecv, azsend, azrecv)),
                )
            )
        )
    else:
        scatter_up = scatter_down = scatter_a = None
    block = 4 * share if ring else D // 2

    def weight_blocks(work, scatter):
        def run(i, carry):
            place = (p.z // 2 + 1 + i) % (ring // 2) if ring else i
            work(pl.ds(pl.multiple_of(place * block, block), block))
            if ring:
                far = 1 - p.z % 2
                for line in (far, 1 - far):
                    scatter.start((2 * place + line + ring - p.z) % ring)
            return carry

        lax.fori_loop(0, D // block, run, 0)

    def up_weights(rows):
        grads[rows, :D] = grad_of(shared, rows, slope)

    def down_weights(rows):
        grads[rows, D:] = grad_of(low_two, rows, active)

    def grad_of(left, rows, right):
        return dot_tn(left[:, rows], right[...])

    def stage_c(r, carry):
        ograd_copy(r).wait()
        sum_b.wait(r)

        def part(row):
            rows = pl.ds(pl.multiple_of(own_at(r) + row, 128), 128)
            here = pl.ds(row, 128)
            residual = xone[r, here, :] * gain_one + bias_one + sum_b.total(r, here)
            normal, scale = norm_of(residual)
            stage[r, here, :] = (normal * gain_two + bias_two).astype(BF16)
            grad = ograd[r, here, :].astype(F32)
            value = norm_back(grad * gain_two, normal, scale)
            gtwo[r, here, :] = value
            low_two[rows, :] = value.astype(BF16)
            nsum[16:24, :] += fold(grad * normal)
            nsum[24:32, :] += fold(grad)

        steps(HALF, 128, part)
        pass_on(low_two, 1, p.own(r), r).start()
        mixed_here(r).start()
        mixed_pair(p.own(r), r).start()
        sum_b.close(r)
        sum_c.keep_last(r)
        sum_c.hold(r, back(own_at(r)))
        pass_on(low_two, 1, p.other(r), r).wait_recv()

        @pl.when(r == chunks - 1)
        def _():
            weight_blocks(down_weights, scatter_down)

        sum_c.give(r, back(other_at(r)))
        return carry

    lax.fori_loop(0, chunks, stage_c, 0)
    weight_blocks(up_weights, scatter_up)
    sum_c.keep(chunks - 1)

    def settle(r, carry):
        pass_on(shared, 0, p.own(r), r).wait_send()
        pass_on(low_two, 1, p.own(r), r).wait_send()
        return carry

    lax.fori_loop(0, chunks, settle, 0)
    pl.semaphore_signal(free, inc=1, device_id=p.pair, device_id_type=pl.DeviceIdType.MESH)
    if not ring:
        pltpu.sync_copy(grads, outf)
    low_one, gtext, gbox = shared, active, slope.at[:, :QK]
    gctx, gscore = slope.at[:SEQ, QK:], low_two.at[:SEQ, :SEQ]
    score_scale = HEAD_DIM**-0.5

    def context_back(r, side):
        rows = pl.ds(pl.multiple_of(r * SEQ + side * HALF, HALF), HALF)
        there = pl.ds(pl.multiple_of(side * HALF, HALF), HALF)
        gctx[there, :] = dot(low_one[rows, :], wop[...]).astype(BF16)

    def attend_back(r):
        k_rows = pl.ds(pl.multiple_of(r * SEQ, SEQ), SEQ)
        low = lower_half((SEQ, 128))
        for h in range(HEADS):
            tile = slice(h * 128, (h + 1) * 128)
            dprob[...] = dot_nt(gctx[:, tile], vk[k_rows, tile])

            def soften(row):
                rows = pl.ds(row, 256)
                grad = dprob[rows, :]
                prob = probs[r, h, rows, :].astype(F32)
                weighted = jnp.sum(prob * grad, axis=-1, keepdims=True)
                gscore[rows, :] = (prob * (grad - weighted)).astype(BF16)

            steps(SEQ, 256, soften)
            left = dot(gscore[...], rk[k_rows, tile]) * score_scale
            right = dot_tn(gscore[...], lq[k_rows, tile]) * score_scale
            value = dot_tn(probs[r, h], gctx[:, tile])
            gtext[k_rows, tile] = jnp.where(
                low, left + pltpu.roll(left, HEAD_DIM, 1), right + pltpu.roll(right, HEAD_DIM, 1)
            ).astype(BF16)
            gbox[k_rows, tile] = jnp.where(low, right, left).astype(BF16)
            gtext[k_rows, QK + h * 128 : QK + (h + 1) * 128] = value.astype(BF16)

    def partial_of(rows):
        return dot_nt(gtext[rows, :], wtx[...])

    pl.semaphore_wait(free, 1)

    def stage_d(r, carry):
        sum_c.wait(r)

        def part(row):
            rows = pl.ds(pl.multiple_of(own_at(r) + row, 128), 128)
            here = pl.ds(row, 128)
            grad = gtwo[r, here, :] + sum_c.total(r, here)
            normal = xone[r, here, :]
            value = norm_back(grad * gain_one, normal, rone[r, here, 0:1])
            gtwo[r, here, :] = value
            low_one[rows, :] = value.astype(BF16)
            nsum[0:8, :] += fold(grad * normal)
            nsum[8:16, :] += fold(grad)

        steps(HALF, 128, part)
        pass_on(low_one, 2, p.own(r), r).start()
        sum_c.close(r)
        sum_d.keep_last(r)
        context_back(r, p.half)
        pass_on(low_one, 2, p.other(r), r).wait_recv()
        context_back(r, 1 - p.half)
        if ring:

            @pl.when(r == min(1, chunks - 1))
            def _():
                for k in range(1, ring):
                    scatter_down.middle(k)

            @pl.when(r == chunks - 1)
            def _():
                for k in range(1, ring):
                    scatter_up.middle(k)

        attend_back(r)
        sum_d.give(r, partial_of(p.other(r)))
        sum_d.hold(r, partial_of(p.own(r)))
        return carry

    lax.fori_loop(0, chunks, stage_d, 0)

    def attention_weights(rows):
        text = grad_of(hidden, rows, gtext)
        grads[rows, :QK] = text[:, :QK]
        grads[rows, QK : 2 * QK] = text[:, QK:] + grad_of(low_one, rows, ctx)
        grads[rows, 2 * QK : ATT] = grad_of(emb, rows, gbox)

    if ring:
        scatter_down.own(outf)
        scatter_up.own(outf)
    weight_blocks(attention_weights, scatter_a)
    sum_d.keep(chunks - 1)
    for row in range(4):
        nsum[row : row + 1, :] = jnp.sum(nsum[row * 8 : row * 8 + 8, :], axis=0, keepdims=True)
    if ring:
        norm_pair = remote(nsum.at[0:8], nrecv.at[0], ns.at[0], nr.at[0], p.pair)
        norm_pair.start()
        scatter_a.middle(1)
        norm_pair.wait_recv()
        nsum[8:16, :] = nsum[0:8, :] + nrecv[0]
        norm_x = remote(nsum.at[8:16], nrecv.at[1], ns.at[1], nr.at[1], p.xdev)
        norm_x.start()
        for k in range(2, ring):
            scatter_a.middle(k)
        scatter_a.own(outa)
        norm_x.wait_recv()
        nsum[16:24, :] = nsum[8:16, :] + nrecv[1]
        norm_z = [
            remote(nsum.at[16:24], nrecv.at[1 + k], ns.at[1 + k], nr.at[1 + k], p.zdev(k))
            for k in range(1, ring)
        ]
        for copy in norm_z:
            copy.start()
    else:
        pltpu.sync_copy(grads.at[:, :ATT], outa)
        nout[...] = nsum[0:8, :]

    def igrad_here(r):
        return pltpu.make_async_copy(gtwo.at[r], igrad.at[p.own(r), :], out_l.at[1, r])

    def igrad_pair(rows, r):
        return remote(gtwo.at[r], igrad.at[rows, :], out_s.at[1, r], out_r.at[1, r], p.pair)

    def stage_e(r, carry):
        sum_d.wait(r)
        gtwo[r] = gtwo[r] + sum_d.total(r, slice(None))
        igrad_here(r).start()
        igrad_pair(p.own(r), r).start()
        sum_d.close(r)
        pass_on(low_one, 2, p.own(r), r).wait_send()
        mixed_here(r).wait()
        mixed_pair(p.own(r), r).wait_send()
        mixed_pair(p.other(r), r).wait_recv()
        return carry

    lax.fori_loop(0, chunks, stage_e, 0)
    if ring:
        for gather in (gather_a, gather_f, gather_n):
            gather.drain()
        scatter_down.finish(outf)
        scatter_up.finish(outf)
        scatter_a.finish(outa)
        for scatter in (scatter_down, scatter_up, scatter_a):
            scatter.sent()
        summed = nsum[16:24, :]
        for k in range(1, ring):
            norm_z[k - 1].wait_recv()
            summed = summed + nrecv[1 + k]
        for d in range(2 * ring):

            @pl.when(p.dp == d)
            def _():
                nout[:, :share] = summed[:, d * share : (d + 1) * share]

        for copy in [norm_pair, norm_x] + norm_z:
            copy.wait_send()

    def end(r, carry):
        igrad_here(r).wait()
        igrad_pair(p.own(r), r).wait_send()
        igrad_pair(p.other(r), r).wait_recv()
        return carry

    lax.fori_loop(0, chunks, end, 0)


def adam_step(weight, gradient, moment, second, rate, decay):
    moment_new = beta_first * moment + (1.0 - beta_first) * gradient
    second_new = beta_second * second + (1.0 - beta_second) * gradient * gradient
    moment_hat = moment_new / (1.0 - beta_first**STEP)
    second_hat = second_new / (1.0 - beta_second**STEP)
    weight_new = weight - rate * (
        moment_hat / (jnp.sqrt(second_hat) + epsilon_adam) + decay * weight
    )
    return (weight_new, moment_new, second_new)


def vmem():
    return pl.BlockSpec(memory_space=pltpu.VMEM)


def dma(*shape):
    return pltpu.SemaphoreType.DMA(shape)


def heads_of(value):
    return [value[:, h * HEAD_DIM : (h + 1) * HEAD_DIM] for h in range(value.shape[1] // HEAD_DIM)]


def interleave(first, second):
    pairs = zip(heads_of(first), heads_of(second))
    return jnp.concatenate([part for pair in pairs for part in pair], axis=1)


def split_pair(both):
    parts = heads_of(both)
    return jnp.concatenate(parts[::2], axis=1), jnp.concatenate(parts[1::2], axis=1)


def pack_attention(attn_in, attn_out):
    low = [attn_in[i].astype(BF16) for i in range(5)]
    return jnp.concatenate(
        [
            interleave(low[0], low[1]),
            interleave(attn_out[...].T.astype(BF16), low[2]),
            interleave(low[4], low[3]),
        ],
        axis=1,
    )


def finish_kernel(*refs):
    grads, (mixed_in, igrad_in), olds = refs[:3], refs[3:5], refs[5:20]
    (mixed, igrad), news, held, made = refs[20:22], refs[22:37], refs[37:55], refs[55:70]
    passing, (in_sems, out_sems, fetch_sems, copy_sems) = refs[70:72], refs[72:]
    reads = [
        pltpu.make_async_copy(src, dst, in_sems.at[i])
        for i, (src, dst) in enumerate(zip(grads + olds, held))
    ]
    fetches, copies = [], []
    for src, mid, dst in zip((mixed_in, igrad_in), passing, (mixed, igrad)):
        size = src.shape[0] // 4
        for part in range(4):
            rows, i = pl.ds(part * size, size), len(copies)
            fetches.append(
                pltpu.make_async_copy(src.at[rows, :], mid.at[rows, :], fetch_sems.at[i])
            )
            copies.append(
                pltpu.make_async_copy(mid.at[rows, :], dst.at[rows, :], copy_sems.at[i])
            )
    for copy in reads + fetches:
        copy.start()
    writes = [
        pltpu.make_async_copy(src, dst, out_sems.at[i])
        for i, (src, dst) in enumerate(zip(made, news))
    ]
    for fetch, copy in zip(fetches, copies):
        fetch.wait()
        copy.start()
    for copy in reads[:3]:
        copy.wait()
    reda, redf, nred = held[:3]
    held = held[3:]

    def update(number, gradients, rate, decay):
        for copy in reads[3 + 3 * number : 6 + 3 * number]:
            copy.wait()
        for at, gradient in gradients:
            old = [held[3 * number + i][at] for i in range(3)]
            new = adam_step(old[0], gradient, old[1], old[2], rate, decay)
            for i in range(3):
                made[3 * number + i][at] = new[i]
        for copy in writes[3 * number : 3 * number + 3]:
            copy.start()

    grad_q, grad_k = split_pair(reda[:, :QK])
    grad_o, grad_v = split_pair(reda[:, QK : 2 * QK])
    grad_kb, grad_qb = split_pair(reda[:, 2 * QK :])
    update(0, enumerate((grad_q, grad_k, grad_v, grad_qb, grad_kb)), rate_matrix, decay_matrix)
    update(1, [(Ellipsis, grad_o.T)], rate_matrix, decay_matrix)
    update(2, [(Ellipsis, redf[:, :D])], rate_matrix, decay_matrix)
    update(3, [(Ellipsis, redf[:, D:])], rate_matrix, decay_matrix)
    update(4, [(Ellipsis, nred[0:4, : held[12].shape[1]])], rate_norm, 0.0)
    for copy in copies + writes:
        copy.wait()


def box_lanes():
    quarter = D // 4
    place = np.arange(D)
    rows = np.zeros((8, D), np.float32)
    rows[0] = np.exp((place % quarter) * (-math.log(10000.0) / quarter))
    rows[1] = place >= 2 * quarter
    rows[2] = place // quarter % 2
    return jnp.asarray(rows)


def per_device(
    devices,
    hidden_in,
    page_ids,
    pad_mask,
    boxes,
    out_grad,
    attn_in,
    attn_in_moment,
    attn_in_second,
    attn_out,
    attn_out_moment,
    attn_out_second,
    ffn_in,
    ffn_in_moment,
    ffn_in_second,
    ffn_out,
    ffn_out_moment,
    ffn_out_second,
    norm_weight,
    norm_moment,
    norm_second,
):
    tokens = hidden_in.shape[0]
    chunks = tokens // SEQ
    share = attn_in.shape[1]
    ring = devices // 2 if devices % 4 == 0 and share % 32 == 0 else 0
    weights = (attn_in, attn_out, ffn_in, ffn_out.T, norm_weight)
    if not ring:
        packf = jnp.concatenate([ffn_in.astype(BF16), ffn_out.T.astype(BF16)], axis=1)
        pnorm = lax.all_gather(norm_weight, "dp", axis=1, tiled=True)
        weights = (
            lax.all_gather(pack_attention(attn_in, attn_out), "dp", axis=0, tiled=True),
            lax.all_gather(packf, "dp", axis=0, tiled=True),
            jnp.pad(pnorm, ((0, 4), (0, 0))),
        )
    pages, padding = (part.reshape(tokens // 128, 128) for part in (page_ids, pad_mask))
    count = max(ring, 1)
    any_space = pl.BlockSpec(memory_space=pl.ANY)
    inner = share if ring else 16
    tile = pltpu.VMEM((tokens, D), BF16)
    wide = pltpu.VMEM((tokens, QK), BF16)
    own = pltpu.VMEM((chunks, HALF, D), F32)
    own_low = pltpu.VMEM((chunks, HALF, D), BF16)
    att_share = pltpu.VMEM((count, inner, ATT), BF16)
    ffn_share = pltpu.VMEM((count, inner, FFN), BF16)
    att_along = pltpu.VMEM((max(count - 1, 1), inner, ATT), BF16)
    ffn_along = pltpu.VMEM((max(count - 1, 1), inner, FFN), BF16)
    mixed, input_grad, reda, redf, nred = pl.pallas_call(
        partial(layer_kernel, ring, chunks),
        out_shape=(
            jax.ShapeDtypeStruct((tokens, D), BF16),
            jax.ShapeDtypeStruct((tokens, D), F32),
            jax.ShapeDtypeStruct((share if ring else D, ATT), F32),
            jax.ShapeDtypeStruct((share if ring else D, FFN), F32),
            jax.ShapeDtypeStruct((8, max(share, 128)) if ring else (8, D), F32),
        ),
        in_specs=[any_space] + [vmem()] * 4 + [(vmem(),) * len(weights), any_space],
        out_specs=(any_space,) * 2 + (vmem() if ring else any_space,) * 2 + (vmem(),),
        scratch_shapes=[
            pltpu.VMEM((D, ATT), BF16),
            pltpu.VMEM((D, FFN), BF16),
            pltpu.VMEM((2 * count, 8, max(share, 128)), F32),
            pltpu.VMEM((8, D), F32),
            pltpu.VMEM((8, tokens), F32),
            pltpu.VMEM((tokens, 128), F32),
            tile,
            pltpu.VMEM((D, D), BF16),
            pltpu.VMEM((D, QK), BF16),
            wide,
            wide,
            wide,
            pltpu.VMEM((chunks, HEADS, SEQ, SEQ), BF16),
            wide,
            tile,
            pltpu.VMEM((SEQ, D), F32),
            own_low,
            own,
            pltpu.VMEM((chunks, HALF, 128), F32),
            own,
            tile,
            tile,
            tile,
            tile,
            own_low,
            pltpu.VMEM((D, FFN), F32),
            pltpu.VMEM((32, D), F32),
            pltpu.VMEM((count + 1, 8, D), F32),
            ffn_share,
            ffn_along,
            ffn_share,
            ffn_along,
            att_share,
            att_along,
            att_share,
            att_along,
            own_low,
            own_low,
            own_low,
            pltpu.VMEM((2, chunks, HALF, D), BF16),
            pltpu.SemaphoreType.REGULAR,
        ]
        + [dma(3, 2, count)]
        + [dma(3, count)] * 3
        + [dma(2, chunks)] * 4
        + [dma(3, chunks)] * 2
        + [dma(2, chunks)] * 3
        + [dma(chunks)]
        + [dma(count + 1)] * 2
        + [pltpu.SemaphoreType.DMA]
        + [dma(3, count)] * 4,
        compiler_params=pltpu.CompilerParams(
            collective_id=0, has_side_effects=True, vmem_limit_bytes=VMEM_LIMIT
        ),
    )(hidden_in, boxes.T, pages, padding, box_lanes(), weights, out_grad)
    if not ring:
        reda, redf = (
            lax.psum_scatter(part, "dp", scatter_dimension=0, tiled=True) for part in (reda, redf)
        )
        nred = lax.psum(nred, ("dp", "mp")) * 0.5
        nred = lax.dynamic_slice_in_dim(nred, lax.axis_index("dp") * share, share, 1)
    old = (
        (attn_in, attn_in_moment, attn_in_second)
        + (attn_out, attn_out_moment, attn_out_second)
        + (ffn_in, ffn_in_moment, ffn_in_second)
        + (ffn_out.T, ffn_out_moment.T, ffn_out_second.T)
        + (norm_weight, norm_moment, norm_second)
    )
    large = (mixed, input_grad)
    summed = (reda, redf, nred)
    new = pl.pallas_call(
        finish_kernel,
        out_shape=tuple(jax.ShapeDtypeStruct(part.shape, part.dtype) for part in large + old),
        in_specs=[any_space] * 20,
        out_specs=(any_space,) * 17,
        scratch_shapes=[pltpu.VMEM(part.shape, F32) for part in summed + old + old]
        + [pltpu.VMEM(part.shape, part.dtype) for part in large]
        + [dma(18), dma(15), dma(8), dma(8)],
        compiler_params=pltpu.CompilerParams(vmem_limit_bytes=VMEM_LIMIT),
    )(*summed, *large, *old)
    return new[:11] + tuple(part.T for part in new[11:14]) + new[14:]


def solution(mesh):
    rows = P("dp", None)
    into = P(None, "dp", "mp")
    out = P("mp", "dp")
    up = P("dp", "mp")
    norm = P(None, "dp")
    return jax.shard_map(
        partial(per_device, mesh.shape["dp"]),
        mesh=mesh,
        in_specs=(rows, P("dp"), P("dp"), rows, rows)
        + (into,) * 3
        + (out,) * 3
        + (up,) * 3
        + (out,) * 3
        + (norm,) * 3,
        out_specs=(rows, rows) + (into,) * 3 + (out,) * 3 + (up,) * 3 + (out,) * 3 + (norm,) * 3,
        check_vma=False,
    )
```

```python
from functools import partial
import math

import jax
import jax.numpy as jnp
import numpy as np
from jax import lax
from jax.experimental import pallas as pl
from jax.experimental.pallas import tpu as pltpu
from jax.sharding import PartitionSpec as P

D = 768
HEAD_DIM = 64
SEQ = 512
HALF = SEQ // 2
STEP = 10
HEADS = 3
QK = HEADS * 128
ATT = 3 * QK
FFN = 2 * D

epsilon_norm = 1e-12
epsilon_adam = 1e-08
beta_first = 0.9
beta_second = 0.999
rate_matrix = 0.05
rate_norm = 0.2
decay_matrix = 0.01
masked_score = -1e30

F32 = jnp.float32
BF16 = jnp.bfloat16
VMEM_LIMIT = 60 * 1024 * 1024


def dot(a, b):
    return jnp.dot(a, b, preferred_element_type=F32)


def dot_nt(a, b):
    return lax.dot_general(a, b, (((1,), (1,)), ((), ())), preferred_element_type=F32)


def dot_tn(a, b):
    return lax.dot_general(a, b, (((0,), (0,)), ((), ())), preferred_element_type=F32)


def remote(src, dst, send, recv, device):
    return pltpu.make_async_remote_copy(
        src_ref=src,
        dst_ref=dst,
        send_sem=send,
        recv_sem=recv,
        device_id=device,
        device_id_type=pl.DeviceIdType.MESH,
    )


def steps(total, size, body):
    def run(i, carry):
        body(pl.multiple_of(i * size, size))
        return carry

    lax.fori_loop(0, total // size, run, 0)


def lower_half(shape):
    return lax.broadcasted_iota(jnp.int32, shape, len(shape) - 1) % 128 < HEAD_DIM


class Place:
    def __init__(self, ring):
        self.dp = lax.axis_index("dp")
        self.mp = lax.axis_index("mp")
        self.half = self.mp % 2
        self.pair = (self.dp, self.mp + 1 - 2 * self.half)
        self.across = (self.dp, (self.mp + 2) % 4)
        self.diagonal = (self.dp, (self.mp + 2) % 4 + 1 - 2 * self.half)
        self.ring = ring
        self.z = self.dp // 2
        self.x = self.dp % 2
        self.xdev = (self.dp + 1 - 2 * self.x, self.mp)

    def zdev(self, k):
        return (((self.z + k) % self.ring) * 2 + self.x, self.mp)

    def greet(self):
        peers = [self.pair, self.across, self.diagonal]
        if self.ring:
            peers += [self.xdev] + [self.zdev(k) for k in range(1, self.ring)]
        barrier = pltpu.get_barrier_semaphore()
        for peer in peers:
            pl.semaphore_signal(
                barrier, inc=1, device_id=peer, device_id_type=pl.DeviceIdType.MESH
            )
        pl.semaphore_wait(barrier, len(peers))

    def own(self, r):
        return pl.ds(pl.multiple_of(r * SEQ + self.half * HALF, HALF), HALF)

    def other(self, r):
        return pl.ds(pl.multiple_of(r * SEQ + (1 - self.half) * HALF, HALF), HALF)


class Gather:
    def __init__(self, place, kind, at, sems):
        self.p, self.at = place, at
        zs, zr, xs, xr = sems
        self.zs, self.zr, self.xs, self.xr = (
            zs.at[kind],
            zr.at[kind],
            xs.at[kind],
            xr.at[kind],
        )

    def hop(self, line, up):
        p = self.p
        view = self.at(2 * line + p.x)
        peer = (p.dp + 2, p.mp) if up else (p.dp - 2, p.mp)
        return remote(view, view, self.zs.at[int(up), line], self.zr.at[line], peer)

    def side(self, line, x):
        view = self.at(2 * line + x)
        return remote(view, view, self.xs.at[line], self.xr.at[line], self.p.xdev)

    def send(self, line, up):
        p = self.p

        @pl.when(p.z < p.ring - 1 if up else p.z > 0)
        def _():
            self.hop(line, up).start()

    def start(self):
        self.send(self.p.z, True)
        self.send(self.p.z, False)

    def cross(self):
        self.side(self.p.z, self.p.x).start()

    def step(self, s):
        p = self.p

        @pl.when(p.z >= s)
        def _():
            self.hop(p.z - s, True).wait_recv()
            self.send(p.z - s, True)
            self.side(p.z - s, p.x).start()

        @pl.when(p.z + s < p.ring)
        def _():
            self.hop(p.z + s, False).wait_recv()
            self.send(p.z + s, False)
            self.side(p.z + s, p.x).start()

    def finish(self):
        for line in range(self.p.ring):
            self.side(line, 1 - self.p.x).wait_recv()

    def drain(self):
        p = self.p
        for line in range(p.ring):
            self.side(line, p.x).wait_send()

            @pl.when((p.z >= line) & (p.z < p.ring - 1))
            def _():
                self.hop(line, True).wait_send()

            @pl.when((p.z <= line) & (p.z > 0))
            def _():
                self.hop(line, False).wait_send()


class Sum:
    def __init__(self, place, parity, psend, precv, sums, yrecv, sems):
        self.p = place
        self.psend, self.precv = psend, precv
        self.sums, self.yrecv = sums, yrecv.at[parity]
        ps, pr, ys, yr = sems
        self.ps, self.pr, self.ys, self.yr = (
            ps.at[parity],
            pr.at[parity],
            ys.at[parity],
            yr.at[parity],
        )

    def to_pair(self, r):
        return remote(
            self.psend.at[r], self.precv.at[r], self.ps.at[r], self.pr.at[r], self.p.pair
        )

    def over(self, r):
        return remote(
            self.sums.at[r], self.yrecv.at[r], self.ys.at[r], self.yr.at[r], self.p.across
        )

    def give(self, r, value):
        self.psend[r] = value.astype(BF16)
        self.to_pair(r).start()

    def hold(self, r, value):
        self.sums[r] = value.astype(BF16)

    def keep(self, r):
        self.to_pair(r).wait_recv()
        self.sums[r] = (self.sums[r].astype(F32) + self.precv[r].astype(F32)).astype(BF16)
        self.over(r).start()

    def keep_last(self, r):
        @pl.when(r > 0)
        def _():
            self.keep(r - 1)

    def wait(self, r):
        self.over(r).wait_recv()

    def total(self, r, rows):
        return self.sums[r, rows, :].astype(F32) + self.yrecv[r, rows, :].astype(F32)

    def close(self, r):
        self.to_pair(r).wait_send()
        self.over(r).wait_send()


def rolled(value):
    return pltpu.roll(value.astype(F32), HEAD_DIM, 1)


def embed_rows(coords, lanes, out, row):
    rows = pl.ds(row, 64)
    here = coords[rows, :]
    across, upward = here[:, 0:1], here[:, 1:2]
    frequency, second, shift = lanes[0:1, :], lanes[1:2, :], lanes[2:3, :]
    angle = (across + (upward - across) * second) * frequency
    turns = jnp.round(angle * (2.0 / math.pi))
    rest = ((angle - turns * 1.5703125) - turns * 4.837512969970703125e-4) - turns * (
        7.54978995489188216e-8
    )
    square = rest * rest
    sine = rest + rest * square * (
        -1.6666654611e-1 + square * (8.3321608736e-3 + square * -1.9515295891e-4)
    )
    cosine = (
        1.0
        - 0.5 * square
        + square
        * square
        * (
            4.166664568298827e-2
            + square * (-1.388731625493765e-3 + square * 2.443315711809948e-5)
        )
    )
    quarter = (turns + shift).astype(jnp.int32)
    value = jnp.where((quarter & 1) == 1, cosine, sine)
    out[rows, :] = jnp.where((quarter & 2) == 2, -value, value).astype(BF16)


def norm_of(values):
    center = jnp.mean(values, axis=-1, keepdims=True)
    shifted = values - center
    spread = jnp.mean(shifted * shifted, axis=-1, keepdims=True)
    scale = lax.rsqrt(spread + epsilon_norm)
    return shifted * scale, scale


def norm_back(upstream, normal, scale):
    first = jnp.mean(upstream, axis=-1, keepdims=True)
    second = jnp.mean(upstream * normal, axis=-1, keepdims=True)
    return (upstream - first - normal * second) * scale


def fold(values):
    rows, width = values.shape
    return jnp.sum(values.reshape(rows // 8, 8, width), axis=0)


class Scatter:
    def __init__(self, place, share, src, cols, xsend, xrecv, zsend, zrecv, sems):
        self.p, self.share, self.src, self.cols = place, share, src, cols
        self.xsend, self.xrecv, self.zsend, self.zrecv = xsend, xrecv, zsend, zrecv
        self.xs, self.xr, self.zs, self.zr = sems

    def rows(self, k, x):
        d = ((self.p.z + k) % self.p.ring) * 2 + x
        return pl.ds(pl.multiple_of(d * self.share, self.share), self.share)

    def xcopy(self, k):
        return remote(
            self.xsend.at[k, :, self.cols],
            self.xrecv.at[k, :, self.cols],
            self.xs.at[k],
            self.xr.at[k],
            self.p.xdev,
        )

    def zcopy(self, k):
        return remote(
            self.zsend.at[k - 1, :, self.cols],
            self.zrecv.at[k - 1, :, self.cols],
            self.zs.at[k],
            self.zr.at[k],
            self.p.zdev(k),
        )

    def start(self, k):
        value = self.src[self.rows(k, 1 - self.p.x), self.cols]
        self.xsend[k, :, self.cols] = value.astype(BF16)
        self.xcopy(k).start()

    def added(self, k):
        self.xcopy(k).wait_recv()
        mine = self.src[self.rows(k, self.p.x), self.cols]
        return mine + self.xrecv[k, :, self.cols].astype(F32)

    def middle(self, k):
        self.zsend[k - 1, :, self.cols] = self.added(k).astype(BF16)
        self.zcopy(k).start()

    def own(self, out):
        out[:, self.cols] = self.added(0)

    def sent(self):
        for k in range(self.p.ring):
            self.xcopy(k).wait_send()
        for k in range(1, self.p.ring):
            self.zcopy(k).wait_send()

    def finish(self, out):
        value = out[:, self.cols]
        for k in range(1, self.p.ring):
            self.zcopy(k).wait_recv()
            value = value + self.zrecv[k - 1, :, self.cols].astype(F32)
        out[:, self.cols] = value


def layer_kernel(
    ring,
    chunks,
    hidden_hbm,
    boxes,
    pages,
    padding,
    lanes,
    weights,
    out_grad,
    mixed,
    igrad,
    outa,
    outf,
    nout,
    wa,
    wf,
    nbuf,
    norm,
    tags,
    cols,
    hidden,
    wtx,
    wop,
    wo,
    lq,
    rk,
    vk,
    probs,
    ctx,
    emb,
    big,
    ograd,
    xone,
    rone,
    gtwo,
    shared,
    active,
    slope,
    low_two,
    stage,
    grads,
    nsum,
    nrecv,
    xsend,
    zsend,
    fxrecv,
    fzrecv,
    axsend,
    azsend,
    axrecv,
    azrecv,
    psend,
    precv,
    sums,
    yrecv,
    free,
    gather_zs,
    gather_zr,
    gather_xs,
    gather_xr,
    ps,
    pr,
    ys,
    yr,
    share_s,
    share_r,
    out_s,
    out_r,
    out_l,
    ol,
    ns,
    nr,
    hs,
    ctx_s,
    ctx_r,
    wo_s,
    wo_r,
    sxs,
    sxr,
    szs,
    szr,
):
    p = Place(ring)
    tokens = hidden.shape[0]

    def ograd_copy(r):
        return pltpu.make_async_copy(out_grad.at[p.own(r), :], ograd.at[r], ol.at[r])

    hidden_copy = pltpu.make_async_copy(hidden_hbm, hidden, hs)
    hidden_copy.start()
    for r in range(chunks):
        ograd_copy(r).start()
    sums_sems = (ps, pr, ys, yr)
    sum_b, sum_c, sum_d = (
        Sum(p, number % 2, psend, precv, sums, yrecv, sums_sems) for number in range(3)
    )
    if ring:
        attn_in, attn_out, ffn_in, ffn_out, norm_in = weights
        share = ffn_in.shape[0]
        gather_sems = (gather_zs, gather_zr, gather_xs, gather_xr)

        def rows_of(ref):
            return lambda d: ref.at[pl.ds(pl.multiple_of(d * share, share), share), :]

        gather_a = Gather(p, 0, rows_of(wa), gather_sems)
        gather_f = Gather(p, 1, rows_of(wf), gather_sems)
        gather_n = Gather(p, 2, lambda d: nbuf.at[d], gather_sems)
        mine = pl.ds(pl.multiple_of(p.dp * share, share), share)
        wa[mine, :] = pack_attention(attn_in, attn_out)
        p.greet()
        gather_a.start()
        gather_a.cross()
        wf[mine, :D] = ffn_in[...].astype(BF16)
        wf[mine, D:] = ffn_out[...].astype(BF16)
        nbuf[p.dp] = jnp.zeros_like(nbuf[0])
        nbuf[p.dp, 0:4, :share] = norm_in[...]
    else:
        p.greet()
        wa[...], wf[...], norm[...] = (part[...] for part in weights)
    key = jnp.where(padding[...] == 0, pages[...], -1)
    tags[...] = jnp.zeros_like(tags)
    tags[0:2, :] = boxes[...].astype(F32)
    for row in range(tokens // 128):
        span = slice(row * 128, row * 128 + 128)
        tags[2:3, span] = pages[row : row + 1, :].astype(F32)
        tags[3:4, span] = key[row : row + 1, :].astype(F32)
    for row in range(0, tokens, SEQ):
        cols[row : row + SEQ, 0:8] = tags[:, row : row + SEQ].T
    parts = max(ring - 1, 1) if tokens % (64 * max(ring - 1, 1)) == 0 else 1
    for part in range(parts):
        base = part * (tokens // parts)
        steps(
            tokens // parts,
            64,
            lambda row: embed_rows(cols, lanes, emb, pl.multiple_of(base + row, 64)),
        )
        if ring and part + 1 < parts:
            gather_a.step(part + 1)
    if ring:
        gather_f.start()
        gather_n.start()
        for s in range(parts, ring):
            gather_a.step(s)
        gather_f.cross()
        gather_n.cross()
        gather_a.finish()
        gather_f.step(1)
        gather_n.step(1)

    def build(row):
        rows = pl.ds(row, 256)
        low = lower_half((256, 128))
        for h in range(HEADS):
            qk_cols = slice(h * 128, (h + 1) * 128)
            ov_cols = slice(QK + h * 128, QK + (h + 1) * 128)
            ov = wa[rows, ov_cols].astype(F32)
            wtx[rows, h * 256 : h * 256 + 128] = wa[rows, qk_cols]
            wtx[rows, h * 256 + 128 : h * 256 + 256] = jnp.where(
                low, rolled(wa[rows, qk_cols]), ov
            ).astype(BF16)
            wop[rows, qk_cols] = jnp.where(low, 0.0, rolled(ov)).astype(BF16)
        first, second, third = (
            wa[rows, QK + h * 128 : QK + (h + 1) * 128].astype(F32) for h in range(HEADS)
        )
        wo[row // 256, :, :128] = jnp.where(low, first, rolled(second)).astype(BF16)
        wo[row // 256, :, 128:] = jnp.where(low, third, 0.0).astype(BF16)

    steps(D, 256, build)

    def wo_slot(k):
        return stage.at[0 : D // 256, :, k * 256 : (k + 1) * 256]

    def wo_copy(k):
        if k == 2:
            return remote(wo_slot(1), wo_slot(2), wo_s.at[2], wo_r.at[2], p.pair)
        return remote(wo, wo_slot(k), wo_s.at[k], wo_r.at[k], (p.pair, p.across)[k])

    wo_copy(1).start()
    wo_copy(0).start()
    hidden_copy.wait()

    def project(row):
        rows = pl.ds(row, HALF)
        text = dot(hidden[rows, :], wtx[...])
        box = dot(emb[rows, :], wa[:, 2 * QK :])
        low = lower_half((HALF, 128))
        for h in range(HEADS):
            tile = slice(h * 128, (h + 1) * 128)
            word, extra = text[:, h * 256 : h * 256 + 128], box[:, tile]
            lq[rows, tile] = jnp.where(low, word, extra).astype(BF16)
            rk[rows, tile] = jnp.where(low, extra, word).astype(BF16)
            vk[rows, tile] = text[:, h * 256 + 128 : h * 256 + 256].astype(BF16)

    scores = big.at[:HALF, :SEQ]
    pre, post = big.at[:HALF, :], big.at[HALF:, :]
    dprob = big.at[:, :SEQ]

    def ctx_kept(r, own):
        rows = pl.ds(pl.multiple_of(r * SEQ + HALF, HALF), HALF)
        return active.at[rows, 256:512] if own else active.at[rows, 0:256]

    def ctx_copy(k, r):
        rows = pl.ds(pl.multiple_of(r * SEQ, HALF), HALF)
        peer = (p.pair, p.across, p.diagonal)[k]
        slot = active.at[rows, k * 256 : (k + 1) * 256]
        return remote(ctx_kept(r, k == 1), slot, ctx_s.at[k, r], ctx_r.at[k, r], peer)

    def attend(r, side, kept):
        found = []
        start = pl.multiple_of(side * HALF, HALF)
        q_rows = pl.ds(pl.multiple_of(r * SEQ + start, HALF), HALF)
        k_rows = pl.ds(pl.multiple_of(r * SEQ, SEQ), SEQ)
        low = lower_half((HALF, 128))
        pages = cols[q_rows, 2:3]
        here = lax.broadcasted_iota(jnp.int32, (HALF, SEQ), 0) + start
        there = lax.broadcasted_iota(jnp.int32, (HALF, SEQ), 1)
        allowed = (pages == tags[3:4, k_rows]) | (here == there)
        for h in range(HEADS):
            tile = slice(h * 128, (h + 1) * 128)
            left = lq[q_rows, tile]
            both = jnp.concatenate([left, jnp.where(low, left, jnp.zeros_like(left))], axis=1)
            right = jnp.concatenate([rk[k_rows, tile], vk[k_rows, tile]], axis=1)
            scores[...] = dot_nt(both, right)
            value = jnp.where(allowed, scores[...] * HEAD_DIM**-0.5, masked_score)
            raised = jnp.exp(value - jnp.max(value, axis=-1, keepdims=True))
            value = raised / jnp.sum(raised, axis=-1, keepdims=True)
            probs[r, h, pl.ds(start, HALF), :] = value.astype(BF16)
            found.append(dot(probs[r, h, pl.ds(start, HALF), :], vk[k_rows, tile]))
            turned = pltpu.roll(found[h], HEAD_DIM, 1)
            ctx[q_rows, tile] = jnp.where(low, turned, 0.0).astype(BF16)
            if h == 0:
                even = turned
        kept[:, :128] = jnp.where(low, even, found[1]).astype(BF16)
        kept[:, 128:] = ctx[q_rows, 256:384]

    def stage_a(r, carry):
        project(pl.multiple_of(r * SEQ, SEQ))
        project(pl.multiple_of(r * SEQ + HALF, HALF))
        attend(r, 1 - p.half, ctx_kept(r, False))
        ctx_copy(2, r).start()
        ctx_copy(0, r).start()
        attend(r, p.half, ctx_kept(r, True))
        ctx_copy(1, r).start()

        @pl.when(r == 0)
        def _():
            wo_copy(1).wait_recv()
            wo_copy(2).start()

        if ring > 3:

            @pl.when(r < 2)
            def _():
                gather_f.step(r + 2)
                gather_n.step(r + 2)

        return carry

    lax.fori_loop(0, chunks, stage_a, 0)
    if ring:
        for s in range(4 if ring > 3 and chunks > 1 else 2 + (ring > 3), ring):
            gather_f.step(s)
            gather_n.step(s)
        gather_n.finish()
        norm[...] = jnp.concatenate([nbuf[d, :, :share] for d in range(2 * ring)], axis=1)
        gather_f.finish()
    gain_one, bias_one = norm[0:1, :], norm[1:2, :]
    gain_two, bias_two = norm[2:3, :], norm[3:4, :]

    def pass_on(ref, number, rows, r):
        view = ref.at[rows, :]
        return remote(view, view, share_s.at[number, r], share_r.at[number, r], p.pair)

    def up_down(rows_at):
        rows = pl.ds(rows_at, HALF)
        pre[...] = dot(shared[rows, :], wf[:, :D])

        def gelu(row):
            here = pl.ds(row, 64)
            there = pl.ds(pl.multiple_of(rows_at + row, 64), 64)
            value = pre[here, :]
            below = 0.5 + 0.5 * lax.erf(value * math.sqrt(0.5))
            active[there, :] = (value * below).astype(BF16)
            density = jnp.exp(-0.5 * value * value) * (1.0 / math.sqrt(2.0 * math.pi))
            slope[there, :] = (below + value * density).astype(BF16)

        steps(HALF, 64, gelu)
        return dot_nt(active[rows, :], wf[:, D:])

    def own_at(r):
        return pl.multiple_of(r * SEQ + p.half * HALF, HALF)

    def other_at(r):
        return pl.multiple_of(r * SEQ + (1 - p.half) * HALF, HALF)

    wo_copy(0).wait_recv()
    wo_copy(2).wait_recv()
    for k in range(3):
        wo_copy(k).wait_send()

    def stage_b(r, carry):
        for k in range(3):
            ctx_copy(k, r).wait_recv()
        theirs = active[pl.ds(pl.multiple_of(r * SEQ, HALF), HALF), :]
        mine = ctx_kept(r, True)[...]
        for j in range(D // 256):
            cut = [dot_nt(theirs[:, k * 256 : k * 256 + 256], wo_slot(k)[j]) for k in range(3)]
            pre[:, j * 256 : (j + 1) * 256] = dot_nt(mine, wo[j]) + cut[0]
            post[:, j * 256 : (j + 1) * 256] = cut[1] + cut[2]

        def part(row):
            rows = pl.ds(pl.multiple_of(own_at(r) + row, 128), 128)
            here = pl.ds(row, 128)
            normal, scale = norm_of(hidden[rows, :].astype(F32) + (pre[here, :] + post[here, :]))
            xone[r, here, :] = normal
            rone[r, here, :] = jnp.broadcast_to(scale, (128, 128))
            shared[rows, :] = (normal * gain_one + bias_one).astype(BF16)

        steps(HALF, 128, part)
        pass_on(shared, 0, p.own(r), r).start()
        for k in range(3):
            ctx_copy(k, r).wait_send()
        sum_b.keep_last(r)
        sum_b.hold(r, up_down(own_at(r)))
        pass_on(shared, 0, p.other(r), r).wait_recv()
        sum_b.give(r, up_down(other_at(r)))
        return carry

    lax.fori_loop(0, chunks, stage_b, 0)
    sum_b.keep(chunks - 1)
    nsum[...] = jnp.zeros_like(nsum)

    def mixed_here(r):
        return pltpu.make_async_copy(stage.at[r], mixed.at[p.own(r), :], out_l.at[0, r])

    def mixed_pair(rows, r):
        return remote(stage.at[r], mixed.at[rows, :], out_s.at[0, r], out_r.at[0, r], p.pair)

    def back(rows_at):
        rows = pl.ds(rows_at, HALF)
        pre[...] = dot(low_two[rows, :], wf[:, D:])

        def times(row):
            here = pl.ds(row, 64)
            there = pl.ds(pl.multiple_of(rows_at + row, 64), 64)
            slope[there, :] = (pre[here, :] * slope[there, :].astype(F32)).astype(BF16)

        steps(HALF, 64, times)
        return dot_nt(slope[rows, :], wf[:, :D])

    if ring:
        scatter_sems = (sxs, sxr, szs, szr)
        held = (axsend, axrecv, azsend, azrecv)
        scatter_up, scatter_down, *scatter_heads = (
            Scatter(p, share, src, cols_of, *held, [part.at[number] for part in scatter_sems])
            for number, (src, cols_of, held) in enumerate(
                (
                    (grads, slice(0, D), (xsend, fxrecv, zsend, fzrecv)),
                    (grads, slice(D, FFN), (xsend, fxrecv, zsend, fzrecv)),
                    (grads, slice(0, QK), held),
                    (grads, slice(QK, 2 * QK), held),
                    (grads, slice(2 * QK, ATT), held),
                )
            )
        )
    else:
        scatter_up = scatter_down = None
        scatter_heads = [None] * HEADS
    block = 4 * share if ring else D // 2

    def weight_blocks(work, scatter):
        def run(i, carry):
            place = (p.z // 2 + 1 + i) % (ring // 2) if ring else i
            work(pl.ds(pl.multiple_of(place * block, block), block))
            if ring:
                far = 1 - p.z % 2
                for line in (far, 1 - far):
                    scatter.start((2 * place + line + ring - p.z) % ring)
            return carry

        lax.fori_loop(0, D // block, run, 0)

    def up_weights(rows):
        grads[rows, :D] = grad_of(shared, rows, slope)

    def down_weights(rows):
        grads[rows, D:] = grad_of(low_two, rows, active)

    def grad_of(left, rows, right):
        return dot_tn(left[:, rows], right[...])

    def stage_c(r, carry):
        ograd_copy(r).wait()
        sum_b.wait(r)

        def part(row):
            rows = pl.ds(pl.multiple_of(own_at(r) + row, 128), 128)
            here = pl.ds(row, 128)
            residual = xone[r, here, :] * gain_one + bias_one + sum_b.total(r, here)
            normal, scale = norm_of(residual)
            stage[r, here, :] = (normal * gain_two + bias_two).astype(BF16)
            grad = ograd[r, here, :].astype(F32)
            value = norm_back(grad * gain_two, normal, scale)
            gtwo[r, here, :] = value
            low_two[rows, :] = value.astype(BF16)
            nsum[16:24, :] += fold(grad * normal)
            nsum[24:32, :] += fold(grad)

        steps(HALF, 128, part)
        pass_on(low_two, 1, p.own(r), r).start()
        mixed_here(r).start()
        mixed_pair(p.own(r), r).start()
        sum_b.close(r)
        sum_c.keep_last(r)
        sum_c.hold(r, back(own_at(r)))
        pass_on(low_two, 1, p.other(r), r).wait_recv()

        @pl.when(r == chunks - 1)
        def _():
            weight_blocks(down_weights, scatter_down)

        sum_c.give(r, back(other_at(r)))
        return carry

    lax.fori_loop(0, chunks, stage_c, 0)
    weight_blocks(up_weights, scatter_up)
    sum_c.keep(chunks - 1)

    def settle(r, carry):
        pass_on(shared, 0, p.own(r), r).wait_send()
        pass_on(low_two, 1, p.own(r), r).wait_send()
        return carry

    lax.fori_loop(0, chunks, settle, 0)
    pl.semaphore_signal(free, inc=1, device_id=p.pair, device_id_type=pl.DeviceIdType.MESH)
    if not ring:
        pltpu.sync_copy(grads, outf)
    low_one, gtext, gbox = shared, active, slope.at[:, :QK]
    gctx, gscore = slope.at[:SEQ, QK:], low_two.at[:SEQ, :SEQ]
    score_scale = HEAD_DIM**-0.5

    def attention_weights(h, rows):
        at, tile = h * QK, slice(h * 128, (h + 1) * 128)
        text = grad_of(hidden, rows, gtext.at[:, h * 256 : (h + 1) * 256])
        grads[rows, at : at + 128] = text[:, :128]
        grads[rows, at + 128 : at + 256] = text[:, 128:] + grad_of(low_one, rows, ctx.at[:, tile])
        grads[rows, at + 256 : at + 384] = grad_of(emb, rows, gbox.at[:, tile])

    def context_back(r, side):
        rows = pl.ds(pl.multiple_of(r * SEQ + side * HALF, HALF), HALF)
        there = pl.ds(pl.multiple_of(side * HALF, HALF), HALF)
        gctx[there, :] = dot(low_one[rows, :], wop[...]).astype(BF16)

    def attend_back(r):
        k_rows = pl.ds(pl.multiple_of(r * SEQ, SEQ), SEQ)
        low = lower_half((SEQ, 128))
        for h in range(HEADS):
            tile = slice(h * 128, (h + 1) * 128)
            dprob[...] = dot_nt(gctx[:, tile], vk[k_rows, tile])

            def soften(row):
                rows = pl.ds(row, SEQ)
                grad = dprob[rows, :]
                prob = probs[r, h, rows, :].astype(F32)
                weighted = jnp.sum(prob * grad, axis=-1, keepdims=True)
                gscore[rows, :] = (prob * (grad - weighted)).astype(BF16)

            steps(SEQ, SEQ, soften)
            left = dot(gscore[...], rk[k_rows, tile]) * score_scale
            right = dot_tn(gscore[...], lq[k_rows, tile]) * score_scale
            value = dot_tn(probs[r, h], gctx[:, tile])
            gtext[k_rows, h * 256 : h * 256 + 128] = jnp.where(
                low, left + pltpu.roll(left, HEAD_DIM, 1), right + pltpu.roll(right, HEAD_DIM, 1)
            ).astype(BF16)
            gbox[k_rows, tile] = jnp.where(low, right, left).astype(BF16)
            gtext[k_rows, h * 256 + 128 : h * 256 + 256] = value.astype(BF16)

            @pl.when(r == chunks - 1)
            def _():
                weight_blocks(partial(attention_weights, h), scatter_heads[h])


    def partial_of(rows):
        return dot_nt(gtext[rows, :], wtx[...])

    pl.semaphore_wait(free, 1)

    def stage_d(r, carry):
        sum_c.wait(r)

        def part(row):
            rows = pl.ds(pl.multiple_of(own_at(r) + row, 128), 128)
            here = pl.ds(row, 128)
            grad = gtwo[r, here, :] + sum_c.total(r, here)
            normal = xone[r, here, :]
            value = norm_back(grad * gain_one, normal, rone[r, here, 0:1])
            gtwo[r, here, :] = value
            low_one[rows, :] = value.astype(BF16)
            nsum[0:8, :] += fold(grad * normal)
            nsum[8:16, :] += fold(grad)

        steps(HALF, 128, part)
        pass_on(low_one, 2, p.own(r), r).start()
        sum_c.close(r)
        sum_d.keep_last(r)
        context_back(r, p.half)
        pass_on(low_one, 2, p.other(r), r).wait_recv()
        context_back(r, 1 - p.half)
        if ring:

            @pl.when(r == min(1, chunks - 1))
            def _():
                for k in range(1, ring):
                    scatter_down.middle(k)

            @pl.when(r == chunks - 1)
            def _():
                for k in range(1, ring):
                    scatter_up.middle(k)
                scatter_down.own(outf)
                scatter_up.own(outf)

        attend_back(r)
        sum_d.give(r, partial_of(p.other(r)))
        sum_d.hold(r, partial_of(p.own(r)))
        return carry

    lax.fori_loop(0, chunks, stage_d, 0)

    sum_d.keep(chunks - 1)
    for row in range(4):
        nsum[row : row + 1, :] = jnp.sum(nsum[row * 8 : row * 8 + 8, :], axis=0, keepdims=True)
    if ring:
        norm_pair = remote(nsum.at[0:8], nrecv.at[0], ns.at[0], nr.at[0], p.pair)
        norm_pair.start()
        for k in range(1, ring):
            scatter_heads[0].middle(k)
        norm_pair.wait_recv()
        nsum[8:16, :] = nsum[0:8, :] + nrecv[0]
        norm_x = remote(nsum.at[8:16], nrecv.at[1], ns.at[1], nr.at[1], p.xdev)
        norm_x.start()
        for scatter in scatter_heads[1:]:
            for k in range(1, ring):
                scatter.middle(k)
        for scatter in scatter_heads:
            scatter.own(outa)
        norm_x.wait_recv()
        nsum[16:24, :] = nsum[8:16, :] + nrecv[1]
        norm_z = [
            remote(nsum.at[16:24], nrecv.at[1 + k], ns.at[1 + k], nr.at[1 + k], p.zdev(k))
            for k in range(1, ring)
        ]
        for copy in norm_z:
            copy.start()
    else:
        pltpu.sync_copy(grads.at[:, :ATT], outa)
        nout[...] = nsum[0:8, :]

    def igrad_here(r):
        return pltpu.make_async_copy(stage.at[r], igrad.at[p.own(r), :], out_l.at[1, r])

    def igrad_pair(rows, r):
        return remote(stage.at[r], igrad.at[rows, :], out_s.at[1, r], out_r.at[1, r], p.pair)

    def stage_e(r, carry):
        mixed_here(r).wait()
        mixed_pair(p.own(r), r).wait_send()
        mixed_pair(p.other(r), r).wait_recv()
        sum_d.wait(r)
        stage[r] = (gtwo[r] + sum_d.total(r, slice(None))).astype(BF16)
        igrad_here(r).start()
        igrad_pair(p.own(r), r).start()
        sum_d.close(r)
        pass_on(low_one, 2, p.own(r), r).wait_send()
        return carry

    lax.fori_loop(0, chunks, stage_e, 0)
    if ring:
        for gather in (gather_a, gather_f, gather_n):
            gather.drain()
        scatter_down.finish(outf)
        scatter_up.finish(outf)
        for scatter in scatter_heads:
            scatter.finish(outa)
        for scatter in [scatter_down, scatter_up] + scatter_heads:
            scatter.sent()
        summed = nsum[16:24, :]
        for k in range(1, ring):
            norm_z[k - 1].wait_recv()
            summed = summed + nrecv[1 + k]
        for d in range(2 * ring):

            @pl.when(p.dp == d)
            def _():
                nout[:, :share] = summed[:, d * share : (d + 1) * share]

        for copy in [norm_pair, norm_x] + norm_z:
            copy.wait_send()

    def end(r, carry):
        igrad_here(r).wait()
        igrad_pair(p.own(r), r).wait_send()
        igrad_pair(p.other(r), r).wait_recv()
        return carry

    lax.fori_loop(0, chunks, end, 0)


def adam_step(weight, gradient, moment, second, rate, decay):
    moment_new = beta_first * moment + (1.0 - beta_first) * gradient
    second_new = beta_second * second + (1.0 - beta_second) * gradient * gradient
    moment_hat = moment_new / (1.0 - beta_first**STEP)
    second_hat = second_new / (1.0 - beta_second**STEP)
    weight_new = weight - rate * (
        moment_hat / (jnp.sqrt(second_hat) + epsilon_adam) + decay * weight
    )
    return (weight_new, moment_new, second_new)


def vmem():
    return pl.BlockSpec(memory_space=pltpu.VMEM)


def dma(*shape):
    return pltpu.SemaphoreType.DMA(shape)


def heads_of(value):
    return [value[:, h * HEAD_DIM : (h + 1) * HEAD_DIM] for h in range(value.shape[1] // HEAD_DIM)]


def interleave(first, second):
    pairs = zip(heads_of(first), heads_of(second))
    return jnp.concatenate([part for pair in pairs for part in pair], axis=1)


def pack_attention(attn_in, attn_out):
    low = [attn_in[i].astype(BF16) for i in range(5)]
    return jnp.concatenate(
        [
            interleave(low[0], low[1]),
            interleave(attn_out[...].T.astype(BF16), low[2]),
            interleave(low[4], low[3]),
        ],
        axis=1,
    )


def finish_kernel(*refs):
    grads, (mixed_in, igrad_in), olds = refs[:3], refs[3:5], refs[5:20]
    (mixed, igrad), news, held, made = refs[20:22], refs[22:37], refs[37:55], refs[55:70]
    passing, leaving = refs[70:72], (refs[70], refs[72])
    in_sems, out_sems, fetch_sems, copy_sems = refs[73:]
    reads = [
        pltpu.make_async_copy(src, dst, in_sems.at[i])
        for i, (src, dst) in enumerate(zip(grads + olds, held))
    ]
    fetches, copies = [], []
    for src, mid, end, dst in zip((mixed_in, igrad_in), passing, leaving, (mixed, igrad)):
        size = src.shape[0] // 4
        for part in range(4):
            rows, i = pl.ds(part * size, size), len(copies)
            fetches.append(
                pltpu.make_async_copy(src.at[rows, :], mid.at[rows, :], fetch_sems.at[i])
            )
            copies.append(
                pltpu.make_async_copy(end.at[rows, :], dst.at[rows, :], copy_sems.at[i])
            )
    for copy in reads + fetches:
        copy.start()
    writes = [
        pltpu.make_async_copy(src, dst, out_sems.at[i])
        for i, (src, dst) in enumerate(zip(made, news))
    ]
    size = igrad.shape[0] // 4
    for number, (fetch, copy) in enumerate(zip(fetches, copies)):
        fetch.wait()
        if number >= 4:
            rows = pl.ds((number - 4) * size, size)
            leaving[1][rows, :] = passing[1][rows, :].astype(F32)
        copy.start()
    for copy in reads[:3]:
        copy.wait()
    reda, redf, nred = held[:3]
    held = held[3:]

    def update(number, gradients, rate, decay):
        for copy in reads[3 + 3 * number : 6 + 3 * number]:
            copy.wait()
        for at, gradient in gradients:
            old = [held[3 * number + i][at] for i in range(3)]
            new = adam_step(old[0], gradient, old[1], old[2], rate, decay)
            for i in range(3):
                made[3 * number + i][at] = new[i]
        for copy in writes[3 * number : 3 * number + 3]:
            copy.start()

    parts = heads_of(reda[...])
    grad_q, grad_k, grad_o, grad_v, grad_kb, grad_qb = (
        jnp.concatenate(parts[i::6], axis=1) for i in range(6)
    )
    update(0, enumerate((grad_q, grad_k, grad_v, grad_qb, grad_kb)), rate_matrix, decay_matrix)
    update(1, [(Ellipsis, grad_o.T)], rate_matrix, decay_matrix)
    update(2, [(Ellipsis, redf[:, :D])], rate_matrix, decay_matrix)
    update(3, [(Ellipsis, redf[:, D:])], rate_matrix, decay_matrix)
    update(4, [(Ellipsis, nred[0:4, : held[12].shape[1]])], rate_norm, 0.0)
    for copy in copies + writes:
        copy.wait()


def box_lanes():
    quarter = D // 4
    place = np.arange(D)
    rows = np.zeros((8, D), np.float32)
    rows[0] = np.exp((place % quarter) * (-math.log(10000.0) / quarter))
    rows[1] = place >= 2 * quarter
    rows[2] = place // quarter % 2
    return jnp.asarray(rows)


def per_device(
    devices,
    hidden_in,
    page_ids,
    pad_mask,
    boxes,
    out_grad,
    attn_in,
    attn_in_moment,
    attn_in_second,
    attn_out,
    attn_out_moment,
    attn_out_second,
    ffn_in,
    ffn_in_moment,
    ffn_in_second,
    ffn_out,
    ffn_out_moment,
    ffn_out_second,
    norm_weight,
    norm_moment,
    norm_second,
):
    tokens = hidden_in.shape[0]
    chunks = tokens // SEQ
    share = attn_in.shape[1]
    ring = devices // 2 if devices % 4 == 0 and share % 32 == 0 else 0
    weights = (attn_in, attn_out, ffn_in, ffn_out.T, norm_weight)
    if not ring:
        packf = jnp.concatenate([ffn_in.astype(BF16), ffn_out.T.astype(BF16)], axis=1)
        pnorm = lax.all_gather(norm_weight, "dp", axis=1, tiled=True)
        weights = (
            lax.all_gather(pack_attention(attn_in, attn_out), "dp", axis=0, tiled=True),
            lax.all_gather(packf, "dp", axis=0, tiled=True),
            jnp.pad(pnorm, ((0, 4), (0, 0))),
        )
    pages, padding = (part.reshape(tokens // 128, 128) for part in (page_ids, pad_mask))
    count = max(ring, 1)
    any_space = pl.BlockSpec(memory_space=pl.ANY)
    inner = share if ring else 16
    tile = pltpu.VMEM((tokens, D), BF16)
    wide = pltpu.VMEM((tokens, QK), BF16)
    own = pltpu.VMEM((chunks, HALF, D), F32)
    own_low = pltpu.VMEM((chunks, HALF, D), BF16)
    att_share = pltpu.VMEM((count, inner, ATT), BF16)
    ffn_share = pltpu.VMEM((count, inner, FFN), BF16)
    att_along = pltpu.VMEM((max(count - 1, 1), inner, ATT), BF16)
    ffn_along = pltpu.VMEM((max(count - 1, 1), inner, FFN), BF16)
    mixed, input_grad, reda, redf, nred = pl.pallas_call(
        partial(layer_kernel, ring, chunks),
        out_shape=(
            jax.ShapeDtypeStruct((tokens, D), BF16),
            jax.ShapeDtypeStruct((tokens, D), BF16),
            jax.ShapeDtypeStruct((share if ring else D, ATT), F32),
            jax.ShapeDtypeStruct((share if ring else D, FFN), F32),
            jax.ShapeDtypeStruct((8, max(share, 128)) if ring else (8, D), F32),
        ),
        in_specs=[any_space] + [vmem()] * 4 + [(vmem(),) * len(weights), any_space],
        out_specs=(any_space,) * 2 + (vmem() if ring else any_space,) * 2 + (vmem(),),
        scratch_shapes=[
            pltpu.VMEM((D, ATT), BF16),
            pltpu.VMEM((D, FFN), BF16),
            pltpu.VMEM((2 * count, 8, max(share, 128)), F32),
            pltpu.VMEM((8, D), F32),
            pltpu.VMEM((8, tokens), F32),
            pltpu.VMEM((tokens, 128), F32),
            tile,
            pltpu.VMEM((D, D), BF16),
            pltpu.VMEM((D, QK), BF16),
            pltpu.VMEM((D // 256, 256, 256), BF16),
            wide,
            wide,
            wide,
            pltpu.VMEM((chunks, HEADS, SEQ, SEQ), BF16),
            wide,
            tile,
            pltpu.VMEM((SEQ, D), F32),
            own_low,
            own,
            pltpu.VMEM((chunks, HALF, 128), F32),
            own,
            tile,
            tile,
            tile,
            tile,
            pltpu.VMEM((max(chunks, D // 256), HALF, D), BF16),
            pltpu.VMEM((D, FFN), F32),
            pltpu.VMEM((32, D), F32),
            pltpu.VMEM((count + 1, 8, D), F32),
            ffn_share,
            ffn_along,
            ffn_share,
            ffn_along,
            att_share,
            att_along,
            att_share,
            att_along,
            own_low,
            own_low,
            own_low,
            pltpu.VMEM((2, chunks, HALF, D), BF16),
            pltpu.SemaphoreType.REGULAR,
        ]
        + [dma(3, 2, count)]
        + [dma(3, count)] * 3
        + [dma(2, chunks)] * 4
        + [dma(3, chunks)] * 2
        + [dma(2, chunks)] * 3
        + [dma(chunks)]
        + [dma(count + 1)] * 2
        + [pltpu.SemaphoreType.DMA]
        + [dma(3, chunks)] * 2
        + [dma(3)] * 2
        + [dma(5, count)] * 4,
        compiler_params=pltpu.CompilerParams(
            collective_id=0, has_side_effects=True, vmem_limit_bytes=VMEM_LIMIT
        ),
    )(hidden_in, boxes.T, pages, padding, box_lanes(), weights, out_grad)
    if not ring:
        reda, redf = (
            lax.psum_scatter(part, "dp", scatter_dimension=0, tiled=True) for part in (reda, redf)
        )
        nred = lax.psum(nred, ("dp", "mp")) * 0.5
        nred = lax.dynamic_slice_in_dim(nred, lax.axis_index("dp") * share, share, 1)
    old = (
        (attn_in, attn_in_moment, attn_in_second)
        + (attn_out, attn_out_moment, attn_out_second)
        + (ffn_in, ffn_in_moment, ffn_in_second)
        + (ffn_out.T, ffn_out_moment.T, ffn_out_second.T)
        + (norm_weight, norm_moment, norm_second)
    )
    large = (mixed, input_grad)
    wide_grad = jax.ShapeDtypeStruct(input_grad.shape, F32)
    summed = (reda, redf, nred)
    new = pl.pallas_call(
        finish_kernel,
        out_shape=tuple(
            jax.ShapeDtypeStruct(part.shape, part.dtype) for part in (mixed, wide_grad) + old
        ),
        in_specs=[any_space] * 20,
        out_specs=(any_space,) * 17,
        scratch_shapes=[pltpu.VMEM(part.shape, F32) for part in summed + old + old]
        + [pltpu.VMEM(part.shape, part.dtype) for part in large + (wide_grad,)]
        + [dma(18), dma(15), dma(8), dma(8)],
        compiler_params=pltpu.CompilerParams(vmem_limit_bytes=VMEM_LIMIT),
    )(*summed, *large, *old)
    return new[:11] + tuple(part.T for part in new[11:14]) + new[14:]


def solution(mesh):
    rows = P("dp", None)
    into = P(None, "dp", "mp")
    out = P("mp", "dp")
    up = P("dp", "mp")
    norm = P(None, "dp")
    return jax.shard_map(
        partial(per_device, mesh.shape["dp"]),
        mesh=mesh,
        in_specs=(rows, P("dp"), P("dp"), rows, rows)
        + (into,) * 3
        + (out,) * 3
        + (up,) * 3
        + (out,) * 3
        + (norm,) * 3,
        out_specs=(rows, rows) + (into,) * 3 + (out,) * 3 + (up,) * 3 + (out,) * 3 + (norm,) * 3,
        check_vma=False,
    )
```

```python
from functools import partial
import math

import jax
import jax.numpy as jnp
import numpy as np
from jax import lax
from jax.experimental import pallas as pl
from jax.experimental.pallas import tpu as pltpu
from jax.sharding import PartitionSpec as P

D = 768
HEAD_DIM = 64
SEQ = 512
HALF = SEQ // 2
STEP = 10
HEADS = 3
QK = HEADS * 128
ATT = 3 * QK
FFN = 2 * D

epsilon_norm = 1e-12
epsilon_adam = 1e-08
beta_first = 0.9
beta_second = 0.999
rate_matrix = 0.05
rate_norm = 0.2
decay_matrix = 0.01
masked_score = -1e30

F32 = jnp.float32
BF16 = jnp.bfloat16
VMEM_LIMIT = 60 * 1024 * 1024


def dot(a, b):
    return jnp.dot(a, b, preferred_element_type=F32)


def dot_nt(a, b):
    return lax.dot_general(a, b, (((1,), (1,)), ((), ())), preferred_element_type=F32)


def dot_tn(a, b):
    return lax.dot_general(a, b, (((0,), (0,)), ((), ())), preferred_element_type=F32)


def remote(src, dst, send, recv, device):
    return pltpu.make_async_remote_copy(
        src_ref=src,
        dst_ref=dst,
        send_sem=send,
        recv_sem=recv,
        device_id=device,
        device_id_type=pl.DeviceIdType.MESH,
    )


def steps(total, size, body):
    def run(i, carry):
        body(pl.multiple_of(i * size, size))
        return carry

    lax.fori_loop(0, total // size, run, 0)


def lower_half(shape):
    return lax.broadcasted_iota(jnp.int32, shape, len(shape) - 1) % 128 < HEAD_DIM


class Place:
    def __init__(self, ring):
        self.dp = lax.axis_index("dp")
        self.mp = lax.axis_index("mp")
        self.half = self.mp % 2
        self.pair = (self.dp, self.mp + 1 - 2 * self.half)
        self.across = (self.dp, (self.mp + 2) % 4)
        self.diagonal = (self.dp, (self.mp + 2) % 4 + 1 - 2 * self.half)
        self.ring = ring
        self.z = self.dp // 2
        self.x = self.dp % 2
        self.xdev = (self.dp + 1 - 2 * self.x, self.mp)

    def zdev(self, k):
        return (((self.z + k) % self.ring) * 2 + self.x, self.mp)

    def greet(self):
        peers = [self.pair, self.across, self.diagonal]
        if self.ring:
            peers += [self.xdev] + [self.zdev(k) for k in range(1, self.ring)]
        barrier = pltpu.get_barrier_semaphore()
        for peer in peers:
            pl.semaphore_signal(
                barrier, inc=1, device_id=peer, device_id_type=pl.DeviceIdType.MESH
            )
        pl.semaphore_wait(barrier, len(peers))

    def own(self, r):
        return pl.ds(pl.multiple_of(r * SEQ + self.half * HALF, HALF), HALF)

    def other(self, r):
        return pl.ds(pl.multiple_of(r * SEQ + (1 - self.half) * HALF, HALF), HALF)


class Gather:
    def __init__(self, place, kind, at, sems):
        self.p, self.at = place, at
        zs, zr, xs, xr = sems
        self.zs, self.zr, self.xs, self.xr = (
            zs.at[kind],
            zr.at[kind],
            xs.at[kind],
            xr.at[kind],
        )

    def hop(self, line, up):
        p = self.p
        view = self.at(2 * line + p.x)
        peer = (p.dp + 2, p.mp) if up else (p.dp - 2, p.mp)
        return remote(view, view, self.zs.at[int(up), line], self.zr.at[line], peer)

    def side(self, line, x):
        view = self.at(2 * line + x)
        return remote(view, view, self.xs.at[line], self.xr.at[line], self.p.xdev)

    def send(self, line, up):
        p = self.p

        @pl.when(p.z < p.ring - 1 if up else p.z > 0)
        def _():
            self.hop(line, up).start()

    def start(self):
        self.send(self.p.z, True)
        self.send(self.p.z, False)

    def cross(self):
        self.side(self.p.z, self.p.x).start()

    def step(self, s):
        p = self.p

        @pl.when(p.z >= s)
        def _():
            self.hop(p.z - s, True).wait_recv()
            self.send(p.z - s, True)
            self.side(p.z - s, p.x).start()

        @pl.when(p.z + s < p.ring)
        def _():
            self.hop(p.z + s, False).wait_recv()
            self.send(p.z + s, False)
            self.side(p.z + s, p.x).start()

    def finish(self):
        for line in range(self.p.ring):
            self.side(line, 1 - self.p.x).wait_recv()

    def drain(self):
        p = self.p
        for line in range(p.ring):
            self.side(line, p.x).wait_send()

            @pl.when((p.z >= line) & (p.z < p.ring - 1))
            def _():
                self.hop(line, True).wait_send()

            @pl.when((p.z <= line) & (p.z > 0))
            def _():
                self.hop(line, False).wait_send()


class Sum:
    def __init__(self, place, parity, psend, precv, sums, yrecv, sems):
        self.p = place
        self.psend, self.precv = psend, precv
        self.sums, self.yrecv = sums, yrecv.at[parity]
        ps, pr, ys, yr = sems
        self.ps, self.pr, self.ys, self.yr = (
            ps.at[parity],
            pr.at[parity],
            ys.at[parity],
            yr.at[parity],
        )

    def to_pair(self, r):
        return remote(
            self.psend.at[r], self.precv.at[r], self.ps.at[r], self.pr.at[r], self.p.pair
        )

    def over(self, r):
        return remote(
            self.sums.at[r], self.yrecv.at[r], self.ys.at[r], self.yr.at[r], self.p.across
        )

    def give(self, r, value):
        self.psend[r] = value.astype(BF16)
        self.to_pair(r).start()

    def hold(self, r, value):
        self.sums[r] = value.astype(BF16)

    def keep(self, r):
        self.to_pair(r).wait_recv()
        self.sums[r] = (self.sums[r].astype(F32) + self.precv[r].astype(F32)).astype(BF16)
        self.over(r).start()

    def keep_last(self, r):
        @pl.when(r > 0)
        def _():
            self.keep(r - 1)

    def wait(self, r):
        self.over(r).wait_recv()

    def total(self, r, rows):
        return self.sums[r, rows, :].astype(F32) + self.yrecv[r, rows, :].astype(F32)

    def close(self, r):
        self.to_pair(r).wait_send()
        self.over(r).wait_send()


def rolled(value):
    return pltpu.roll(value.astype(F32), HEAD_DIM, 1)


def embed_rows(coords, lanes, out, row):
    rows = pl.ds(row, 64)
    here = coords[rows, :]
    across, upward = here[:, 0:1], here[:, 1:2]
    frequency, second, shift = lanes[0:1, :], lanes[1:2, :], lanes[2:3, :]
    angle = (across + (upward - across) * second) * frequency
    turns = jnp.round(angle * (2.0 / math.pi))
    rest = ((angle - turns * 1.5703125) - turns * 4.837512969970703125e-4) - turns * (
        7.54978995489188216e-8
    )
    square = rest * rest
    sine = rest + rest * square * (
        -1.6666654611e-1 + square * (8.3321608736e-3 + square * -1.9515295891e-4)
    )
    cosine = (
        1.0
        - 0.5 * square
        + square
        * square
        * (
            4.166664568298827e-2
            + square * (-1.388731625493765e-3 + square * 2.443315711809948e-5)
        )
    )
    quarter = (turns + shift).astype(jnp.int32)
    value = jnp.where((quarter & 1) == 1, cosine, sine)
    out[rows, :] = jnp.where((quarter & 2) == 2, -value, value).astype(BF16)


def norm_of(values):
    center = jnp.mean(values, axis=-1, keepdims=True)
    shifted = values - center
    spread = jnp.mean(shifted * shifted, axis=-1, keepdims=True)
    scale = lax.rsqrt(spread + epsilon_norm)
    return shifted * scale, scale


def norm_back(upstream, normal, scale):
    first = jnp.mean(upstream, axis=-1, keepdims=True)
    second = jnp.mean(upstream * normal, axis=-1, keepdims=True)
    return (upstream - first - normal * second) * scale


def fold(values):
    rows, width = values.shape
    return jnp.sum(values.reshape(rows // 8, 8, width), axis=0)


class Scatter:
    def __init__(self, place, share, src, cols, xsend, xrecv, zsend, zrecv, sems):
        self.p, self.share, self.src, self.cols = place, share, src, cols
        self.xsend, self.xrecv, self.zsend, self.zrecv = xsend, xrecv, zsend, zrecv
        self.xs, self.xr, self.zs, self.zr = sems

    def rows(self, k, x):
        d = ((self.p.z + k) % self.p.ring) * 2 + x
        return pl.ds(pl.multiple_of(d * self.share, self.share), self.share)

    def xcopy(self, k):
        return remote(
            self.xsend.at[k, :, self.cols],
            self.xrecv.at[k, :, self.cols],
            self.xs.at[k],
            self.xr.at[k],
            self.p.xdev,
        )

    def zcopy(self, k):
        return remote(
            self.zsend.at[k - 1, :, self.cols],
            self.zrecv.at[k - 1, :, self.cols],
            self.zs.at[k],
            self.zr.at[k],
            self.p.zdev(k),
        )

    def start(self, k):
        value = self.src[self.rows(k, 1 - self.p.x), self.cols]
        self.xsend[k, :, self.cols] = value.astype(BF16)
        self.xcopy(k).start()

    def added(self, k):
        self.xcopy(k).wait_recv()
        mine = self.src[self.rows(k, self.p.x), self.cols]
        return mine + self.xrecv[k, :, self.cols].astype(F32)

    def middle(self, k):
        self.zsend[k - 1, :, self.cols] = self.added(k).astype(BF16)
        self.zcopy(k).start()

    def kth(self, i):
        p = self.p
        place = (p.z // 2 + 1 + i // 2) % (p.ring // 2)
        line = (i + 1 + p.z) % 2
        return (2 * place + line + p.ring - p.z) % p.ring

    def middles(self, first, last):
        for i in range(first, last):
            self.middle(self.kth(i))

    def own(self, out):
        out[:, self.cols] = self.added(0)

    def sent(self):
        for k in range(self.p.ring):
            self.xcopy(k).wait_send()
        for k in range(1, self.p.ring):
            self.zcopy(k).wait_send()

    def finish(self, out):
        value = out[:, self.cols]
        for k in range(1, self.p.ring):
            self.zcopy(k).wait_recv()
            value = value + self.zrecv[k - 1, :, self.cols].astype(F32)
        out[:, self.cols] = value


def layer_kernel(
    ring,
    chunks,
    hidden_hbm,
    boxes,
    pages,
    padding,
    lanes,
    weights,
    out_grad,
    mixed,
    igrad,
    outa,
    outf,
    nout,
    wa,
    wf,
    nbuf,
    norm,
    tags,
    cols,
    hidden,
    wtx,
    wop,
    wo,
    lq,
    rk,
    vk,
    probs,
    ctx,
    emb,
    big,
    ograd,
    xone,
    rone,
    gtwo,
    shared,
    active,
    slope,
    low_two,
    stage,
    grads,
    nsum,
    nrecv,
    xsend,
    zsend,
    fxrecv,
    fzrecv,
    axsend,
    azsend,
    axrecv,
    azrecv,
    psend,
    precv,
    sums,
    yrecv,
    free,
    gather_zs,
    gather_zr,
    gather_xs,
    gather_xr,
    ps,
    pr,
    ys,
    yr,
    share_s,
    share_r,
    out_s,
    out_r,
    out_l,
    ol,
    ns,
    nr,
    hs,
    ctx_s,
    ctx_r,
    wo_s,
    wo_r,
    sxs,
    sxr,
    szs,
    szr,
):
    p = Place(ring)
    tokens = hidden.shape[0]

    def ograd_copy(r):
        return pltpu.make_async_copy(out_grad.at[p.own(r), :], ograd.at[r], ol.at[r])

    hidden_copy = pltpu.make_async_copy(hidden_hbm, hidden, hs)
    hidden_copy.start()
    for r in range(chunks):
        ograd_copy(r).start()
    sums_sems = (ps, pr, ys, yr)
    sum_b, sum_c, sum_d = (
        Sum(p, number % 2, psend, precv, sums, yrecv, sums_sems) for number in range(3)
    )
    if ring:
        attn_in, attn_out, ffn_in, ffn_out, norm_in = weights
        share = ffn_in.shape[0]
        gather_sems = (gather_zs, gather_zr, gather_xs, gather_xr)

        def rows_of(ref):
            return lambda d: ref.at[pl.ds(pl.multiple_of(d * share, share), share), :]

        gather_a = Gather(p, 0, rows_of(wa), gather_sems)
        gather_f = Gather(p, 1, rows_of(wf), gather_sems)
        gather_n = Gather(p, 2, lambda d: nbuf.at[d], gather_sems)
        mine = pl.ds(pl.multiple_of(p.dp * share, share), share)
        wa[mine, :] = pack_attention(attn_in, attn_out)
        p.greet()
        gather_a.start()
        gather_a.cross()
        wf[mine, :D] = ffn_in[...].astype(BF16)
        wf[mine, D:] = ffn_out[...].astype(BF16)
        nbuf[p.dp] = jnp.zeros_like(nbuf[0])
        nbuf[p.dp, 0:4, :share] = norm_in[...]
    else:
        p.greet()
        wa[...], wf[...], norm[...] = (part[...] for part in weights)
    key = jnp.where(padding[...] == 0, pages[...], -1)
    tags[...] = jnp.zeros_like(tags)
    tags[0:2, :] = boxes[...].astype(F32)
    for row in range(tokens // 128):
        span = slice(row * 128, row * 128 + 128)
        tags[2:3, span] = pages[row : row + 1, :].astype(F32)
        tags[3:4, span] = key[row : row + 1, :].astype(F32)
    for row in range(0, tokens, SEQ):
        cols[row : row + SEQ, 0:8] = tags[:, row : row + SEQ].T
    parts = max(ring - 1, 1) if tokens % (64 * max(ring - 1, 1)) == 0 else 1
    for part in range(parts):
        base = part * (tokens // parts)
        steps(
            tokens // parts,
            64,
            lambda row: embed_rows(cols, lanes, emb, pl.multiple_of(base + row, 64)),
        )
        if ring and part + 1 < parts:
            gather_a.step(part + 1)
    if ring:
        gather_f.start()
        gather_n.start()
        for s in range(parts, ring):
            gather_a.step(s)
        gather_f.cross()
        gather_n.cross()
        gather_a.finish()
        gather_f.step(1)
        gather_n.step(1)

    def build(row):
        rows = pl.ds(row, 256)
        low = lower_half((256, 128))
        for h in range(HEADS):
            qk_cols = slice(h * 128, (h + 1) * 128)
            ov_cols = slice(QK + h * 128, QK + (h + 1) * 128)
            ov = wa[rows, ov_cols].astype(F32)
            wtx[rows, h * 256 : h * 256 + 128] = wa[rows, qk_cols]
            wtx[rows, h * 256 + 128 : h * 256 + 256] = jnp.where(
                low, rolled(wa[rows, qk_cols]), ov
            ).astype(BF16)
            wop[rows, qk_cols] = jnp.where(low, 0.0, rolled(ov)).astype(BF16)
        first, second, third = (
            wa[rows, QK + h * 128 : QK + (h + 1) * 128].astype(F32) for h in range(HEADS)
        )
        wo[row // 256, :, :128] = jnp.where(low, first, rolled(second)).astype(BF16)
        wo[row // 256, :, 128:] = jnp.where(low, third, 0.0).astype(BF16)

    steps(D, 256, build)

    def wo_slot(k):
        return stage.at[0 : D // 256, :, k * 256 : (k + 1) * 256]

    def wo_copy(k):
        if k == 2:
            return remote(wo_slot(1), wo_slot(2), wo_s.at[2], wo_r.at[2], p.pair)
        return remote(wo, wo_slot(k), wo_s.at[k], wo_r.at[k], (p.pair, p.across)[k])

    wo_copy(1).start()
    wo_copy(0).start()
    hidden_copy.wait()

    def project(row):
        rows = pl.ds(row, HALF)
        text = dot(hidden[rows, :], wtx[...])
        box = dot(emb[rows, :], wa[:, 2 * QK :])
        low = lower_half((HALF, 128))
        for h in range(HEADS):
            tile = slice(h * 128, (h + 1) * 128)
            word, extra = text[:, h * 256 : h * 256 + 128], box[:, tile]
            lq[rows, tile] = jnp.where(low, word, extra).astype(BF16)
            rk[rows, tile] = jnp.where(low, extra, word).astype(BF16)
            vk[rows, tile] = text[:, h * 256 + 128 : h * 256 + 256].astype(BF16)

    scores = big.at[:HALF, :SEQ]
    pre, post = big.at[:HALF, :], big.at[HALF:, :]
    dprob = big.at[:, :SEQ]

    def ctx_kept(r, own):
        rows = pl.ds(pl.multiple_of(r * SEQ + HALF, HALF), HALF)
        return active.at[rows, 256:512] if own else active.at[rows, 0:256]

    def ctx_copy(k, r):
        rows = pl.ds(pl.multiple_of(r * SEQ, HALF), HALF)
        peer = (p.pair, p.across, p.diagonal)[k]
        slot = active.at[rows, k * 256 : (k + 1) * 256]
        return remote(ctx_kept(r, k == 1), slot, ctx_s.at[k, r], ctx_r.at[k, r], peer)

    def attend(r, side, kept):
        found = []
        start = pl.multiple_of(side * HALF, HALF)
        q_rows = pl.ds(pl.multiple_of(r * SEQ + start, HALF), HALF)
        k_rows = pl.ds(pl.multiple_of(r * SEQ, SEQ), SEQ)
        low = lower_half((HALF, 128))
        pages = cols[q_rows, 2:3]
        here = lax.broadcasted_iota(jnp.int32, (HALF, SEQ), 0) + start
        there = lax.broadcasted_iota(jnp.int32, (HALF, SEQ), 1)
        allowed = (pages == tags[3:4, k_rows]) | (here == there)
        for h in range(HEADS):
            tile = slice(h * 128, (h + 1) * 128)
            left = lq[q_rows, tile]
            both = jnp.concatenate([left, jnp.where(low, left, jnp.zeros_like(left))], axis=1)
            right = jnp.concatenate([rk[k_rows, tile], vk[k_rows, tile]], axis=1)
            scores[...] = dot_nt(both, right)
            value = jnp.where(allowed, scores[...] * HEAD_DIM**-0.5, masked_score)
            raised = jnp.exp(value - jnp.max(value, axis=-1, keepdims=True))
            value = raised / jnp.sum(raised, axis=-1, keepdims=True)
            probs[r, h, pl.ds(start, HALF), :] = value.astype(BF16)
            found.append(dot(probs[r, h, pl.ds(start, HALF), :], vk[k_rows, tile]))
            turned = pltpu.roll(found[h], HEAD_DIM, 1)
            ctx[q_rows, tile] = jnp.where(low, turned, 0.0).astype(BF16)
            if h == 0:
                even = turned
        kept[:, :128] = jnp.where(low, even, found[1]).astype(BF16)
        kept[:, 128:] = ctx[q_rows, 256:384]

    def stage_a(r, carry):
        project(pl.multiple_of(r * SEQ, SEQ))
        project(pl.multiple_of(r * SEQ + HALF, HALF))
        attend(r, 1 - p.half, ctx_kept(r, False))
        ctx_copy(2, r).start()
        ctx_copy(0, r).start()
        attend(r, p.half, ctx_kept(r, True))
        ctx_copy(1, r).start()

        @pl.when(r == 0)
        def _():
            wo_copy(1).wait_recv()
            wo_copy(2).start()

        if ring > 3:

            @pl.when(r < 2)
            def _():
                gather_f.step(r + 2)
                gather_n.step(r + 2)

        return carry

    lax.fori_loop(0, chunks, stage_a, 0)
    if ring:
        for s in range(4 if ring > 3 and chunks > 1 else 2 + (ring > 3), ring):
            gather_f.step(s)
            gather_n.step(s)
        gather_n.finish()
        norm[...] = jnp.concatenate([nbuf[d, :, :share] for d in range(2 * ring)], axis=1)
        gather_f.finish()
    gain_one, bias_one = norm[0:1, :], norm[1:2, :]
    gain_two, bias_two = norm[2:3, :], norm[3:4, :]

    def pass_on(ref, number, rows, r):
        view = ref.at[rows, :]
        return remote(view, view, share_s.at[number, r], share_r.at[number, r], p.pair)

    def up_down(rows_at):
        rows = pl.ds(rows_at, HALF)
        pre[...] = dot(shared[rows, :], wf[:, :D])

        def gelu(row):
            here = pl.ds(row, 64)
            there = pl.ds(pl.multiple_of(rows_at + row, 64), 64)
            value = pre[here, :]
            below = 0.5 + 0.5 * lax.erf(value * math.sqrt(0.5))
            active[there, :] = (value * below).astype(BF16)
            density = jnp.exp(-0.5 * value * value) * (1.0 / math.sqrt(2.0 * math.pi))
            slope[there, :] = (below + value * density).astype(BF16)

        steps(HALF, 64, gelu)
        return dot_nt(active[rows, :], wf[:, D:])

    def own_at(r):
        return pl.multiple_of(r * SEQ + p.half * HALF, HALF)

    def other_at(r):
        return pl.multiple_of(r * SEQ + (1 - p.half) * HALF, HALF)

    wo_copy(0).wait_recv()
    wo_copy(2).wait_recv()
    for k in range(3):
        wo_copy(k).wait_send()

    def stage_b(r, carry):
        for k in range(3):
            ctx_copy(k, r).wait_recv()
        theirs = active[pl.ds(pl.multiple_of(r * SEQ, HALF), HALF), :]
        mine = ctx_kept(r, True)[...]
        for j in range(D // 256):
            cut = [dot_nt(theirs[:, k * 256 : k * 256 + 256], wo_slot(k)[j]) for k in range(3)]
            pre[:, j * 256 : (j + 1) * 256] = dot_nt(mine, wo[j]) + cut[0]
            post[:, j * 256 : (j + 1) * 256] = cut[1] + cut[2]

        def part(row):
            rows = pl.ds(pl.multiple_of(own_at(r) + row, 128), 128)
            here = pl.ds(row, 128)
            normal, scale = norm_of(hidden[rows, :].astype(F32) + (pre[here, :] + post[here, :]))
            xone[r, here, :] = normal
            rone[r, here, :] = jnp.broadcast_to(scale, (128, 128))
            shared[rows, :] = (normal * gain_one + bias_one).astype(BF16)

        steps(HALF, 128, part)
        pass_on(shared, 0, p.own(r), r).start()
        for k in range(3):
            ctx_copy(k, r).wait_send()
        sum_b.keep_last(r)
        sum_b.hold(r, up_down(own_at(r)))
        pass_on(shared, 0, p.other(r), r).wait_recv()
        sum_b.give(r, up_down(other_at(r)))
        return carry

    lax.fori_loop(0, chunks, stage_b, 0)
    sum_b.keep(chunks - 1)
    nsum[...] = jnp.zeros_like(nsum)

    def mixed_here(r):
        return pltpu.make_async_copy(stage.at[r], mixed.at[p.own(r), :], out_l.at[0, r])

    def mixed_pair(rows, r):
        return remote(stage.at[r], mixed.at[rows, :], out_s.at[0, r], out_r.at[0, r], p.pair)

    def back(rows_at):
        rows = pl.ds(rows_at, HALF)
        pre[...] = dot(low_two[rows, :], wf[:, D:])

        def times(row):
            here = pl.ds(row, 64)
            there = pl.ds(pl.multiple_of(rows_at + row, 64), 64)
            slope[there, :] = (pre[here, :] * slope[there, :].astype(F32)).astype(BF16)

        steps(HALF, 64, times)
        return dot_nt(slope[rows, :], wf[:, :D])

    if ring:
        scatter_sems = (sxs, sxr, szs, szr)
        held = (axsend, axrecv, azsend, azrecv)
        scatter_up, scatter_down, *scatter_heads = (
            Scatter(p, share, src, cols_of, *held, [part.at[number] for part in scatter_sems])
            for number, (src, cols_of, held) in enumerate(
                (
                    (grads, slice(0, D), (xsend, fxrecv, zsend, fzrecv)),
                    (grads, slice(D, FFN), (xsend, fxrecv, zsend, fzrecv)),
                    (grads, slice(0, QK), held),
                    (grads, slice(QK, 2 * QK), held),
                    (grads, slice(2 * QK, ATT), held),
                )
            )
        )
    else:
        scatter_up = scatter_down = None
        scatter_heads = [None] * HEADS
    block = 4 * share if ring else D // 2

    def weight_blocks(work, scatter):
        def run(i, carry):
            place = (p.z // 2 + 1 + i) % (ring // 2) if ring else i
            work(pl.ds(pl.multiple_of(place * block, block), block))
            if ring:
                for line in range(2):
                    scatter.start(scatter.kth(2 * i + line))
            return carry

        lax.fori_loop(0, D // block, run, 0)

    def up_weights(rows):
        grads[rows, :D] = grad_of(shared, rows, slope)

    def down_weights(rows):
        grads[rows, D:] = grad_of(low_two, rows, active)

    def grad_of(left, rows, right):
        return dot_tn(left[:, rows], right[...])

    def stage_c(r, carry):
        ograd_copy(r).wait()
        sum_b.wait(r)

        def part(row):
            rows = pl.ds(pl.multiple_of(own_at(r) + row, 128), 128)
            here = pl.ds(row, 128)
            residual = xone[r, here, :] * gain_one + bias_one + sum_b.total(r, here)
            normal, scale = norm_of(residual)
            stage[r, here, :] = (normal * gain_two + bias_two).astype(BF16)
            grad = ograd[r, here, :].astype(F32)
            value = norm_back(grad * gain_two, normal, scale)
            gtwo[r, here, :] = value
            low_two[rows, :] = value.astype(BF16)
            nsum[16:24, :] += fold(grad * normal)
            nsum[24:32, :] += fold(grad)

        steps(HALF, 128, part)
        pass_on(low_two, 1, p.own(r), r).start()
        mixed_here(r).start()
        mixed_pair(p.own(r), r).start()
        sum_b.close(r)
        sum_c.keep_last(r)
        sum_c.hold(r, back(own_at(r)))
        pass_on(low_two, 1, p.other(r), r).wait_recv()

        @pl.when(r == chunks - 1)
        def _():
            weight_blocks(down_weights, scatter_down)

        sum_c.give(r, back(other_at(r)))
        return carry

    lax.fori_loop(0, chunks, stage_c, 0)
    weight_blocks(up_weights, scatter_up)
    sum_c.keep(chunks - 1)

    def settle(r, carry):
        pass_on(shared, 0, p.own(r), r).wait_send()
        pass_on(low_two, 1, p.own(r), r).wait_send()
        return carry

    lax.fori_loop(0, chunks, settle, 0)
    pl.semaphore_signal(free, inc=1, device_id=p.pair, device_id_type=pl.DeviceIdType.MESH)
    if not ring:
        pltpu.sync_copy(grads, outf)
    low_one, gtext, gbox = shared, active, slope.at[:, :QK]
    gctx, gscore = slope.at[:SEQ, QK:], low_two.at[:SEQ, :SEQ]
    score_scale = HEAD_DIM**-0.5

    def attention_weights(h, rows):
        at, tile = h * QK, slice(h * 128, (h + 1) * 128)
        text = grad_of(hidden, rows, gtext.at[:, h * 256 : (h + 1) * 256])
        grads[rows, at : at + 128] = text[:, :128]
        grads[rows, at + 128 : at + 256] = text[:, 128:] + grad_of(low_one, rows, ctx.at[:, tile])
        grads[rows, at + 256 : at + 384] = grad_of(emb, rows, gbox.at[:, tile])

    def context_back(r, side):
        rows = pl.ds(pl.multiple_of(r * SEQ + side * HALF, HALF), HALF)
        there = pl.ds(pl.multiple_of(side * HALF, HALF), HALF)
        gctx[there, :] = dot(low_one[rows, :], wop[...]).astype(BF16)

    def attend_back(r):
        k_rows = pl.ds(pl.multiple_of(r * SEQ, SEQ), SEQ)
        low = lower_half((SEQ, 128))
        for h in range(HEADS):
            tile = slice(h * 128, (h + 1) * 128)
            dprob[...] = dot_nt(gctx[:, tile], vk[k_rows, tile])

            def soften(row):
                rows = pl.ds(row, SEQ)
                grad = dprob[rows, :]
                prob = probs[r, h, rows, :].astype(F32)
                weighted = jnp.sum(prob * grad, axis=-1, keepdims=True)
                gscore[rows, :] = (prob * (grad - weighted)).astype(BF16)

            steps(SEQ, SEQ, soften)
            left = dot(gscore[...], rk[k_rows, tile]) * score_scale
            right = dot_tn(gscore[...], lq[k_rows, tile]) * score_scale
            value = dot_tn(probs[r, h], gctx[:, tile])
            gtext[k_rows, h * 256 : h * 256 + 128] = jnp.where(
                low, left + pltpu.roll(left, HEAD_DIM, 1), right + pltpu.roll(right, HEAD_DIM, 1)
            ).astype(BF16)
            gbox[k_rows, tile] = jnp.where(low, right, left).astype(BF16)
            gtext[k_rows, h * 256 + 128 : h * 256 + 256] = value.astype(BF16)

            @pl.when(r == chunks - 1)
            def _():
                weight_blocks(partial(attention_weights, h), scatter_heads[h])


    def partial_of(rows):
        return dot_nt(gtext[rows, :], wtx[...])

    pl.semaphore_wait(free, 1)

    def stage_d(r, carry):
        sum_c.wait(r)

        def part(row):
            rows = pl.ds(pl.multiple_of(own_at(r) + row, 128), 128)
            here = pl.ds(row, 128)
            grad = gtwo[r, here, :] + sum_c.total(r, here)
            normal = xone[r, here, :]
            value = norm_back(grad * gain_one, normal, rone[r, here, 0:1])
            gtwo[r, here, :] = value
            low_one[rows, :] = value.astype(BF16)
            nsum[0:8, :] += fold(grad * normal)
            nsum[8:16, :] += fold(grad)

        steps(HALF, 128, part)
        pass_on(low_one, 2, p.own(r), r).start()
        sum_c.close(r)
        sum_d.keep_last(r)
        context_back(r, p.half)
        pass_on(low_one, 2, p.other(r), r).wait_recv()
        context_back(r, 1 - p.half)
        if ring:

            @pl.when(r == 0)
            def _():
                scatter_down.middles(0, ring - 1)

            @pl.when((r == 1) & (r < chunks - 1))
            def _():
                scatter_up.middles(0, 1)

            @pl.when(r == chunks - 1)
            def _():
                scatter_up.middles(1 if chunks > 2 else 0, ring - 1)
                scatter_down.own(outf)
                scatter_up.own(outf)

        attend_back(r)
        sum_d.give(r, partial_of(p.other(r)))
        sum_d.hold(r, partial_of(p.own(r)))
        return carry

    lax.fori_loop(0, chunks, stage_d, 0)

    sum_d.keep(chunks - 1)
    for row in range(4):
        nsum[row : row + 1, :] = jnp.sum(nsum[row * 8 : row * 8 + 8, :], axis=0, keepdims=True)
    if ring:
        norm_pair = remote(nsum.at[0:8], nrecv.at[0], ns.at[0], nr.at[0], p.pair)
        norm_pair.start()
        scatter_heads[0].middles(0, ring - 1)
        norm_pair.wait_recv()
        nsum[8:16, :] = nsum[0:8, :] + nrecv[0]
        norm_x = remote(nsum.at[8:16], nrecv.at[1], ns.at[1], nr.at[1], p.xdev)
        norm_x.start()
        for scatter in scatter_heads[1:]:
            scatter.middles(0, ring - 1)
        for scatter in scatter_heads:
            scatter.own(outa)
        norm_x.wait_recv()
        nsum[16:24, :] = nsum[8:16, :] + nrecv[1]
        norm_z = [
            remote(nsum.at[16:24], nrecv.at[1 + k], ns.at[1 + k], nr.at[1 + k], p.zdev(k))
            for k in range(1, ring)
        ]
        for copy in norm_z:
            copy.start()
    else:
        pltpu.sync_copy(grads.at[:, :ATT], outa)
        nout[...] = nsum[0:8, :]

    def igrad_here(r):
        return pltpu.make_async_copy(stage.at[r], igrad.at[p.own(r), :], out_l.at[1, r])

    def igrad_pair(rows, r):
        return remote(stage.at[r], igrad.at[rows, :], out_s.at[1, r], out_r.at[1, r], p.pair)

    def stage_e(r, carry):
        mixed_here(r).wait()
        mixed_pair(p.own(r), r).wait_send()
        mixed_pair(p.other(r), r).wait_recv()
        sum_d.wait(r)
        stage[r] = (gtwo[r] + sum_d.total(r, slice(None))).astype(BF16)
        igrad_here(r).start()
        igrad_pair(p.own(r), r).start()
        sum_d.close(r)
        pass_on(low_one, 2, p.own(r), r).wait_send()
        return carry

    lax.fori_loop(0, chunks, stage_e, 0)
    if ring:
        for gather in (gather_a, gather_f, gather_n):
            gather.drain()
        scatter_down.finish(outf)
        scatter_up.finish(outf)
        for scatter in scatter_heads:
            scatter.finish(outa)
        for scatter in [scatter_down, scatter_up] + scatter_heads:
            scatter.sent()
        summed = nsum[16:24, :]
        for k in range(1, ring):
            norm_z[k - 1].wait_recv()
            summed = summed + nrecv[1 + k]
        for d in range(2 * ring):

            @pl.when(p.dp == d)
            def _():
                nout[:, :share] = summed[:, d * share : (d + 1) * share]

        for copy in [norm_pair, norm_x] + norm_z:
            copy.wait_send()

    def end(r, carry):
        igrad_here(r).wait()
        igrad_pair(p.own(r), r).wait_send()
        igrad_pair(p.other(r), r).wait_recv()
        return carry

    lax.fori_loop(0, chunks, end, 0)


def adam_step(weight, gradient, moment, second, rate, decay):
    moment_new = beta_first * moment + (1.0 - beta_first) * gradient
    second_new = beta_second * second + (1.0 - beta_second) * gradient * gradient
    moment_hat = moment_new / (1.0 - beta_first**STEP)
    second_hat = second_new / (1.0 - beta_second**STEP)
    weight_new = weight - rate * (
        moment_hat / (jnp.sqrt(second_hat) + epsilon_adam) + decay * weight
    )
    return (weight_new, moment_new, second_new)


def vmem():
    return pl.BlockSpec(memory_space=pltpu.VMEM)


def dma(*shape):
    return pltpu.SemaphoreType.DMA(shape)


def heads_of(value):
    return [value[:, h * HEAD_DIM : (h + 1) * HEAD_DIM] for h in range(value.shape[1] // HEAD_DIM)]


def interleave(first, second):
    pairs = zip(heads_of(first), heads_of(second))
    return jnp.concatenate([part for pair in pairs for part in pair], axis=1)


def pack_attention(attn_in, attn_out):
    low = [attn_in[i].astype(BF16) for i in range(5)]
    return jnp.concatenate(
        [
            interleave(low[0], low[1]),
            interleave(attn_out[...].T.astype(BF16), low[2]),
            interleave(low[4], low[3]),
        ],
        axis=1,
    )


def finish_kernel(*refs):
    grads, (mixed_in, igrad_in), olds = refs[:3], refs[3:5], refs[5:20]
    (mixed, igrad), news, held, made = refs[20:22], refs[22:37], refs[37:55], refs[55:70]
    passing, leaving = refs[70:72], (refs[70], refs[72])
    in_sems, out_sems, fetch_sems, copy_sems = refs[73:]
    reads = [
        pltpu.make_async_copy(src, dst, in_sems.at[i])
        for i, (src, dst) in enumerate(zip(grads + olds, held))
    ]
    fetches, copies = [], []
    for src, mid, end, dst in zip((mixed_in, igrad_in), passing, leaving, (mixed, igrad)):
        size = src.shape[0] // 4
        for part in range(4):
            rows, i = pl.ds(part * size, size), len(copies)
            fetches.append(
                pltpu.make_async_copy(src.at[rows, :], mid.at[rows, :], fetch_sems.at[i])
            )
            copies.append(
                pltpu.make_async_copy(end.at[rows, :], dst.at[rows, :], copy_sems.at[i])
            )
    for copy in reads + fetches:
        copy.start()
    writes = [
        pltpu.make_async_copy(src, dst, out_sems.at[i])
        for i, (src, dst) in enumerate(zip(made, news))
    ]
    size = igrad.shape[0] // 4
    for number, (fetch, copy) in enumerate(zip(fetches, copies)):
        fetch.wait()
        if number >= 4:
            rows = pl.ds((number - 4) * size, size)
            leaving[1][rows, :] = passing[1][rows, :].astype(F32)
        copy.start()
    for copy in reads[:3]:
        copy.wait()
    reda, redf, nred = held[:3]
    held = held[3:]

    def update(number, gradients, rate, decay):
        for copy in reads[3 + 3 * number : 6 + 3 * number]:
            copy.wait()
        for at, gradient in gradients:
            old = [held[3 * number + i][at] for i in range(3)]
            new = adam_step(old[0], gradient, old[1], old[2], rate, decay)
            for i in range(3):
                made[3 * number + i][at] = new[i]
        for copy in writes[3 * number : 3 * number + 3]:
            copy.start()

    parts = heads_of(reda[...])
    grad_q, grad_k, grad_o, grad_v, grad_kb, grad_qb = (
        jnp.concatenate(parts[i::6], axis=1) for i in range(6)
    )
    update(0, enumerate((grad_q, grad_k, grad_v, grad_qb, grad_kb)), rate_matrix, decay_matrix)
    update(1, [(Ellipsis, grad_o.T)], rate_matrix, decay_matrix)
    update(2, [(Ellipsis, redf[:, :D])], rate_matrix, decay_matrix)
    update(3, [(Ellipsis, redf[:, D:])], rate_matrix, decay_matrix)
    update(4, [(Ellipsis, nred[0:4, : held[12].shape[1]])], rate_norm, 0.0)
    for copy in copies + writes:
        copy.wait()


def box_lanes():
    quarter = D // 4
    place = np.arange(D)
    rows = np.zeros((8, D), np.float32)
    rows[0] = np.exp((place % quarter) * (-math.log(10000.0) / quarter))
    rows[1] = place >= 2 * quarter
    rows[2] = place // quarter % 2
    return jnp.asarray(rows)


def per_device(
    devices,
    hidden_in,
    page_ids,
    pad_mask,
    boxes,
    out_grad,
    attn_in,
    attn_in_moment,
    attn_in_second,
    attn_out,
    attn_out_moment,
    attn_out_second,
    ffn_in,
    ffn_in_moment,
    ffn_in_second,
    ffn_out,
    ffn_out_moment,
    ffn_out_second,
    norm_weight,
    norm_moment,
    norm_second,
):
    tokens = hidden_in.shape[0]
    chunks = tokens // SEQ
    share = attn_in.shape[1]
    ring = devices // 2 if devices % 4 == 0 and share % 32 == 0 else 0
    weights = (attn_in, attn_out, ffn_in, ffn_out.T, norm_weight)
    if not ring:
        packf = jnp.concatenate([ffn_in.astype(BF16), ffn_out.T.astype(BF16)], axis=1)
        pnorm = lax.all_gather(norm_weight, "dp", axis=1, tiled=True)
        weights = (
            lax.all_gather(pack_attention(attn_in, attn_out), "dp", axis=0, tiled=True),
            lax.all_gather(packf, "dp", axis=0, tiled=True),
            jnp.pad(pnorm, ((0, 4), (0, 0))),
        )
    pages, padding = (part.reshape(tokens // 128, 128) for part in (page_ids, pad_mask))
    count = max(ring, 1)
    any_space = pl.BlockSpec(memory_space=pl.ANY)
    inner = share if ring else 16
    tile = pltpu.VMEM((tokens, D), BF16)
    wide = pltpu.VMEM((tokens, QK), BF16)
    own = pltpu.VMEM((chunks, HALF, D), F32)
    own_low = pltpu.VMEM((chunks, HALF, D), BF16)
    att_share = pltpu.VMEM((count, inner, ATT), BF16)
    ffn_share = pltpu.VMEM((count, inner, FFN), BF16)
    att_along = pltpu.VMEM((max(count - 1, 1), inner, ATT), BF16)
    ffn_along = pltpu.VMEM((max(count - 1, 1), inner, FFN), BF16)
    mixed, input_grad, reda, redf, nred = pl.pallas_call(
        partial(layer_kernel, ring, chunks),
        out_shape=(
            jax.ShapeDtypeStruct((tokens, D), BF16),
            jax.ShapeDtypeStruct((tokens, D), BF16),
            jax.ShapeDtypeStruct((share if ring else D, ATT), F32),
            jax.ShapeDtypeStruct((share if ring else D, FFN), F32),
            jax.ShapeDtypeStruct((8, max(share, 128)) if ring else (8, D), F32),
        ),
        in_specs=[any_space] + [vmem()] * 4 + [(vmem(),) * len(weights), any_space],
        out_specs=(any_space,) * 2 + (vmem() if ring else any_space,) * 2 + (vmem(),),
        scratch_shapes=[
            pltpu.VMEM((D, ATT), BF16),
            pltpu.VMEM((D, FFN), BF16),
            pltpu.VMEM((2 * count, 8, max(share, 128)), F32),
            pltpu.VMEM((8, D), F32),
            pltpu.VMEM((8, tokens), F32),
            pltpu.VMEM((tokens, 128), F32),
            tile,
            pltpu.VMEM((D, D), BF16),
            pltpu.VMEM((D, QK), BF16),
            pltpu.VMEM((D // 256, 256, 256), BF16),
            wide,
            wide,
            wide,
            pltpu.VMEM((chunks, HEADS, SEQ, SEQ), BF16),
            wide,
            tile,
            pltpu.VMEM((SEQ, D), F32),
            own_low,
            own,
            pltpu.VMEM((chunks, HALF, 128), F32),
            own,
            tile,
            tile,
            tile,
            tile,
            pltpu.VMEM((max(chunks, D // 256), HALF, D), BF16),
            pltpu.VMEM((D, FFN), F32),
            pltpu.VMEM((32, D), F32),
            pltpu.VMEM((count + 1, 8, D), F32),
            ffn_share,
            ffn_along,
            ffn_share,
            ffn_along,
            att_share,
            att_along,
            att_share,
            att_along,
            own_low,
            own_low,
            own_low,
            pltpu.VMEM((2, chunks, HALF, D), BF16),
            pltpu.SemaphoreType.REGULAR,
        ]
        + [dma(3, 2, count)]
        + [dma(3, count)] * 3
        + [dma(2, chunks)] * 4
        + [dma(3, chunks)] * 2
        + [dma(2, chunks)] * 3
        + [dma(chunks)]
        + [dma(count + 1)] * 2
        + [pltpu.SemaphoreType.DMA]
        + [dma(3, chunks)] * 2
        + [dma(3)] * 2
        + [dma(5, count)] * 4,
        compiler_params=pltpu.CompilerParams(
            collective_id=0, has_side_effects=True, vmem_limit_bytes=VMEM_LIMIT
        ),
    )(hidden_in, boxes.T, pages, padding, box_lanes(), weights, out_grad)
    if not ring:
        reda, redf = (
            lax.psum_scatter(part, "dp", scatter_dimension=0, tiled=True) for part in (reda, redf)
        )
        nred = lax.psum(nred, ("dp", "mp")) * 0.5
        nred = lax.dynamic_slice_in_dim(nred, lax.axis_index("dp") * share, share, 1)
    old = (
        (attn_in, attn_in_moment, attn_in_second)
        + (attn_out, attn_out_moment, attn_out_second)
        + (ffn_in, ffn_in_moment, ffn_in_second)
        + (ffn_out.T, ffn_out_moment.T, ffn_out_second.T)
        + (norm_weight, norm_moment, norm_second)
    )
    large = (mixed, input_grad)
    wide_grad = jax.ShapeDtypeStruct(input_grad.shape, F32)
    summed = (reda, redf, nred)
    new = pl.pallas_call(
        finish_kernel,
        out_shape=tuple(
            jax.ShapeDtypeStruct(part.shape, part.dtype) for part in (mixed, wide_grad) + old
        ),
        in_specs=[any_space] * 20,
        out_specs=(any_space,) * 17,
        scratch_shapes=[pltpu.VMEM(part.shape, F32) for part in summed + old + old]
        + [pltpu.VMEM(part.shape, part.dtype) for part in large + (wide_grad,)]
        + [dma(18), dma(15), dma(8), dma(8)],
        compiler_params=pltpu.CompilerParams(vmem_limit_bytes=VMEM_LIMIT),
    )(*summed, *large, *old)
    return new[:11] + tuple(part.T for part in new[11:14]) + new[14:]


def solution(mesh):
    rows = P("dp", None)
    into = P(None, "dp", "mp")
    out = P("mp", "dp")
    up = P("dp", "mp")
    norm = P(None, "dp")
    return jax.shard_map(
        partial(per_device, mesh.shape["dp"]),
        mesh=mesh,
        in_specs=(rows, P("dp"), P("dp"), rows, rows)
        + (into,) * 3
        + (out,) * 3
        + (up,) * 3
        + (out,) * 3
        + (norm,) * 3,
        out_specs=(rows, rows) + (into,) * 3 + (out,) * 3 + (up,) * 3 + (out,) * 3 + (norm,) * 3,
        check_vma=False,
    )
```
